128 devices in a mesh: seq: 8 (over z_lo, x), mp: 16 (over z_hi, y, core).
Axes of the slice: x: 4, y: 4, z: 4 (z_hi: 2, z_lo: 2; z = z_hi * 2 + z_lo), core: 2. Of those that a mesh axis runs over, the one named last changes fastest.
Arguments:
- features: bfloat16 [8192, 768], P('seq'), may hold values from -13 to 13
- base_tokens: int32 [524288], P('seq'), may hold values from 0 to 3
- base_proj: float32 [4, 768], replicated, may hold values from -6 to 6
- conv_weight: bfloat16 [5, 1536, 768], P(None, 'mp'), may hold values from -0.23399274 to 0.23399274
- conv_bias: float32 [1536], P('mp'), may hold values from -3 to 3
- w_query: bfloat16 [1536, 1536], P('mp'), may hold values from -0.5434805 to 0.5434805
- w_key: bfloat16 [1536, 1536], P('mp'), may hold values from -0.5434805 to 0.5434805
- w_value: bfloat16 [1536, 1536], P('mp'), may hold values from -0.15625 to 0.15625
- w_out: bfloat16 [1536, 1536], P('mp'), may hold values from -0.15625 to 0.15625
- cotangent: bfloat16 [4096, 1536], P('seq', 'mp'), may hold values from -6 to 6
Outputs:
- layer_out: bfloat16 [4096, 1536], P('seq', 'mp')
- grad_conv_weight: float32 [5, 1536, 768], P(None, 'mp')
- grad_conv_bias: float32 [1536], P('mp')
- grad_w_query: float32 [1536, 1536], P('mp')
- grad_w_key: float32 [1536, 1536], P('mp')
- grad_w_value: float32 [1536, 1536], P('mp')
- grad_w_out: float32 [1536, 1536], P('mp')
The draws below stay inside these ranges and needn't reach their ends.
All inputs are finite; a program needn't handle non-finite values.
Results may differ from the reference program's by a relative error of at most 0.03.
Values may be sent and summed in bfloat16 or wider, within the bound.
A program may use at most 128 MiB of HBM per device.

```python
import math
import jax
import jax.numpy as jnp
from jax import lax

D = 1536
CIN = 768
HEADS = 8
KERNEL = 5
BIN_WIDTH = 64
BINS = 8192
TOKENS = 4096
BASES = 524288
HEAD = 192


def draw_features(key, part):
    key = jax.random.fold_in(key, 11)
    first, second = jax.random.split(key, 2)
    row_scale = jnp.exp(jax.random.uniform(first, (BINS, 1), jnp.float32, math.log(0.3), math.log(3.0)))
    values = jnp.clip(jax.random.normal(second, (BINS, CIN), jnp.float32), -4.0, 4.0) * row_scale
    return values.astype(jnp.bfloat16)


def draw_conv_weight(key, part):
    key = jax.random.fold_in(key, 13)
    first, second = jax.random.split(key, 2)
    ramp = jnp.arange(D, dtype=jnp.float32) / D
    noise = jnp.exp(jax.random.uniform(first, (D,), jnp.float32, math.log(0.5), math.log(2.0)))
    col_scale = 0.6 * jnp.exp(ramp * math.log(3.0)) * noise
    entries = jnp.clip(jax.random.normal(second, (KERNEL, D, CIN), jnp.float32), -4.0, 4.0)
    return (entries * col_scale[None, :, None] * (KERNEL * CIN) ** (-0.5)).astype(jnp.bfloat16)


def draw_w_query(key, part):
    key = jax.random.fold_in(key, 17)
    own_part = jnp.clip(jax.random.normal(key, (D, D), jnp.float32), -4.0, 4.0)
    values = own_part
    return (values * D ** (-0.5)).astype(jnp.bfloat16)


def draw_w_key(key, part):
    key = jax.random.fold_in(key, 19)
    own_part = jnp.clip(jax.random.normal(key, (D, D), jnp.float32), -4.0, 4.0)
    values = own_part
    return (values * D ** (-0.5)).astype(jnp.bfloat16)


def plant(array, stream_key, smallest, high):
    longest = array.shape.index(max(array.shape))
    spots = []
    for shift in (0, 1):
        where = [jax.random.randint(jax.random.fold_in(stream_key, axis), (), 0, length) for axis, length in enumerate(array.shape)]
        where[longest] = (where[longest] + shift) % array.shape[longest]
        spots.append(tuple(where))
    return array.at[spots[0]].set(smallest).at[spots[1]].set(high)


def steps_of(stream_key, shape, cuts, least, largest):
    loudness = 1.0
    for position, parts in cuts:
        steps = jax.random.uniform(jax.random.fold_in(jax.random.fold_in(stream_key, 6), position), (parts,), jnp.float32, least / len(cuts), largest / len(cuts))
        loudness = loudness * jnp.repeat(jnp.exp(steps), shape[position] // parts).reshape((-1,) + (1,) * (len(shape) - 1 - position))
    return loudness


def centred(own_key, extent, deviation, bound, cuts=(), kind=jnp.bfloat16):
    loudness = steps_of(own_key, extent, cuts, -0.22, 0.18) if cuts else 1.0
    array = jax.random.normal(own_key, extent, jnp.float32) * deviation * loudness
    return jnp.minimum(jnp.maximum(array, -bound), bound).astype(kind)


def setup_inputs(seed: int = 0) -> dict:
    keys = jax.random.split(jax.random.key(seed), 11)
    features = draw_features(jax.random.fold_in(keys[10], 71), 0)
    base_tokens = plant(jax.random.randint(keys[1], (BASES,), 0, 4), jax.random.fold_in(keys[1], 1), 0, 3).astype(jnp.int32)
    base_proj = centred(keys[2], (4, CIN), 1.0, 6.0, (), jnp.float32)
    conv_weight = draw_conv_weight(jax.random.fold_in(keys[10], 71), 0)
    conv_bias = centred(keys[4], (D,), 0.5, 3.0, ((0, 16),), jnp.float32)
    w_query = draw_w_query(jax.random.fold_in(keys[10], 71), 0)
    w_key = draw_w_key(jax.random.fold_in(keys[10], 71), 0)
    w_value = centred(keys[7], (D, D), D ** -0.5, 0.15625, ((0, 16),))
    w_out = centred(keys[8], (D, D), D ** -0.5, 0.15625, ((0, 16),))
    cotangent = centred(keys[9], (TOKENS, D), 1.0, 6.0, ((0, 8), (1, 16)))
    return dict(features=features, base_tokens=base_tokens, base_proj=base_proj, conv_weight=conv_weight, conv_bias=conv_bias, w_query=w_query, w_key=w_key, w_value=w_value, w_out=w_out, cotangent=cotangent)


EPS = 1e-06

def composition(base_tokens):
    letters = jnp.arange(4, dtype=jnp.int32)
    matches = (base_tokens[None, :] == letters[:, None]).astype(jnp.float32)
    return lax.optimization_barrier(jnp.sum(matches.reshape(4, -1, BIN_WIDTH), axis=2)) / BIN_WIDTH

def gelu_slope(pre_act):
    return jax.vjp(jax.nn.gelu, pre_act)[1](jnp.ones_like(pre_act))[0]

def convolve(padded, weight, offset):
    length = padded.shape[0] - (KERNEL - 1)
    running = jnp.zeros((length, weight.shape[1]), jnp.float32) + offset[None, :]
    for tap_index in range(KERNEL):
        running = running + lax.dot_general(padded[tap_index:tap_index + length], weight[tap_index], (((1,), (1,)), ((), ())), preferred_element_type=jnp.float32)
    return running

def attend(query_rows, key_rows, value_rows, block_rows):
    score_scale = query_rows.shape[1] ** (-0.5)

    def one_block(row_block):
        scores = lax.dot_general(row_block, key_rows, (((1,), (1,)), ((), ())), preferred_element_type=jnp.float32) * score_scale
        row_max = lax.optimization_barrier(jnp.max(scores, axis=1, keepdims=True))
        log_total = jnp.log(lax.optimization_barrier(jnp.sum(jnp.exp(scores - row_max), axis=1, keepdims=True))) + row_max
        attn_probs = jnp.exp(scores - log_total).astype(jnp.bfloat16)
        result = jnp.dot(attn_probs, value_rows, preferred_element_type=jnp.float32).astype(jnp.bfloat16)
        return (result, log_total[:, 0])
    results, totals = lax.map(one_block, query_rows.reshape(-1, block_rows, query_rows.shape[1]))
    return (results.reshape(-1, value_rows.shape[1]), totals.reshape(-1))

def attend_grad(query_rows, key_rows, value_rows, totals, grad_rows, block_rows, width):
    score_scale = query_rows.shape[1] ** (-0.5)
    head_dim = query_rows.shape[1]

    def one_block(running, pieces):
        row_block, row_totals, row_grads = pieces
        scores = lax.dot_general(row_block, key_rows, (((1,), (1,)), ((), ())), preferred_element_type=jnp.float32) * score_scale
        attn_probs = jnp.exp(scores - row_totals[:, None])
        grad_probs = lax.dot_general(row_grads, value_rows, (((1,), (1,)), ((), ())), preferred_element_type=jnp.float32)
        row_delta = lax.optimization_barrier(jnp.sum(attn_probs * grad_probs, axis=1, keepdims=True))
        grad_scores = (attn_probs * (grad_probs - row_delta) * score_scale).astype(jnp.bfloat16)
        grad_query = jnp.dot(grad_scores, key_rows[:, :width], preferred_element_type=jnp.float32).astype(jnp.bfloat16)
        key_sum = running[0] + lax.dot_general(grad_scores, row_block[:, :width], (((0,), (0,)), ((), ())), preferred_element_type=jnp.float32)
        value_sum = running[1] + lax.dot_general(attn_probs.astype(jnp.bfloat16), row_grads[:, :width], (((0,), (0,)), ((), ())), preferred_element_type=jnp.float32)
        return ((key_sum, value_sum), grad_query)
    initial = (jnp.zeros((key_rows.shape[0], width), jnp.float32), jnp.zeros((key_rows.shape[0], width), jnp.float32))
    sums, grads = lax.scan(one_block, initial, (query_rows.reshape(-1, block_rows, head_dim), totals.reshape(-1, block_rows), grad_rows.reshape(-1, block_rows, head_dim)))
    return (grads.reshape(-1, width), sums[0], sums[1])

def split_heads(matrix):
    return matrix.reshape(TOKENS, HEADS, HEAD).transpose(1, 0, 2)

def merge_heads(stacked):
    return stacked.transpose(1, 0, 2).reshape(TOKENS, D)

def reference(features, base_tokens, base_proj, conv_weight, conv_bias, w_query, w_key, w_value, w_out, cotangent):
    mixed_in = features.astype(jnp.float32) + lax.dot_general(composition(base_tokens), base_proj, (((0,), (0,)), ((), ())), precision=lax.Precision.HIGHEST, preferred_element_type=jnp.float32)
    conv_input = mixed_in.astype(jnp.bfloat16)
    padded = jnp.pad(conv_input, ((KERNEL // 2, KERNEL // 2), (0, 0)))
    pre_act = convolve(padded, conv_weight, conv_bias)
    tok = lax.optimization_barrier(jnp.mean(jax.nn.gelu(pre_act).reshape(-1, 2, D), axis=1)).astype(jnp.bfloat16)
    tok_wide = tok.astype(jnp.float32)
    inverse = lax.rsqrt(lax.optimization_barrier(jnp.mean(tok_wide * tok_wide, axis=1, keepdims=True)) + EPS)
    unit_rows = tok_wide * inverse
    normed = unit_rows.astype(jnp.bfloat16)
    contract_cols = (((1,), (1,)), ((), ()))
    contract_rows = (((0,), (0,)), ((), ()))
    query_all = lax.dot_general(normed, w_query, contract_cols, preferred_element_type=jnp.float32).astype(jnp.bfloat16)
    key_all = lax.dot_general(normed, w_key, contract_cols, preferred_element_type=jnp.float32).astype(jnp.bfloat16)
    value_all = lax.dot_general(normed, w_value, contract_cols, preferred_element_type=jnp.float32).astype(jnp.bfloat16)
    block_rows = min(512, TOKENS)

    def head_forward(pieces):
        return attend(pieces[0], pieces[1], pieces[2], block_rows)
    query_heads, key_heads, value_heads = (split_heads(query_all), split_heads(key_all), split_heads(value_all))
    out_heads, log_totals = lax.map(head_forward, (query_heads, key_heads, value_heads))
    head_out = merge_heads(out_heads)
    attn_out = jnp.dot(head_out, w_out, preferred_element_type=jnp.float32)
    layer_out = (tok_wide + attn_out).astype(jnp.bfloat16)
    grad_out = lax.dot_general(cotangent, w_out, contract_cols, preferred_element_type=jnp.float32).astype(jnp.bfloat16)
    grad_w_out = lax.dot_general(head_out, cotangent, contract_rows, preferred_element_type=jnp.float32)

    def head_backward(pieces):
        return attend_grad(pieces[0], pieces[1], pieces[2], pieces[3], pieces[4], block_rows, HEAD)
    grad_q_heads, key_sums, value_sums = lax.map(head_backward, (query_heads, key_heads, value_heads, log_totals, split_heads(grad_out)))
    grad_query = merge_heads(grad_q_heads)
    grad_key = merge_heads(key_sums).astype(jnp.bfloat16)
    grad_value = merge_heads(value_sums).astype(jnp.bfloat16)
    grad_w_query = lax.dot_general(grad_query, normed, contract_rows, preferred_element_type=jnp.float32)
    grad_w_key = lax.dot_general(grad_key, normed, contract_rows, preferred_element_type=jnp.float32)
    grad_w_value = lax.dot_general(grad_value, normed, contract_rows, preferred_element_type=jnp.float32)
    normed_grad = jnp.dot(grad_query, w_query, preferred_element_type=jnp.float32)
    normed_grad = normed_grad + jnp.dot(grad_key, w_key, preferred_element_type=jnp.float32)
    normed_grad = normed_grad + jnp.dot(grad_value, w_value, preferred_element_type=jnp.float32)
    row_stat = lax.optimization_barrier(jnp.sum(normed_grad * unit_rows, axis=1, keepdims=True)) / D
    tok_grad = cotangent.astype(jnp.float32) + inverse * (normed_grad - unit_rows * row_stat)
    spread_grad = jnp.broadcast_to(tok_grad[:, None, :], (TOKENS, 2, D)).reshape(-1, D)
    pre_grad = (0.5 * spread_grad * gelu_slope(pre_act)).astype(jnp.bfloat16)
    length = pre_grad.shape[0]
    grad_conv_weight = jnp.stack([lax.dot_general(pre_grad, padded[tap_index:tap_index + length], contract_rows, preferred_element_type=jnp.float32) for tap_index in range(KERNEL)])
    grad_conv_bias = lax.optimization_barrier(jnp.sum(pre_grad.astype(jnp.float32), axis=0))
    return (layer_out, grad_conv_weight, grad_conv_bias, grad_w_query, grad_w_key, grad_w_value, grad_w_out)
```

```python
import functools

import jax
import jax.numpy as jnp
from jax import lax
from jax.experimental import pallas as pl
from jax.experimental.pallas import tpu as pltpu
from jax.sharding import PartitionSpec as P

D = 1536
CIN = 768
TAPS = 5
BIN_WIDTH = 64
EPS = 1e-06
HEAD = 192
SHARE = 96
TOK = 256
PAIRS = 512
WIDE = 640
BF = jnp.bfloat16
F32 = jnp.float32
MESH = pl.DeviceIdType.MESH
SCALE = HEAD ** (-0.5)
ROOT2PI = 0.7978845608028654

TOK_AG, COT_AG, OUT_RS, NORM_RS = 0, 16, 32, 48
G_RS, G_AG, C_RS, C_AG = 64, 72, 80, 88
W_SIB, HALO, Q_X, DO_X, ST_X, O_X, DQ_X = 96, 100, 104, 108, 112, 116, 120
KV_Z, KV_SIB, DKV_SIB, DKV_Z, G_SIB = 124, 125, 127, 129, 130
SEMS = 132


def mm(a, b):
    return jnp.dot(a, b, preferred_element_type=F32)


def nt(a, b):
    return lax.dot_general(a, b, (((1,), (1,)), ((), ())), preferred_element_type=F32)


def tn(a, b):
    return lax.dot_general(a, b, (((0,), (0,)), ((), ())), preferred_element_type=F32)


def kernel(
    feat, toks, bproj, cw, cbias, wq, wk, wv, wo, cot,
    o_layer, o_conv, o_bias, o_q, o_k, o_v, o_o,
    xf, r3, xe, halo, wt, w4, z, slope, tok_own, cot_own, tok_t, cot_t, norm_t,
    q, kv, kn, vn, do, et, dp, st, st_in, o_f, o_send, o_in, ot, fac,
    dq_f, dq_send, dq_in, dkv, dkv_send, dkv_in, z_send, z_in, dqkv, ng,
    n_send, n_in, a_send, a_in, g_part, g_send, g_sib, g_acc, g_in, g_red, g_all,
    pgs, c_send, c_in, c_red, c_all, ssem, rsem,
):
    s = lax.axis_index("seq")
    m = lax.axis_index("mp")
    zl = s // 4
    x = s % 4
    c = m % 2
    sib = (s, m + 1 - 2 * c)
    zpart = ((1 - zl) * 4 + x, m)
    sent = []

    def xpeer(r):
        return (zl * 4 + (x + r) % 4, m)

    def seqpeer(r):
        return ((s + r) % 8, m)

    def mppeer(r):
        return (s, (m + r) % 16)

    def push(src, dst, sem, dev):
        copy = pltpu.make_async_remote_copy(
            src_ref=src, dst_ref=dst, send_sem=ssem.at[sem], recv_sem=rsem.at[sem],
            device_id=dev, device_id_type=MESH,
        )
        copy.start()
        sent.append(copy)

    def land(dst, sem):
        pltpu.make_async_remote_copy(
            src_ref=dst, dst_ref=dst, send_sem=ssem.at[sem], recv_sem=rsem.at[sem],
            device_id=sib, device_id_type=MESH,
        ).wait_recv()

    def al(v, n):
        return pl.multiple_of(v, n)

    barrier = pltpu.get_barrier_semaphore()
    for r in range(1, 16):
        pl.semaphore_signal(barrier, inc=1, device_id=mppeer(r), device_id_type=MESH)
    for r in range(1, 8):
        pl.semaphore_signal(barrier, inc=1, device_id=seqpeer(r), device_id_type=MESH)

    bp = bproj[...]
    hi = bp.astype(BF).astype(F32)
    mid = (bp - hi).astype(BF).astype(F32)
    low = (bp - hi - mid).astype(BF).astype(F32)
    r3[...] = jnp.zeros_like(r3)
    for k, part in enumerate((hi, mid, low)):
        r3[8 * k : 8 * k + 4, 0:CIN] = part
        r3[8 * k + 4 : 8 * k + 8, CIN:D] = part
    lane = lax.broadcasted_iota(jnp.int32, (128, 32), 0)
    col = lax.broadcasted_iota(jnp.int32, (128, 32), 1)
    group = jnp.where(lane >= BIN_WIDTH, 4, 0)
    counts = jnp.zeros((PAIRS, 32), F32)
    for b in range(4):
        pick = jnp.where((col < 24) & (col % 8 == group + b), 1.0, 0.0).astype(BF)
        match = jnp.where(toks[...] == b, 1.0, 0.0).astype(BF)
        counts = counts + mm(match, pick)
    comp = (counts * (1.0 / BIN_WIDTH)).astype(BF)
    for k in range(6):
        xf[k] = feat[:, 128 * k : 128 * k + 128].astype(F32)
    for k in range(6):
        for half in range(2):
            lo = CIN * half + 128 * k
            extra = mm(comp, r3[:, lo : lo + 128].astype(BF))
            own = xf[k, pl.ds(half, PAIRS, stride=2), :]
            xe[0:PAIRS, lo : lo + 128] = (own + extra).astype(BF)

    pl.semaphore_wait(barrier, 22)
    push(xe.at[pl.ds(PAIRS - 16, 16)], halo.at[0], HALO, seqpeer(1))
    push(xe.at[pl.ds(0, 16)], halo.at[1], HALO + 1, seqpeer(7))
    for k, w in enumerate((wq, wk, wv, wo)):
        rows = pl.ds(al(HEAD * k + SHARE * c, 32), SHARE)
        push(w, w4.at[rows], W_SIB + k, sib)

    zero = jnp.zeros((SHARE, CIN), BF)
    left = (cw[0], zero, cw[2], cw[1], cw[4], cw[3])
    right = (cw[1], cw[0], cw[3], cw[2], zero, cw[4])
    for g in range(6):
        wt[SHARE * g : SHARE * g + SHARE, 0:CIN] = left[g]
        wt[SHARE * g : SHARE * g + SHARE, CIN:D] = right[g]

    @pl.loop(0, 2)
    def _(i):
        rows = pl.ds(al(i * 256, 256), 256)
        z[:, rows] = nt(wt[...], xe[rows, :])

    land(halo.at[0], HALO)
    land(halo.at[1], HALO + 1)
    at = lax.broadcasted_iota(jnp.int32, (16, D), 0)
    after = halo[1].astype(F32)
    before = halo[0].astype(F32)
    after = jnp.where((at == 0) & (s < 7), after, 0.0)
    before = jnp.where((at == 15) & (s > 0), before, 0.0)
    xe[PAIRS:WIDE, :] = jnp.zeros((WIDE - PAIRS, D), BF)
    xe[PAIRS : PAIRS + 16, :] = after.astype(BF)
    xe[WIDE - 16 : WIDE, :] = before.astype(BF)
    z[:, PAIRS:WIDE] = nt(wt[...], xe[PAIRS:WIDE, :])

    total = jnp.zeros((SHARE, PAIRS), F32)
    for half in range(2):
        r0, r1, r2 = (SHARE * (2 * d + half) for d in range(3))
        pre = pltpu.roll(z[r0 : r0 + SHARE, :], 1, 1)[:, 0:PAIRS]
        pre = pre + z[r1 : r1 + SHARE, 0:PAIRS]
        pre = pre + pltpu.roll(z[r2 : r2 + SHARE, :], WIDE - 1, 1)[:, 0:PAIRS]
        pre = pre + cbias[...]
        square = pre * pre
        bend = jnp.tanh(ROOT2PI * (pre + 0.044715 * (square * pre)))
        total = total + pre * (0.5 * (1.0 + bend))
        slope[half] = 0.5 * (1.0 + bend) + (0.5 * pre) * (1.0 - bend * bend) * (
            ROOT2PI * (1.0 + (3.0 * 0.044715) * square)
        )
    tok_own[...] = (0.5 * total).astype(BF)
    mine = pl.ds(al(SHARE * m, 32), SHARE)

    def spread(own, full, base):
        for r in range(1, 16):
            cols = pl.ds(al(TOK * ((m + r) % 2), TOK), TOK)
            push(own.at[:, cols], full.at[mine], base + r, mppeer(r))
        full[mine, :] = own[:, pl.ds(al(TOK * c, TOK), TOK)]

    def gathered(full, base):
        for r in range(1, 16):
            rows = pl.ds(al(SHARE * ((m - r + 16) % 16), 32), SHARE)
            land(full.at[rows], base + r)

    spread(tok_own, tok_t, TOK_AG)
    cot_own[...] = jnp.transpose(cot[...].astype(F32)).astype(BF)
    spread(cot_own, cot_t, COT_AG)

    for k, w in enumerate((wq, wk, wv, wo)):
        w4[pl.ds(al(HEAD * k + SHARE * c, 32), SHARE), :] = w[...]
    for k in range(4):
        land(w4.at[pl.ds(al(HEAD * k + SHARE * (1 - c), 32), SHARE)], W_SIB + k)

    gathered(tok_t, TOK_AG)
    wide = tok_t[...].astype(F32)
    inverse = lax.rsqrt(jnp.sum(wide * wide, axis=0, keepdims=True) * (1.0 / D) + EPS)
    norm_t[...] = (wide * inverse).astype(BF)
    qkv = mm(w4[0 : 3 * HEAD, :], norm_t[...]).astype(BF)
    q[0] = qkv[0:HEAD]
    kv[0] = qkv[HEAD : 3 * HEAD]
    push(kv.at[0], kv.at[2], KV_Z, zpart)
    push(kv.at[0], kv.at[1], KV_SIB, sib)
    for r in range(1, 4):
        push(q.at[0], q.at[r], Q_X + r, xpeer(r))

    gathered(cot_t, COT_AG)
    do[0] = mm(w4[3 * HEAD : 4 * HEAD, :], cot_t[...]).astype(BF)
    for r in range(1, 4):
        push(do.at[0], do.at[r], DO_X + r, xpeer(r))

    land(kv.at[2], KV_Z)
    push(kv.at[2], kv.at[3], KV_SIB + 1, sib)
    land(kv.at[1], KV_SIB)
    land(kv.at[3], KV_SIB + 1)
    for i in range(4):
        kn[i] = jnp.transpose(kv[i, 0:HEAD].astype(F32)).astype(BF)
        vn[i] = jnp.transpose(kv[i, HEAD : 2 * HEAD].astype(F32)).astype(BF)
    for r in range(1, 4):
        land(q.at[r], Q_X + r)
        land(do.at[r], DO_X + r)

    @pl.loop(0, 4)
    def _(j):
        top = jnp.full((1, TOK), -jnp.inf, F32)
        for i in range(4):
            scores = mm(kn[i], q[j]) * SCALE
            et[j, TOK * i : TOK * i + TOK, :] = scores
            top = jnp.maximum(top, jnp.max(scores, axis=0, keepdims=True))
        norm = jnp.zeros((1, TOK), F32)
        delta = jnp.zeros((1, TOK), F32)
        out = jnp.zeros((HEAD, TOK), F32)
        for i in range(4):
            rows = slice(TOK * i, TOK * i + TOK)
            e = jnp.exp(et[j, rows, :] - top)
            et[j, rows, :] = e
            norm = norm + jnp.sum(e, axis=0, keepdims=True)
            out = out + mm(kv[i, HEAD : 2 * HEAD, :], e.astype(BF))
            grad = mm(vn[i], do[j])
            dp[j, rows, :] = grad
            delta = delta + jnp.sum(e * grad, axis=0, keepdims=True)
        o_f[j] = out
        st[j, 0:1, :] = top
        st[j, 1:2, :] = norm
        st[j, 2:3, :] = delta
        st[j, 3:8, :] = jnp.zeros((5, TOK), F32)

    for r in range(1, 4):
        push(st, st_in.at[r], ST_X + r, xpeer(r))
    for r in range(1, 4):
        land(st_in.at[r], ST_X + r)

    factors = []
    deltas = []
    for j in range(4):
        every = [st[j]] + [st_in[r, (j - r) % 4] for r in range(1, 4)]
        top = functools.reduce(jnp.maximum, [e[0:1] for e in every])
        norm = sum(e[1:2] * jnp.exp(e[0:1] - top) for e in every)
        log_total = jnp.log(norm) + top
        factors.append(jnp.exp(every[0][0:1] - log_total))
        deltas.append(sum(e[2:3] * jnp.exp(e[0:1] - log_total) for e in every))
        o_f[j] = o_f[j] * factors[j]
    for j in range(4):
        fac[j, 0:1, :] = factors[j]
        fac[j, 1:2, :] = deltas[j]
    for r in range(1, 4):
        o_send[r] = o_f[r].astype(BF)
        push(o_send.at[r], o_in.at[4 - r], O_X + 4 - r, xpeer(4 - r))

    dkv[...] = jnp.zeros_like(dkv)

    @pl.loop(0, 4)
    def _(j):
        factor = fac[j, 0:1, :]
        delta = fac[j, 1:2, :]
        grad_q = jnp.zeros((HEAD, TOK), F32)
        for i in range(4):
            rows = slice(TOK * i, TOK * i + TOK)
            p = et[j, rows, :] * factor
            ds = (p * (dp[j, rows, :] - delta) * SCALE).astype(BF)
            grad_q = grad_q + mm(kv[i, 0:HEAD, :], ds)
            dkv[i, 0:HEAD, :] += nt(q[j], ds)
            dkv[i, HEAD : 2 * HEAD, :] += nt(do[j], p.astype(BF))
        dq_f[j] = grad_q

    dkv_send[0] = dkv[3].astype(BF)
    push(dkv_send.at[0], dkv_in.at[0], DKV_SIB, sib)
    dkv_send[1] = dkv[1].astype(BF)
    push(dkv_send.at[1], dkv_in.at[1], DKV_SIB + 1, sib)
    for r in range(1, 4):
        dq_send[r] = dq_f[r].astype(BF)
        push(dq_send.at[r], dq_in.at[4 - r], DQ_X + 4 - r, xpeer(4 - r))
    land(dkv_in.at[0], DKV_SIB)
    z_send[...] = (dkv[2] + dkv_in[0].astype(F32)).astype(BF)
    push(z_send, z_in, DKV_Z, zpart)

    for r in range(1, 4):
        land(o_in.at[r], O_X + r)
    ot[...] = (o_f[0] + sum(o_in[r].astype(F32) for r in range(1, 4))).astype(BF)

    def scatter(send, into, base):
        for r in range(1, 16):
            rows = pl.ds(al(SHARE * ((m + r) % 16), 32), SHARE)
            push(send.at[rows], into.at[r], base + r, mppeer(r))
        into[0] = send[mine, :]

    def reduced(into, base):
        for r in range(1, 16):
            land(into.at[r], base + r)
        same = sum(into[r].astype(F32) for r in range(0, 16, 2))
        other = sum(into[r].astype(F32) for r in range(1, 16, 2))
        first = jnp.where(c == 0, same, other)
        second = jnp.where(c == 0, other, same)
        return first, second

    @pl.loop(0, 4)
    def _(k):
        cols = pl.ds(al(384 * k, 128), 384)
        a_send[cols, :] = tn(w4[3 * HEAD : 4 * HEAD, cols], ot[...]).astype(BF)

    scatter(a_send, a_in, OUT_RS)

    land(dkv_in.at[1], DKV_SIB + 1)
    for r in range(1, 4):
        land(dq_in.at[r], DQ_X + r)
    grad_q = dq_f[0] + sum(dq_in[r].astype(F32) for r in range(1, 4))
    dqkv[0:HEAD, :] = grad_q.astype(BF)
    land(z_in, DKV_Z)
    dqkv[HEAD : 3 * HEAD, :] = (dkv[0] + dkv_in[1].astype(F32) + z_in[...].astype(F32)).astype(BF)

    @pl.loop(0, 4)
    def _(k):
        cols = pl.ds(al(384 * k, 128), 384)
        ng[cols, :] = tn(w4[0 : 3 * HEAD, cols], dqkv[...])

    wide = tok_t[...].astype(F32)
    inverse = lax.rsqrt(jnp.sum(wide * wide, axis=0, keepdims=True) * (1.0 / D) + EPS)
    unit = wide * inverse
    row_stat = jnp.sum(ng[...] * unit, axis=0, keepdims=True) * (1.0 / D)
    n_send[...] = (inverse * (ng[...] - unit * row_stat)).astype(BF)
    scatter(n_send, n_in, NORM_RS)

    @pl.loop(0, 4)
    def _(k):
        cols = pl.ds(al(384 * k, 128), 384)
        g_part[0 : 3 * HEAD, cols] = nt(dqkv[...], norm_t[cols, :])
        g_part[3 * HEAD : 4 * HEAD, cols] = nt(ot[...], cot_t[cols, :])

    for k in range(4):
        g_send[k] = g_part[pl.ds(al(HEAD * k + SHARE * (1 - c), 32), SHARE), :].astype(BF)
    push(g_send, g_sib, G_SIB, sib)
    land(g_sib, G_SIB)
    for k in range(4):
        own = g_part[pl.ds(al(HEAD * k + SHARE * c, 32), SHARE), :]
        g_acc[k] = (own + g_sib[k].astype(F32)).astype(BF)

    def g_piece(buf, seq):
        return buf.at[:, pl.ds(al(48 * (seq // 4), 16), 48), pl.ds(al(384 * (seq % 4), 128), 384)]

    for r in range(1, 8):
        push(g_piece(g_acc, (s + r) % 8), g_in.at[r], G_RS + r, seqpeer(r))

    tok_wide = tok_own[...].astype(F32)
    first, second = reduced(a_in, OUT_RS)
    out = jnp.concatenate([first, second], axis=1) + tok_wide
    o_layer[...] = jnp.transpose(out).astype(BF)

    first, second = reduced(n_in, NORM_RS)
    tok_grad = cot_own[...].astype(F32) + jnp.concatenate([first, second], axis=1)
    pad = jnp.zeros((SHARE, WIDE - PAIRS), F32)
    for half in range(2):
        pg = jnp.concatenate([0.5 * tok_grad * slope[half], pad], axis=1)
        for d in range(3):
            shift = (WIDE - 1, 0, 1)[d]
            moved = pltpu.roll(pg, shift, 1) if shift else pg
            row = SHARE * (2 * d + half)
            pgs[row : row + SHARE, :] = moved.astype(BF)
    both = pgs[2 * SHARE : 3 * SHARE, 0:PAIRS], pgs[3 * SHARE : 4 * SHARE, 0:PAIRS]
    ones = jnp.ones((16, PAIRS), BF)
    bias = nt(ones, both[0]) + nt(ones, both[1])
    c_send[TAPS * SHARE :, :] = jnp.zeros((32, CIN), BF)
    c_send[TAPS * SHARE : TAPS * SHARE + 16, 0:SHARE] = bias.astype(BF)

    @pl.loop(0, 3)
    def _(k):
        cols = pl.ds(al(256 * k, 256), 256)
        odd_cols = pl.ds(al(CIN + 256 * k, 256), 256)
        me = mm(pgs[...], xe[:, cols])
        mo = mm(pgs[...], xe[:, odd_cols])

        def part(arr, d, half):
            row = SHARE * (2 * (d + 1) + half)
            return arr[row : row + SHARE]

        taps = (
            part(me, -1, 0) + part(mo, -1, 1),
            part(mo, -1, 0) + part(me, 0, 1),
            part(me, 0, 0) + part(mo, 0, 1),
            part(mo, 0, 0) + part(me, 1, 1),
            part(me, 1, 0) + part(mo, 1, 1),
        )
        for t in range(TAPS):
            c_send[SHARE * t : SHARE * t + SHARE, cols] = taps[t].astype(BF)

    def c_piece(buf, seq):
        return buf.at[pl.ds(al(64 * seq, 64), 64)]

    for r in range(1, 8):
        push(c_piece(c_send, (s + r) % 8), c_in.at[r], C_RS + r, seqpeer(r))

    for r in range(1, 8):
        land(g_in.at[r], G_RS + r)
    own_rows = pl.ds(al(48 * zl, 16), 48)
    own_cols = pl.ds(al(384 * x, 128), 384)
    acc = g_acc[:, own_rows, own_cols].astype(F32)
    for r in range(1, 8):
        acc = acc + g_in[r].astype(F32)
    g_red[...] = acc.astype(BF)
    for r in range(1, 8):
        push(g_red, g_piece(g_all, s), G_AG + r, seqpeer(r))
    g_all[:, own_rows, own_cols] = g_red[...]

    for r in range(1, 8):
        land(c_in.at[r], C_RS + r)
    acc = c_send[pl.ds(al(64 * s, 64), 64), :].astype(F32)
    for r in range(1, 8):
        acc = acc + c_in[r].astype(F32)
    c_red[...] = acc.astype(BF)
    for r in range(1, 8):
        push(c_red, c_piece(c_all, s), C_AG + r, seqpeer(r))
    c_all[pl.ds(al(64 * s, 64), 64), :] = c_red[...]

    for r in range(1, 8):
        land(g_piece(g_all, (s - r + 8) % 8), G_AG + r)
    for k, o in enumerate((o_q, o_k, o_v, o_o)):
        o[...] = g_all[k].astype(F32)
    for r in range(1, 8):
        land(c_piece(c_all, (s - r + 8) % 8), C_AG + r)
    for t in range(TAPS):
        o_conv[t] = c_all[SHARE * t : SHARE * t + SHARE, :].astype(F32)
    o_bias[...] = c_all[TAPS * SHARE : TAPS * SHARE + 16, 0:SHARE].astype(F32)[0:1]
    for copy in sent:
        copy.wait_send()


def scratch():
    def v(*shape, dtype=BF):
        return pltpu.VMEM(shape, dtype)

    return [
        v(6, 1024, 128, dtype=F32), v(32, D, dtype=F32), v(WIDE, D), v(2, 16, D), v(576, D), v(768, D),
        v(576, WIDE, dtype=F32), v(2, SHARE, PAIRS, dtype=F32), v(SHARE, PAIRS), v(SHARE, PAIRS),
        v(D, TOK), v(D, TOK), v(D, TOK),
        v(4, HEAD, TOK), v(4, 384, TOK), v(4, TOK, HEAD), v(4, TOK, HEAD), v(4, HEAD, TOK),
        v(4, 1024, TOK, dtype=F32), v(4, 1024, TOK, dtype=F32),
        v(4, 8, TOK, dtype=F32), v(4, 4, 8, TOK, dtype=F32),
        v(4, HEAD, TOK, dtype=F32), v(4, HEAD, TOK), v(4, HEAD, TOK), v(HEAD, TOK),
        v(4, 8, TOK, dtype=F32),
        v(4, HEAD, TOK, dtype=F32), v(4, HEAD, TOK), v(4, HEAD, TOK),
        v(4, 384, TOK, dtype=F32), v(2, 384, TOK), v(2, 384, TOK), v(384, TOK), v(384, TOK),
        v(576, TOK), v(D, TOK, dtype=F32),
        v(D, TOK), v(16, SHARE, TOK), v(D, TOK), v(16, SHARE, TOK),
        v(768, D, dtype=F32), v(4, SHARE, D), v(4, SHARE, D), v(4, SHARE, D),
        v(8, 4, 48, 384), v(4, 48, 384), v(4, SHARE, D),
        v(576, WIDE), v(512, CIN), v(8, 64, CIN), v(64, CIN), v(512, CIN),
        pltpu.SemaphoreType.DMA((SEMS,)), pltpu.SemaphoreType.DMA((SEMS,)),
    ]


def body(features, base_tokens, base_proj, conv_weight, conv_bias, w_query, w_key, w_value, w_out, cotangent):
    vmem = pl.BlockSpec(memory_space=pltpu.VMEM)
    square = jax.ShapeDtypeStruct((SHARE, D), F32)
    outs = pl.pallas_call(
        kernel,
        out_shape=(
            jax.ShapeDtypeStruct((PAIRS, SHARE), BF),
            jax.ShapeDtypeStruct((TAPS, SHARE, CIN), F32),
            jax.ShapeDtypeStruct((1, SHARE), F32),
            square, square, square, square,
        ),
        in_specs=[vmem] * 10,
        out_specs=(vmem,) * 7,
        scratch_shapes=scratch(),
        compiler_params=pltpu.CompilerParams(
            collective_id=0, has_side_effects=True, vmem_limit_bytes=60 * 1024 * 1024
        ),
        cost_estimate=pl.CostEstimate(flops=8_000_000_000, bytes_accessed=8_000_000, transcendentals=1_300_000),
        name="section",
    )(
        features, base_tokens.reshape(PAIRS, 128), base_proj, conv_weight, conv_bias.reshape(SHARE, 1),
        w_query, w_key, w_value, w_out, cotangent,
    )
    layer, conv, bias, gq, gk, gv, go = outs
    return layer, conv, bias.reshape(SHARE), gq, gk, gv, go


def solution(mesh):
    placed = (
        P("seq", None), P("seq"), P(), P(None, "mp", None), P("mp"),
        P("mp", None), P("mp", None), P("mp", None), P("mp", None), P("seq", "mp"),
    )
    return jax.shard_map(
        body,
        mesh=mesh,
        in_specs=placed,
        out_specs=(
            P("seq", "mp"), P(None, "mp", None), P("mp"),
            P("mp", None), P("mp", None), P("mp", None), P("mp", None),
        ),
        check_vma=False,
    )
```

```python
import functools

import jax
import jax.numpy as jnp
from jax import lax
from jax.experimental import pallas as pl
from jax.experimental.pallas import tpu as pltpu
from jax.sharding import PartitionSpec as P

D = 1536
CIN = 768
TAPS = 5
BIN_WIDTH = 64
EPS = 1e-06
HEAD = 192
SHARE = 96
TOK = 256
PAIRS = 512
WIDE = 640
BF = jnp.bfloat16
F32 = jnp.float32
MESH = pl.DeviceIdType.MESH
SCALE = HEAD ** (-0.5)
ROOT2PI = 0.7978845608028654

TOK_AG, COT_AG, OUT_RS, NORM_RS = 0, 16, 32, 48
C_RS, C_AG = 80, 88
W_SIB, HALO, Q_X, DO_X, ST_X, O_X, DQ_X = 96, 100, 104, 108, 112, 116, 120
KV_Z, KV_SIB, DKV_SIB, DKV_Z, G_SIB, G_RS, G_AG = 124, 125, 127, 129, 130, 136, 168
SEMS = 200


def mm(a, b):
    return jnp.dot(a, b, preferred_element_type=F32)


def nt(a, b):
    return lax.dot_general(a, b, (((1,), (1,)), ((), ())), preferred_element_type=F32)


def tn(a, b):
    return lax.dot_general(a, b, (((0,), (0,)), ((), ())), preferred_element_type=F32)


def kernel(
    feat_hbm, toks_hbm, bproj, cw_hbm, cbias, wq, wk, wv, wo, cot_hbm,
    o_layer, c_all, g_all,
    feat, toks, cw, xf, r3, xe, halo, wt, w4, z, slope, tok_own, cot_own, tok_t, cot_t, norm_t,
    q, kv, kn, vn, do, et, dp, st, st_in, o_f, o_send, o_in, ot, fac,
    dq_f, dq_send, dq_in, dkv, dkv_send, dkv_in, z_send, z_in, dqkv, ng,
    n_send, n_in, a_send, a_in, g_part, g_send, g_sib, g_acc, g_in, g_red,
    pgs, c_send, c_in, c_red, ssem, rsem, lsem,
):
    s = lax.axis_index("seq")
    m = lax.axis_index("mp")
    zl = s // 4
    x = s % 4
    c = m % 2
    sib = (s, m + 1 - 2 * c)
    zpart = ((1 - zl) * 4 + x, m)
    sent = []

    def xpeer(r):
        return (zl * 4 + (x + r) % 4, m)

    def seqpeer(r):
        return ((s + r) % 8, m)

    def mppeer(r):
        return (s, (m + r) % 16)

    def push(src, dst, sem, dev):
        copy = pltpu.make_async_remote_copy(
            src_ref=src, dst_ref=dst, send_sem=ssem.at[sem], recv_sem=rsem.at[sem],
            device_id=dev, device_id_type=MESH,
        )
        copy.start()
        sent.append(copy)

    def land(dst, sem):
        pltpu.make_async_remote_copy(
            src_ref=dst, dst_ref=dst, send_sem=ssem.at[sem], recv_sem=rsem.at[sem],
            device_id=sib, device_id_type=MESH,
        ).wait_recv()

    def al(v, n):
        return pl.multiple_of(v, n)

    barrier = pltpu.get_barrier_semaphore()
    for r in range(1, 16):
        pl.semaphore_signal(barrier, inc=1, device_id=mppeer(r), device_id_type=MESH)
    for r in range(1, 8):
        pl.semaphore_signal(barrier, inc=1, device_id=seqpeer(r), device_id_type=MESH)

    loads = [
        pltpu.make_async_copy(toks_hbm, toks, lsem.at[0]),
        pltpu.make_async_copy(feat_hbm, feat, lsem.at[1]),
        pltpu.make_async_copy(cw_hbm, cw, lsem.at[2]),
        pltpu.make_async_copy(cot_hbm, cot_own, lsem.at[3]),
    ]
    for k, w in enumerate((wq, wk, wv, wo)):
        rows = pl.ds(al(HEAD * k + SHARE * c, 32), SHARE)
        loads.append(pltpu.make_async_copy(w, w4.at[rows], lsem.at[4 + k]))
    for load in loads:
        load.start()
    mine = pl.ds(al(SHARE * m, 32), SHARE)

    def spread(own, full, base):
        for r in range(1, 16):
            cols = pl.ds(al(TOK * ((m + r) % 2), TOK), TOK)
            push(own.at[:, cols], full.at[mine], base + r, mppeer(r))

    def keep(own, full):
        full[mine, :] = own[:, pl.ds(al(TOK * c, TOK), TOK)]

    def gathered(full, base):
        for r in range(1, 16):
            rows = pl.ds(al(SHARE * ((m - r + 16) % 16), 32), SHARE)
            land(full.at[rows], base + r)

    pl.semaphore_wait(barrier, 22)
    spread(cot_hbm, cot_t, COT_AG)
    for k, w in enumerate((wo, wq, wk, wv)):
        rows = pl.ds(al(HEAD * ((k + 3) % 4) + SHARE * c, 32), SHARE)
        push(w, w4.at[rows], W_SIB + (k + 3) % 4, sib)

    bp = bproj[...]
    hi = bp.astype(BF).astype(F32)
    mid = (bp - hi).astype(BF).astype(F32)
    low = (bp - hi - mid).astype(BF).astype(F32)
    r3[...] = jnp.zeros_like(r3)
    for k, part in enumerate((hi, mid, low)):
        r3[8 * k : 8 * k + 4, 0:CIN] = part
        r3[8 * k + 4 : 8 * k + 8, CIN:D] = part
    lane = lax.broadcasted_iota(jnp.int32, (128, 32), 0)
    col = lax.broadcasted_iota(jnp.int32, (128, 32), 1)
    group = jnp.where(lane >= BIN_WIDTH, 4, 0)
    counts = jnp.zeros((PAIRS, 32), F32)
    loads[0].wait()
    for b in range(4):
        pick = jnp.where((col < 24) & (col % 8 == group + b), 1.0, 0.0).astype(BF)
        match = jnp.where(toks[...] == b, 1.0, 0.0).astype(BF)
        counts = counts + mm(match, pick)
    comp = (counts * (1.0 / BIN_WIDTH)).astype(BF)
    loads[1].wait()
    for k in range(6):
        xf[k] = feat[:, 128 * k : 128 * k + 128].astype(F32)
    for k in range(0, 6, 2):
        for half in range(2):
            lo = CIN * half + 128 * k
            extra = mm(comp, r3[:, lo : lo + 256].astype(BF))
            for i in range(2):
                own = xf[k + i, pl.ds(half, PAIRS, stride=2), :]
                xe[0:PAIRS, lo + 128 * i : lo + 128 * i + 128] = (own + extra[:, 128 * i : 128 * i + 128]).astype(BF)

    push(xe.at[pl.ds(PAIRS - 16, 16)], halo.at[0], HALO, seqpeer(1))
    push(xe.at[pl.ds(0, 16)], halo.at[1], HALO + 1, seqpeer(7))
    loads[2].wait()
    zero = jnp.zeros((SHARE, CIN), BF)
    left = (cw[0], zero, cw[2], cw[1], cw[4], cw[3])
    right = (cw[1], cw[0], cw[3], cw[2], zero, cw[4])
    for g in range(6):
        wt[SHARE * g : SHARE * g + SHARE, 0:CIN] = left[g]
        wt[SHARE * g : SHARE * g + SHARE, CIN:D] = right[g]

    @pl.loop(0, 2)
    def _(i):
        rows = pl.ds(al(i * 256, 256), 256)
        z[:, rows] = nt(wt[...], xe[rows, :])

    land(halo.at[0], HALO)
    land(halo.at[1], HALO + 1)
    at = lax.broadcasted_iota(jnp.int32, (16, D), 0)
    after = halo[1].astype(F32)
    before = halo[0].astype(F32)
    after = jnp.where((at == 0) & (s < 7), after, 0.0)
    before = jnp.where((at == 15) & (s > 0), before, 0.0)
    xe[PAIRS:WIDE, :] = jnp.zeros((WIDE - PAIRS, D), BF)
    xe[PAIRS : PAIRS + 16, :] = after.astype(BF)
    xe[WIDE - 16 : WIDE, :] = before.astype(BF)
    z[:, PAIRS:WIDE] = nt(wt[...], xe[PAIRS:WIDE, :])

    offset = jnp.transpose(jnp.broadcast_to(cbias[...], (128, SHARE)))[:, 0:1]
    total = jnp.zeros((SHARE, PAIRS), F32)
    for half in range(2):
        r0, r1, r2 = (SHARE * (2 * d + half) for d in range(3))
        pre = pltpu.roll(z[r0 : r0 + SHARE, :], 1, 1)[:, 0:PAIRS]
        pre = pre + z[r1 : r1 + SHARE, 0:PAIRS]
        pre = pre + pltpu.roll(z[r2 : r2 + SHARE, :], WIDE - 1, 1)[:, 0:PAIRS]
        pre = pre + offset
        square = pre * pre
        bend = jnp.tanh(ROOT2PI * (pre + 0.044715 * (square * pre)))
        total = total + pre * (0.5 * (1.0 + bend))
        slope[half] = 0.5 * (1.0 + bend) + (0.5 * pre) * (1.0 - bend * bend) * (
            ROOT2PI * (1.0 + (3.0 * 0.044715) * square)
        )
    tok_own[...] = (0.5 * total).astype(BF)
    spread(tok_own, tok_t, TOK_AG)
    keep(tok_own, tok_t)
    for load in loads[3:]:
        load.wait()
    for k in range(4):
        land(w4.at[pl.ds(al(HEAD * k + SHARE * (1 - c), 32), SHARE)], W_SIB + k)
    keep(cot_own, cot_t)
    gathered(cot_t, COT_AG)
    do[0] = mm(w4[3 * HEAD : 4 * HEAD, :], cot_t[...]).astype(BF)
    for r in range(1, 4):
        push(do.at[0], do.at[r], DO_X + r, xpeer(r))
    gathered(tok_t, TOK_AG)
    wide = tok_t[...].astype(F32)
    inverse = lax.rsqrt(jnp.sum(wide * wide, axis=0, keepdims=True) * (1.0 / D) + EPS)
    norm_t[...] = (wide * inverse).astype(BF)
    qkv = mm(w4[0 : 3 * HEAD, :], norm_t[...]).astype(BF)
    q[0] = qkv[0:HEAD]
    kv[0] = qkv[HEAD : 3 * HEAD]
    push(kv.at[0], kv.at[2], KV_Z, zpart)
    push(kv.at[0], kv.at[1], KV_SIB, sib)
    for r in range(1, 4):
        push(q.at[0], q.at[r], Q_X + r, xpeer(r))

    land(kv.at[2], KV_Z)
    push(kv.at[2], kv.at[3], KV_SIB + 1, sib)
    land(kv.at[1], KV_SIB)
    land(kv.at[3], KV_SIB + 1)
    for i in range(4):
        kn[i] = jnp.transpose(kv[i, 0:HEAD].astype(F32)).astype(BF)
        vn[i] = jnp.transpose(kv[i, HEAD : 2 * HEAD].astype(F32)).astype(BF)
    for r in range(1, 4):
        land(q.at[r], Q_X + r)
        land(do.at[r], DO_X + r)

    @pl.loop(0, 4)
    def _(j):
        top = jnp.full((1, TOK), -jnp.inf, F32)
        for i in range(4):
            scores = mm(kn[i], q[j]) * SCALE
            et[j, TOK * i : TOK * i + TOK, :] = scores
            top = jnp.maximum(top, jnp.max(scores, axis=0, keepdims=True))
        norm = jnp.zeros((1, TOK), F32)
        delta = jnp.zeros((1, TOK), F32)
        out = jnp.zeros((HEAD, TOK), F32)
        for i in range(4):
            rows = slice(TOK * i, TOK * i + TOK)
            e = jnp.exp(et[j, rows, :] - top)
            et[j, rows, :] = e
            norm = norm + jnp.sum(e, axis=0, keepdims=True)
            out = out + mm(kv[i, HEAD : 2 * HEAD, :], e.astype(BF))
            grad = mm(vn[i], do[j])
            dp[j, rows, :] = grad
            delta = delta + jnp.sum(e * grad, axis=0, keepdims=True)
        o_f[j] = out
        st[j, 0:1, :] = top
        st[j, 1:2, :] = norm
        st[j, 2:3, :] = delta
        st[j, 3:8, :] = jnp.zeros((5, TOK), F32)

    for r in range(1, 4):
        push(st, st_in.at[r], ST_X + r, xpeer(r))
    for r in range(1, 4):
        land(st_in.at[r], ST_X + r)

    factors = []
    deltas = []
    for j in range(4):
        every = [st[j]] + [st_in[r, (j - r) % 4] for r in range(1, 4)]
        top = functools.reduce(jnp.maximum, [e[0:1] for e in every])
        norm = sum(e[1:2] * jnp.exp(e[0:1] - top) for e in every)
        log_total = jnp.log(norm) + top
        factors.append(jnp.exp(every[0][0:1] - log_total))
        deltas.append(sum(e[2:3] * jnp.exp(e[0:1] - log_total) for e in every))
        o_f[j] = o_f[j] * factors[j]
    for j in range(4):
        fac[j, 0:1, :] = factors[j]
        fac[j, 1:2, :] = deltas[j]
    for r in range(1, 4):
        o_send[r] = o_f[r].astype(BF)
        push(o_send.at[r], o_in.at[4 - r], O_X + 4 - r, xpeer(4 - r))

    dkv[...] = jnp.zeros_like(dkv)

    @pl.loop(0, 4)
    def _(j):
        factor = fac[j, 0:1, :]
        delta = fac[j, 1:2, :]
        grad_q = jnp.zeros((HEAD, TOK), F32)
        for i in range(4):
            rows = slice(TOK * i, TOK * i + TOK)
            p = et[j, rows, :] * factor
            ds = (p * (dp[j, rows, :] - delta) * SCALE).astype(BF)
            grad_q = grad_q + mm(kv[i, 0:HEAD, :], ds)
            dkv[i, 0:HEAD, :] += nt(q[j], ds)
            dkv[i, HEAD : 2 * HEAD, :] += nt(do[j], p.astype(BF))
        dq_f[j] = grad_q

    dkv_send[0] = dkv[3].astype(BF)
    push(dkv_send.at[0], dkv_in.at[0], DKV_SIB, sib)
    dkv_send[1] = dkv[1].astype(BF)
    push(dkv_send.at[1], dkv_in.at[1], DKV_SIB + 1, sib)
    for r in range(1, 4):
        dq_send[r] = dq_f[r].astype(BF)
        push(dq_send.at[r], dq_in.at[4 - r], DQ_X + 4 - r, xpeer(4 - r))
    land(dkv_in.at[0], DKV_SIB)
    z_send[...] = (dkv[2] + dkv_in[0].astype(F32)).astype(BF)
    push(z_send, z_in, DKV_Z, zpart)

    def grad_w(k, grads, inputs):
        g_part[HEAD * k : HEAD * k + HEAD, :] = nt(grads[...], inputs[...])
        g_send[k] = g_part[pl.ds(al(HEAD * k + SHARE * (1 - c), 32), SHARE), :].astype(BF)
        push(g_send.at[k], g_sib.at[k], G_SIB + k, sib)

    def grad_sum(k):
        land(g_sib.at[k], G_SIB + k)
        own = g_part[pl.ds(al(HEAD * k + SHARE * c, 32), SHARE), :]
        g_acc[k] = (own + g_sib[k].astype(F32)).astype(BF)
        for r in range(1, 8):
            push(g_piece(g_acc, k, (s + r) % 8), g_in.at[r, k], G_RS + 8 * k + r, seqpeer(r))

    def g_piece(buf, k, seq):
        return buf.at[k, pl.ds(al(48 * (seq // 4), 16), 48), pl.ds(al(384 * (seq % 4), 128), 384)]

    for r in range(1, 4):
        land(o_in.at[r], O_X + r)
    ot[...] = (o_f[0] + sum(o_in[r].astype(F32) for r in range(1, 4))).astype(BF)

    def scatter(send, into, base):
        for r in range(1, 16):
            rows = pl.ds(al(SHARE * ((m + r) % 16), 32), SHARE)
            push(send.at[rows], into.at[r], base + r, mppeer(r))
        into[0] = send[mine, :]

    def reduced(into, base):
        for r in range(1, 16):
            land(into.at[r], base + r)
        same = sum(into[r].astype(F32) for r in range(0, 16, 2))
        other = sum(into[r].astype(F32) for r in range(1, 16, 2))
        first = jnp.where(c == 0, same, other)
        second = jnp.where(c == 0, other, same)
        return first, second

    @pl.loop(0, 4)
    def _(k):
        cols = pl.ds(al(384 * k, 128), 384)
        a_send[cols, :] = tn(w4[3 * HEAD : 4 * HEAD, cols], ot[...]).astype(BF)

    scatter(a_send, a_in, OUT_RS)
    grad_w(3, ot, cot_t)

    land(dkv_in.at[1], DKV_SIB + 1)
    for r in range(1, 4):
        land(dq_in.at[r], DQ_X + r)
    grad_q = dq_f[0] + sum(dq_in[r].astype(F32) for r in range(1, 4))
    dqkv[0:HEAD, :] = grad_q.astype(BF)
    land(z_in, DKV_Z)
    dqkv[HEAD : 3 * HEAD, :] = (dkv[0] + dkv_in[1].astype(F32) + z_in[...].astype(F32)).astype(BF)

    @pl.loop(0, 4)
    def _(k):
        cols = pl.ds(al(384 * k, 128), 384)
        ng[cols, :] = tn(w4[0 : 3 * HEAD, cols], dqkv[...])

    wide = tok_t[...].astype(F32)
    inverse = lax.rsqrt(jnp.sum(wide * wide, axis=0, keepdims=True) * (1.0 / D) + EPS)
    unit = wide * inverse
    row_stat = jnp.sum(ng[...] * unit, axis=0, keepdims=True) * (1.0 / D)
    n_send[...] = (inverse * (ng[...] - unit * row_stat)).astype(BF)
    scatter(n_send, n_in, NORM_RS)

    for k in range(3):
        grad_w(k, dqkv.at[HEAD * k : HEAD * k + HEAD], norm_t)
    for k in (3, 0, 1, 2):
        grad_sum(k)

    tok_wide = tok_own[...].astype(F32)
    first, second = reduced(a_in, OUT_RS)
    out = jnp.concatenate([first, second], axis=1) + tok_wide
    o_layer[...] = out.astype(BF)

    first, second = reduced(n_in, NORM_RS)
    tok_grad = cot_own[...].astype(F32) + jnp.concatenate([first, second], axis=1)
    pad = jnp.zeros((SHARE, WIDE - PAIRS), F32)
    for half in range(2):
        pg = jnp.concatenate([0.5 * tok_grad * slope[half], pad], axis=1)
        for d in range(3):
            shift = (WIDE - 1, 0, 1)[d]
            moved = pltpu.roll(pg, shift, 1) if shift else pg
            row = SHARE * (2 * d + half)
            pgs[row : row + SHARE, :] = moved.astype(BF)
    both = pgs[2 * SHARE : 3 * SHARE, 0:PAIRS], pgs[3 * SHARE : 4 * SHARE, 0:PAIRS]
    ones = jnp.ones((16, PAIRS), BF)
    bias = nt(ones, both[0]) + nt(ones, both[1])
    c_send[TAPS * SHARE :, :] = jnp.zeros((32, CIN), BF)
    c_send[TAPS * SHARE : TAPS * SHARE + 16, 0:SHARE] = bias.astype(BF)

    @pl.loop(0, 3)
    def _(k):
        cols = pl.ds(al(256 * k, 256), 256)
        odd_cols = pl.ds(al(CIN + 256 * k, 256), 256)
        me = mm(pgs[...], xe[:, cols])
        mo = mm(pgs[...], xe[:, odd_cols])

        def part(arr, d, half):
            row = SHARE * (2 * (d + 1) + half)
            return arr[row : row + SHARE]

        taps = (
            part(me, -1, 0) + part(mo, -1, 1),
            part(mo, -1, 0) + part(me, 0, 1),
            part(me, 0, 0) + part(mo, 0, 1),
            part(mo, 0, 0) + part(me, 1, 1),
            part(me, 1, 0) + part(mo, 1, 1),
        )
        for t in range(TAPS):
            c_send[SHARE * t : SHARE * t + SHARE, cols] = taps[t].astype(BF)

    def c_piece(buf, seq):
        return buf.at[pl.ds(al(64 * seq, 64), 64)]

    for r in range(1, 8):
        push(c_piece(c_send, (s + r) % 8), c_in.at[r], C_RS + r, seqpeer(r))

    own_rows = pl.ds(al(48 * zl, 16), 48)
    own_cols = pl.ds(al(384 * x, 128), 384)
    for k in (3, 0, 1, 2):
        acc = g_acc[k, own_rows, own_cols].astype(F32)
        for r in range(1, 8):
            land(g_in.at[r, k], G_RS + 8 * k + r)
            acc = acc + g_in[r, k].astype(F32)
        g_red[k] = acc.astype(BF)
        for r in range(1, 8):
            push(g_red.at[k], g_piece(g_all, k, s), G_AG + 8 * k + r, seqpeer(r))
        g_all[k, own_rows, own_cols] = g_red[k]

    for r in range(1, 8):
        land(c_in.at[r], C_RS + r)
    acc = c_send[pl.ds(al(64 * s, 64), 64), :].astype(F32)
    for r in range(1, 8):
        acc = acc + c_in[r].astype(F32)
    c_red[...] = acc.astype(BF)
    for r in range(1, 8):
        push(c_red, c_piece(c_all, s), C_AG + r, seqpeer(r))
    c_all[pl.ds(al(64 * s, 64), 64), :] = c_red[...]

    for r in range(1, 8):
        for k in range(4):
            land(g_piece(g_all, k, (s - r + 8) % 8), G_AG + 8 * k + r)
    for r in range(1, 8):
        land(c_piece(c_all, (s - r + 8) % 8), C_AG + r)
    for copy in sent:
        copy.wait_send()


def scratch():
    def v(*shape, dtype=BF):
        return pltpu.VMEM(shape, dtype)

    return [
        v(1024, CIN), v(PAIRS, 128, dtype=jnp.int32), v(TAPS, SHARE, CIN),
        v(6, 1024, 128, dtype=F32), v(32, D, dtype=F32), v(WIDE, D), v(2, 16, D), v(576, D), v(768, D),
        v(576, WIDE, dtype=F32), v(2, SHARE, PAIRS, dtype=F32), v(SHARE, PAIRS), v(SHARE, PAIRS),
        v(D, TOK), v(D, TOK), v(D, TOK),
        v(4, HEAD, TOK), v(4, 384, TOK), v(4, TOK, HEAD), v(4, TOK, HEAD), v(4, HEAD, TOK),
        v(4, 1024, TOK, dtype=F32), v(4, 1024, TOK, dtype=F32),
        v(4, 8, TOK, dtype=F32), v(4, 4, 8, TOK, dtype=F32),
        v(4, HEAD, TOK, dtype=F32), v(4, HEAD, TOK), v(4, HEAD, TOK), v(HEAD, TOK),
        v(4, 8, TOK, dtype=F32),
        v(4, HEAD, TOK, dtype=F32), v(4, HEAD, TOK), v(4, HEAD, TOK),
        v(4, 384, TOK, dtype=F32), v(2, 384, TOK), v(2, 384, TOK), v(384, TOK), v(384, TOK),
        v(576, TOK), v(D, TOK, dtype=F32),
        v(D, TOK), v(16, SHARE, TOK), v(D, TOK), v(16, SHARE, TOK),
        v(768, D, dtype=F32), v(4, SHARE, D), v(4, SHARE, D), v(4, SHARE, D),
        v(8, 4, 48, 384), v(4, 48, 384),
        v(576, WIDE), v(512, CIN), v(8, 64, CIN), v(64, CIN),
        pltpu.SemaphoreType.DMA((SEMS,)), pltpu.SemaphoreType.DMA((SEMS,)), pltpu.SemaphoreType.DMA((8,)),
    ]


def widen(layer, conv, grads, o_layer, o_conv, o_bias, o_q, o_k, o_v, o_o):
    for t in range(TAPS):
        o_conv[t] = conv[SHARE * t : SHARE * t + SHARE, :].astype(F32)
    o_bias[...] = conv[TAPS * SHARE : TAPS * SHARE + 16, 0:SHARE].astype(F32)[0:1]
    for k, o in enumerate((o_q, o_k, o_v, o_o)):
        o[...] = grads[k].astype(F32)
    o_layer[...] = layer[...]


def body(features, base_tokens, base_proj, conv_weight, conv_bias, w_query, w_key, w_value, w_out, cotangent):
    vmem = pl.BlockSpec(memory_space=pltpu.VMEM)
    hbm = pl.BlockSpec(memory_space=pl.ANY)
    layer = jax.ShapeDtypeStruct((SHARE, PAIRS), BF)
    narrow = pl.pallas_call(
        kernel,
        out_shape=(layer, jax.ShapeDtypeStruct((512, CIN), BF), jax.ShapeDtypeStruct((4, SHARE, D), BF)),
        in_specs=[hbm, hbm, vmem, hbm, vmem, hbm, hbm, hbm, hbm, hbm],
        out_specs=(vmem,) * 3,
        scratch_shapes=scratch(),
        compiler_params=pltpu.CompilerParams(
            collective_id=0, has_side_effects=True, vmem_limit_bytes=60 * 1024 * 1024
        ),
        cost_estimate=pl.CostEstimate(flops=8_000_000_000, bytes_accessed=8_000_000, transcendentals=1_300_000),
        name="section",
    )(
        features, base_tokens.reshape(PAIRS, 128), base_proj, conv_weight, conv_bias.reshape(1, SHARE),
        w_query, w_key, w_value, w_out, cotangent.T,
    )
    square = jax.ShapeDtypeStruct((SHARE, D), F32)
    layer, conv, bias, gq, gk, gv, go = pl.pallas_call(
        widen,
        out_shape=(
            layer, jax.ShapeDtypeStruct((TAPS, SHARE, CIN), F32), jax.ShapeDtypeStruct((1, SHARE), F32),
            square, square, square, square,
        ),
        in_specs=[vmem] * 3,
        out_specs=(vmem,) * 7,
        compiler_params=pltpu.CompilerParams(vmem_limit_bytes=32 * 1024 * 1024),
        name="widen",
    )(*narrow)
    return layer.T, conv, bias.reshape(SHARE), gq, gk, gv, go


def solution(mesh):
    placed = (
        P("seq", None), P("seq"), P(), P(None, "mp", None), P("mp"),
        P("mp", None), P("mp", None), P("mp", None), P("mp", None), P("seq", "mp"),
    )
    return jax.shard_map(
        body,
        mesh=mesh,
        in_specs=placed,
        out_specs=(
            P("seq", "mp"), P(None, "mp", None), P("mp"),
            P("mp", None), P("mp", None), P("mp", None), P("mp", None),
        ),
        check_vma=False,
    )
```

```python
import functools

import jax
import jax.numpy as jnp
from jax import lax
from jax.experimental import pallas as pl
from jax.experimental.pallas import tpu as pltpu
from jax.sharding import PartitionSpec as P

D = 1536
CIN = 768
TAPS = 5
BIN_WIDTH = 64
EPS = 1e-06
HEAD = 192
SHARE = 96
TOK = 256
PAIRS = 512
WIDE = 640
BF = jnp.bfloat16
F32 = jnp.float32
MESH = pl.DeviceIdType.MESH
SCALE = HEAD ** (-0.5)
ROOT2PI = 0.7978845608028654

(
    COT_AG, TOK_AG, W_SIB, HALO, Q_X, DO_X, ST_X, O_X, DQ_X, KV_Z, KV_SIB, KV_FWD, DKV_FAR, DKV_SIB, DKV_Z,
    OUT_Y, OUT_Z, OUT_SIB, NORM_RS,
) = range(19)
G_SIB = 19
G_STEP = G_SIB + 4
C_STEP = G_STEP + 16
SEMS = C_STEP + 8


def mm(a, b):
    return jnp.dot(a, b, preferred_element_type=F32)


def nt(a, b):
    return lax.dot_general(a, b, (((1,), (1,)), ((), ())), preferred_element_type=F32)


def tn(a, b):
    return lax.dot_general(a, b, (((0,), (0,)), ((), ())), preferred_element_type=F32)


def kernel(
    feat_hbm, toks_hbm, bproj, cw_hbm, cbias, wq, wk, wv, wo, cot_hbm,
    o_layer, c_all, g_all,
    feat, toks, cw, w_t, wo_t, xf, r3, xe, halo, wt, w4, z, slope, tok_own, cot_own, tok_t, cot_t, norm_t,
    q, kv, kn, vn, do, et, dp, st, st_in, o_f, o_send, o_in, ot, fac,
    dq_f, dq_send, dq_in, dkv, dkv_send, dkv_in, z_send, z_in, dqkv, ng,
    n_send, n_in, a_send, ay_in, az_send, az_in, az_own, as_send, as_in,
    g_part, g_send, g_sib, g_acc, gx_in, gz_send, gz_in, gbz_in, gb_held, gx_b, g_red,
    pgs, c_send, cx_in, cz_send, cz_in, cbz_in, cb_held, cx_b, c_red, ssem, rsem, lsem,
):
    s = lax.axis_index("seq")
    m = lax.axis_index("mp")
    zl = s // 4
    x = s % 4
    c = m % 2
    sib = (s, m + 1 - 2 * c)
    zpart = ((1 - zl) * 4 + x, m)
    sent = {}

    def xpeer(r):
        return (zl * 4 + (x + r) % 4, m)

    def seqpeer(r):
        return ((s + r) % 8, m)

    def mppeer(r):
        return (s, (m + r) % 16)

    def push(src, dst, sem, dev):
        pltpu.make_async_remote_copy(
            src_ref=src, dst_ref=dst, send_sem=ssem.at[sem], recv_sem=rsem.at[sem],
            device_id=dev, device_id_type=MESH,
        ).start()

    def land(whole, sem):
        copy = pltpu.make_async_remote_copy(
            src_ref=whole, dst_ref=whole, send_sem=ssem.at[sem], recv_sem=rsem.at[sem],
            device_id=sib, device_id_type=MESH,
        )
        copy.wait_recv()
        sent[sem] = copy

    def al(v, n):
        return pl.multiple_of(v, n)

    barrier = pltpu.get_barrier_semaphore()
    for r in range(1, 16):
        pl.semaphore_signal(barrier, inc=1, device_id=mppeer(r), device_id_type=MESH)
    for r in range(1, 8):
        pl.semaphore_signal(barrier, inc=1, device_id=seqpeer(r), device_id_type=MESH)

    loads = [
        pltpu.make_async_copy(toks_hbm, toks, lsem.at[0]),
        pltpu.make_async_copy(feat_hbm, feat, lsem.at[1]),
        pltpu.make_async_copy(cw_hbm, cw, lsem.at[2]),
        pltpu.make_async_copy(cot_hbm, cot_own, lsem.at[3]),
    ]
    for k, w in enumerate((wq, wk, wv, wo)):
        rows = pl.ds(al(HEAD * k + SHARE * c, 32), SHARE)
        loads.append(pltpu.make_async_copy(w, w4.at[rows], lsem.at[4 + k]))
    for load in loads:
        load.start()
    mine = pl.ds(al(SHARE * m, 32), SHARE)

    def spread(own, full, base):
        for r in range(1, 16):
            cols = pl.ds(al(TOK * ((m + r) % 2), TOK), TOK)
            push(own.at[:, cols], full.at[mine], base, mppeer(r))

    def keep(own, full):
        full[mine, :] = own[:, pl.ds(al(TOK * c, TOK), TOK)]

    def gathered(full, base):
        land(full.at[0 : 15 * SHARE], base)

    pl.semaphore_wait(barrier, 22)
    spread(cot_hbm, cot_t, COT_AG)
    for k, w in enumerate((wo, wq, wk, wv)):
        rows = pl.ds(al(HEAD * ((k + 3) % 4) + SHARE * c, 32), SHARE)
        push(w, w4.at[rows], W_SIB, sib)

    bp = bproj[...]
    hi = bp.astype(BF).astype(F32)
    mid = (bp - hi).astype(BF).astype(F32)
    low = (bp - hi - mid).astype(BF).astype(F32)
    r3[...] = jnp.zeros_like(r3)
    for k, part in enumerate((hi, mid, low)):
        r3[8 * k : 8 * k + 4, 0:CIN] = part
        r3[8 * k + 4 : 8 * k + 8, CIN:D] = part
    lane = lax.broadcasted_iota(jnp.int32, (128, 32), 0)
    col = lax.broadcasted_iota(jnp.int32, (128, 32), 1)
    group = jnp.where(lane >= BIN_WIDTH, 4, 0)
    counts = jnp.zeros((PAIRS, 32), F32)
    loads[0].wait()
    for b in range(4):
        pick = jnp.where((col < 24) & (col % 8 == group + b), 1.0, 0.0).astype(BF)
        match = jnp.where(toks[...] == b, 1.0, 0.0).astype(BF)
        counts = counts + mm(match, pick)
    comp = (counts * (1.0 / BIN_WIDTH)).astype(BF)
    loads[1].wait()
    for k in range(6):
        xf[k] = feat[:, 128 * k : 128 * k + 128].astype(F32)
    for k in range(0, 6, 2):
        for half in range(2):
            lo = CIN * half + 128 * k
            extra = mm(comp, r3[:, lo : lo + 256].astype(BF))
            for i in range(2):
                own = xf[k + i, pl.ds(half, PAIRS, stride=2), :]
                xe[0:PAIRS, lo + 128 * i : lo + 128 * i + 128] = (own + extra[:, 128 * i : 128 * i + 128]).astype(BF)

    push(xe.at[pl.ds(PAIRS - 16, 16)], halo.at[0], HALO, seqpeer(1))
    push(xe.at[pl.ds(0, 16)], halo.at[1], HALO, seqpeer(7))
    loads[2].wait()
    zero = jnp.zeros((SHARE, CIN), BF)
    left = (cw[0], zero, cw[2], cw[1], cw[4], cw[3])
    right = (cw[1], cw[0], cw[3], cw[2], zero, cw[4])
    for g in range(6):
        wt[SHARE * g : SHARE * g + SHARE, 0:CIN] = left[g]
        wt[SHARE * g : SHARE * g + SHARE, CIN:D] = right[g]

    @pl.loop(0, 2)
    def _(i):
        rows = pl.ds(al(i * 256, 256), 256)
        z[:, rows] = nt(wt[...], xe[rows, :])

    land(halo, HALO)
    at = lax.broadcasted_iota(jnp.int32, (16, D), 0)
    after = halo[1].astype(F32)
    before = halo[0].astype(F32)
    after = jnp.where((at == 0) & (s < 7), after, 0.0)
    before = jnp.where((at == 15) & (s > 0), before, 0.0)
    xe[PAIRS:WIDE, :] = jnp.zeros((WIDE - PAIRS, D), BF)
    xe[PAIRS : PAIRS + 16, :] = after.astype(BF)
    xe[WIDE - 16 : WIDE, :] = before.astype(BF)
    z[:, PAIRS:WIDE] = nt(wt[...], xe[PAIRS:WIDE, :])

    offset = jnp.transpose(jnp.broadcast_to(cbias[...], (128, SHARE)))[:, 0:1]
    total = jnp.zeros((SHARE, PAIRS), F32)
    for half in range(2):
        r0, r1, r2 = (SHARE * (2 * d + half) for d in range(3))
        pre = pltpu.roll(z[r0 : r0 + SHARE, :], 1, 1)[:, 0:PAIRS]
        pre = pre + z[r1 : r1 + SHARE, 0:PAIRS]
        pre = pre + pltpu.roll(z[r2 : r2 + SHARE, :], WIDE - 1, 1)[:, 0:PAIRS]
        pre = pre + offset
        square = pre * pre
        bend = jnp.tanh(ROOT2PI * (pre + 0.044715 * (square * pre)))
        total = total + pre * (0.5 * (1.0 + bend))
        slope[half] = 0.5 * (1.0 + bend) + (0.5 * pre) * (1.0 - bend * bend) * (
            ROOT2PI * (1.0 + (3.0 * 0.044715) * square)
        )
    tok_own[...] = (0.5 * total).astype(BF)
    spread(tok_own, tok_t, TOK_AG)
    keep(tok_own, tok_t)
    for load in loads[3:]:
        load.wait()
    land(w4.at[0 : 4 * SHARE], W_SIB)
    keep(cot_own, cot_t)
    gathered(cot_t, COT_AG)
    do[0] = mm(w4[3 * HEAD : 4 * HEAD, :], cot_t[...]).astype(BF)
    for r in range(1, 4):
        push(do.at[0], do.at[r], DO_X, xpeer(r))

    @pl.loop(0, 4)
    def _(k):
        cols = pl.ds(al(384 * k, 128), 384)
        w_t[cols, :] = jnp.transpose(w4[0 : 3 * HEAD, cols].astype(F32)).astype(BF)
        wo_t[cols, :] = jnp.transpose(w4[3 * HEAD : 4 * HEAD, cols].astype(F32)).astype(BF)

    gathered(tok_t, TOK_AG)
    wide = tok_t[...].astype(F32)
    inverse = lax.rsqrt(jnp.sum(wide * wide, axis=0, keepdims=True) * (1.0 / D) + EPS)
    norm_t[...] = (wide * inverse).astype(BF)
    qkv = mm(w4[0 : 3 * HEAD, :], norm_t[...]).astype(BF)
    q[0] = qkv[0:HEAD]
    kv[0] = qkv[HEAD : 3 * HEAD]
    push(kv.at[0], kv.at[2], KV_Z, zpart)
    push(kv.at[0], kv.at[1], KV_SIB, sib)
    for r in range(1, 4):
        push(q.at[0], q.at[r], Q_X, xpeer(r))

    land(kv.at[2], KV_Z)
    push(kv.at[2], kv.at[3], KV_FWD, sib)

    def turn(i):
        kn[i] = jnp.transpose(kv[i, 0:HEAD].astype(F32)).astype(BF)
        vn[i] = jnp.transpose(kv[i, HEAD : 2 * HEAD].astype(F32)).astype(BF)

    turn(0)
    land(kv.at[1], KV_SIB)
    turn(1)
    turn(2)
    land(q.at[1:4], Q_X)
    land(do.at[1:4], DO_X)
    land(kv.at[3], KV_FWD)
    turn(3)
    @pl.loop(0, 4)
    def _(j):
        top = jnp.full((1, TOK), -jnp.inf, F32)
        for i in range(4):
            scores = mm(kn[i], q[j]) * SCALE
            et[j, TOK * i : TOK * i + TOK, :] = scores
            top = jnp.maximum(top, jnp.max(scores, axis=0, keepdims=True))
        norm = jnp.zeros((1, TOK), F32)
        delta = jnp.zeros((1, TOK), F32)
        out = jnp.zeros((HEAD, TOK), F32)
        for i in range(4):
            rows = slice(TOK * i, TOK * i + TOK)
            e = jnp.exp(et[j, rows, :] - top)
            et[j, rows, :] = e
            norm = norm + jnp.sum(e, axis=0, keepdims=True)
            out = out + mm(kv[i, HEAD : 2 * HEAD, :], e.astype(BF))
            grad = mm(vn[i], do[j])
            dp[j, rows, :] = grad
            delta = delta + jnp.sum(e * grad, axis=0, keepdims=True)
        o_f[j] = out
        st[j, 0:1, :] = top
        st[j, 1:2, :] = norm
        st[j, 2:3, :] = delta
        st[j, 3:8, :] = jnp.zeros((5, TOK), F32)
        for r in range(1, 4):
            push(st.at[j], st_in.at[r, (j + r) % 4], ST_X, xpeer(r))

    land(st_in.at[1:4], ST_X)

    factors = []
    deltas = []
    for j in range(4):
        every = [st[j]] + [st_in[r, j] for r in range(1, 4)]
        top = functools.reduce(jnp.maximum, [e[0:1] for e in every])
        norm = sum(e[1:2] * jnp.exp(e[0:1] - top) for e in every)
        log_total = jnp.log(norm) + top
        factors.append(jnp.exp(every[0][0:1] - log_total))
        deltas.append(sum(e[2:3] * jnp.exp(e[0:1] - log_total) for e in every))
    for j in range(4):
        fac[j, 0:1, :] = factors[j]
        fac[j, 1:2, :] = deltas[j]
    for r in range(1, 4):
        o_send[r] = (o_f[r] * factors[r]).astype(BF)
        push(o_send.at[r], o_in.at[4 - r], O_X, xpeer(4 - r))

    def backward(i):
        rows = slice(TOK * i, TOK * i + TOK)
        dkv[i] = jnp.zeros((2 * HEAD, TOK), F32)

        @pl.loop(0, 4)
        def _(j):
            p = et[j, rows, :] * fac[j, 0:1, :]
            ds = (p * (dp[j, rows, :] - fac[j, 1:2, :]) * SCALE).astype(BF)
            part = mm(kv[i, 0:HEAD, :], ds)
            dq_f[j] = part if i == 3 else dq_f[j] + part
            dkv[i, 0:HEAD, :] += nt(q[j], ds)
            dkv[i, HEAD : 2 * HEAD, :] += nt(do[j], p.astype(BF))

    backward(3)
    dkv_send[0] = dkv[3].astype(BF)
    push(dkv_send.at[0], dkv_in.at[0], DKV_FAR, sib)
    backward(2)
    land(dkv_in.at[0], DKV_FAR)
    z_send[...] = (dkv[2] + dkv_in[0].astype(F32)).astype(BF)
    push(z_send, z_in, DKV_Z, zpart)
    backward(1)
    dkv_send[1] = dkv[1].astype(BF)
    push(dkv_send.at[1], dkv_in.at[1], DKV_SIB, sib)
    backward(0)
    for r in range(1, 4):
        dq_send[r] = dq_f[r].astype(BF)
        push(dq_send.at[r], dq_in.at[4 - r], DQ_X, xpeer(4 - r))

    def grad_w(k, grads, inputs):
        g_part[HEAD * k : HEAD * k + HEAD, :] = nt(grads[...], inputs[...])
        g_send[k] = g_part[pl.ds(al(HEAD * k + SHARE * (1 - c), 32), SHARE), :].astype(BF)
        push(g_send.at[k], g_sib.at[k], G_SIB + k, sib)

    def grad_sum(k):
        land(g_sib.at[k], G_SIB + k)
        own = g_part[pl.ds(al(HEAD * k + SHARE * c, 32), SHARE), :]
        g_acc[k] = (own + g_sib[k].astype(F32)).astype(BF)

    def g_col(k):
        return lambda buf, at: buf.at[k, :, pl.ds(al(384 * at, 128), 384)]

    def g_row(k):
        return lambda buf, at: buf.at[k, pl.ds(al(48 * at, 16), 48), :]

    def g_piece(k):
        return lambda buf, z, at: buf.at[k, pl.ds(al(48 * z, 16), 48), pl.ds(al(384 * at, 128), 384)]

    def c_col(buf, at):
        return buf.at[:, pl.ds(al(64 * at, 64), 64), 0:384]

    def c_row(buf, at):
        return buf.at[at, :, 384:CIN]

    def c_piece(lanes):
        return lambda buf, z, at: buf.at[z, pl.ds(al(64 * at, 64), 64), lanes]

    def a_first(src, col, into, sem):
        for r in range(1, 4):
            push(col(src, (x + r) % 4), into.at[r], sem, xpeer(r))

    def a_second(src, piece, into, part, send, into_z, sem):
        land(into.at[1:4], sem)

        def total(z):
            own = piece(src, z, x)[...].astype(F32)
            return own + sum(part(into, r, z)[...].astype(F32) for r in range(1, 4))

        send[...] = total(1 - zl).astype(BF)
        push(send, into_z, sem + 1, zpart)
        return total(zl)

    def a_third(held, piece, full, red, into_z, sem):
        land(into_z, sem + 1)
        red[...] = (held + into_z[...].astype(F32)).astype(BF)
        push(red, piece(full, zl, x), sem + 2, zpart)
        piece(full, zl, x)[...] = red[...]

    def a_fourth(col, full, red, sem):
        land(red, sem + 2)
        for r in range(1, 4):
            push(col(full, x), col(full, x), sem + 3, xpeer(r))

    def b_first(src, row, into_z, sem):
        push(row(src, 1 - zl), into_z, sem, zpart)

    def b_second(src, row, part, held, into_z, into, sem):
        land(into_z, sem)
        held[...] = (row(src, zl)[...].astype(F32) + into_z[...].astype(F32)).astype(BF)
        for r in range(1, 4):
            push(part(held, (x + r) % 4), into.at[r], sem + 1, xpeer(r))

    def b_third(part, piece, full, held, into, red, sem):
        land(into.at[1:4], sem + 1)
        red[...] = (part(held, x)[...].astype(F32) + sum(into[r].astype(F32) for r in range(1, 4))).astype(BF)
        for r in range(1, 4):
            push(red, piece(full, zl, x), sem + 2, xpeer(r))
        piece(full, zl, x)[...] = red[...]

    def b_fourth(row, full, into, sem):
        land(into.at[1:4], sem + 2)
        push(row(full, zl), row(full, zl), sem + 3, zpart)

    def ga_part(buf, r, z):
        return buf.at[r, pl.ds(al(48 * z, 16), 48), :]

    def ca_part(buf, r, z):
        return buf.at[r, z]

    def gb_part(buf, at):
        return buf.at[:, pl.ds(al(384 * at, 128), 384)]

    def cb_part(buf, at):
        return buf.at[pl.ds(al(64 * at, 64), 64)]

    def scatter(send, into, base):
        for r in range(1, 16):
            rows = pl.ds(al(SHARE * ((m + r) % 16), 32), SHARE)
            push(send.at[rows], into.at[r], base, mppeer(r))
        into[0] = send[mine, :]

    def reduced(into, base):
        land(into.at[1:16], base)
        same = sum(into[r].astype(F32) for r in range(0, 16, 2))
        other = sum(into[r].astype(F32) for r in range(1, 16, 2))
        first = jnp.where(c == 0, same, other)
        second = jnp.where(c == 0, other, same)
        return first, second

    land(o_in.at[1:4], O_X)
    ot[...] = (o_f[0] * factors[0] + sum(o_in[r].astype(F32) for r in range(1, 4))).astype(BF)
    grad_w(3, ot, cot_t)

    @pl.loop(0, 4)
    def _(k):
        cols = pl.ds(al(384 * k, 128), 384)
        a_send[k // 2, pl.ds(al(384 * (k % 2), 128), 384), :] = mm(wo_t[cols, :], ot[...]).astype(BF)

    y = (m // 2) % 4
    zh = m // 8
    for r in range(1, 4):
        rows = pl.ds(al(HEAD * ((y + r) % 4), 64), HEAD)
        push(a_send.at[:, rows], ay_in.at[r], OUT_Y, (s, zh * 8 + ((y + r) % 4) * 2 + c))
    grad_sum(3)
    a_first(g_acc, g_col(3), gx_in.at[3], G_STEP + 12)

    land(dkv_in.at[1], DKV_SIB)
    land(z_in, DKV_Z)
    dqkv[HEAD : 3 * HEAD, :] = (dkv[0] + dkv_in[1].astype(F32) + z_in[...].astype(F32)).astype(BF)
    land(dq_in.at[1:4], DQ_X)
    grad_q = dq_f[0] + sum(dq_in[r].astype(F32) for r in range(1, 4))
    dqkv[0:HEAD, :] = grad_q.astype(BF)

    @pl.loop(0, 4)
    def _(k):
        cols = pl.ds(al(384 * k, 128), 384)
        ng[cols, :] = mm(w_t[cols, :], dqkv[...])

    wide = tok_t[...].astype(F32)
    inverse = lax.rsqrt(jnp.sum(wide * wide, axis=0, keepdims=True) * (1.0 / D) + EPS)
    unit = wide * inverse
    row_stat = jnp.sum(ng[...] * unit, axis=0, keepdims=True) * (1.0 / D)
    n_send[...] = (inverse * (ng[...] - unit * row_stat)).astype(BF)
    scatter(n_send, n_in, NORM_RS)

    for k in range(3):
        grad_w(k, dqkv.at[HEAD * k : HEAD * k + HEAD], norm_t)
    for k in range(3):
        grad_sum(k)
        if k == 1:
            b_first(g_acc, g_row(1), gbz_in, G_STEP + 4)
        else:
            a_first(g_acc, g_col(k), gx_in.at[k], G_STEP + 4 * k)
    held = {}
    held[3] = a_second(g_acc, g_piece(3), gx_in.at[3], ga_part, gz_send.at[3], gz_in.at[3], G_STEP + 12)
    land(ay_in.at[1:4], OUT_Y)
    rows = pl.ds(al(HEAD * y, 64), HEAD)

    def over_y(z):
        return a_send[z, rows, :].astype(F32) + sum(ay_in[r, z].astype(F32) for r in range(1, 4))

    az_send[...] = over_y(1 - zh).astype(BF)
    push(az_send, az_in, OUT_Z, (s, (m + 8) % 16))
    az_own[...] = over_y(zh)
    first, second = reduced(n_in, NORM_RS)
    tok_grad = cot_own[...].astype(F32) + jnp.concatenate([first, second], axis=1)
    pad = jnp.zeros((SHARE, WIDE - PAIRS), F32)
    for half in range(2):
        pg = jnp.concatenate([0.5 * tok_grad * slope[half], pad], axis=1)
        for d in range(3):
            shift = (WIDE - 1, 0, 1)[d]
            moved = pltpu.roll(pg, shift, 1) if shift else pg
            row = SHARE * (2 * d + half)
            pgs[row : row + SHARE, :] = moved.astype(BF)
    both = pgs[2 * SHARE : 3 * SHARE, 0:PAIRS], pgs[3 * SHARE : 4 * SHARE, 0:PAIRS]
    ones = jnp.ones((16, PAIRS), BF)
    bias = nt(ones, both[0]) + nt(ones, both[1])
    c_send[1, 224:256, :] = jnp.zeros((32, CIN), BF)
    c_send[1, 224:240, 0:SHARE] = bias.astype(BF)

    @pl.loop(0, 3)
    def _(k):
        cols = pl.ds(al(256 * k, 256), 256)
        odd_cols = pl.ds(al(CIN + 256 * k, 256), 256)
        me = mm(pgs[...], xe[:, cols])
        mo = mm(pgs[...], xe[:, odd_cols])

        def part(arr, d, half):
            row = SHARE * (2 * (d + 1) + half)
            return arr[row : row + SHARE]

        taps = (
            part(me, -1, 0) + part(mo, -1, 1),
            part(mo, -1, 0) + part(me, 0, 1),
            part(me, 0, 0) + part(mo, 0, 1),
            part(mo, 0, 0) + part(me, 1, 1),
            part(me, 1, 0) + part(mo, 1, 1),
        )
        for t in range(TAPS):
            tap = taps[t].astype(BF)
            if t < 2:
                c_send[0, SHARE * t : SHARE * t + SHARE, cols] = tap
            elif t == 2:
                c_send[0, 192:256, cols] = tap[0:64]
                c_send[1, 0:32, cols] = tap[64:96]
            else:
                c_send[1, SHARE * t - 256 : SHARE * t - 160, cols] = tap

    low, high = slice(0, 384), slice(384, CIN)
    a_first(c_send, c_col, cx_in, C_STEP)
    b_first(c_send, c_row, cbz_in, C_STEP + 4)

    a_third(held[3], g_piece(3), g_all, g_red.at[3], gz_in.at[3], G_STEP + 12)
    for k in (0, 2):
        held[k] = a_second(g_acc, g_piece(k), gx_in.at[k], ga_part, gz_send.at[k], gz_in.at[k], G_STEP + 4 * k)
    b_second(g_acc, g_row(1), gb_part, gb_held, gbz_in, gx_b, G_STEP + 4)
    a_fourth(g_col(3), g_all, g_red.at[3], G_STEP + 12)
    held_c = a_second(c_send, c_piece(low), cx_in, ca_part, cz_send, cz_in, C_STEP)
    b_second(c_send, c_row, cb_part, cb_held, cbz_in, cx_b, C_STEP + 4)
    for k in (0, 2):
        a_third(held[k], g_piece(k), g_all, g_red.at[k], gz_in.at[k], G_STEP + 4 * k)
    b_third(gb_part, g_piece(1), g_all, gb_held, gx_b, g_red.at[1], G_STEP + 4)
    a_third(held_c, c_piece(low), c_all, c_red.at[0], cz_in, C_STEP)
    b_third(cb_part, c_piece(high), c_all, cb_held, cx_b, c_red.at[1], C_STEP + 4)
    for k in (0, 2):
        a_fourth(g_col(k), g_all, g_red.at[k], G_STEP + 4 * k)
    a_fourth(c_col, c_all, c_red.at[0], C_STEP)
    b_fourth(g_row(1), g_all, gx_b, G_STEP + 4)
    b_fourth(c_row, c_all, cx_b, C_STEP + 4)

    land(az_in, OUT_Z)
    az_own[...] = az_own[...] + az_in[...].astype(F32)
    as_send[...] = az_own[pl.ds(al(SHARE * (1 - c), 32), SHARE), :].astype(BF)
    push(as_send, as_in, OUT_SIB, sib)
    own = az_own[pl.ds(al(SHARE * c, 32), SHARE), :]
    land(as_in, OUT_SIB)
    other = as_in[...].astype(F32)
    out = jnp.concatenate([jnp.where(c == 0, own, other), jnp.where(c == 0, other, own)], axis=1)
    o_layer[...] = (out + tok_own[...].astype(F32)).astype(BF)

    for k in (3, 0, 2):
        land(gx_in.at[k, 1:4], G_STEP + 4 * k + 3)
    land(gbz_in, G_STEP + 7)
    land(cx_in.at[1:4], C_STEP + 3)
    land(cbz_in, C_STEP + 7)
    for copy in sent.values():
        copy.wait_send()


def scratch():
    def v(*shape, dtype=BF):
        return pltpu.VMEM(shape, dtype)

    return [
        v(1024, CIN), v(PAIRS, 128, dtype=jnp.int32), v(TAPS, SHARE, CIN), v(D, 3 * HEAD), v(D, HEAD),
        v(6, 1024, 128, dtype=F32), v(32, D, dtype=F32), v(WIDE, D), v(2, 16, D), v(576, D), v(768, D),
        v(576, WIDE, dtype=F32), v(2, SHARE, PAIRS, dtype=F32), v(SHARE, PAIRS), v(SHARE, PAIRS),
        v(D, TOK), v(D, TOK), v(D, TOK),
        v(4, HEAD, TOK), v(4, 384, TOK), v(4, TOK, HEAD), v(4, TOK, HEAD), v(4, HEAD, TOK),
        v(4, 1024, TOK, dtype=F32), v(4, 1024, TOK, dtype=F32),
        v(4, 8, TOK, dtype=F32), v(4, 4, 8, TOK, dtype=F32),
        v(4, HEAD, TOK, dtype=F32), v(4, HEAD, TOK), v(4, HEAD, TOK), v(HEAD, TOK),
        v(4, 8, TOK, dtype=F32),
        v(4, HEAD, TOK, dtype=F32), v(4, HEAD, TOK), v(4, HEAD, TOK),
        v(4, 384, TOK, dtype=F32), v(2, 384, TOK), v(2, 384, TOK), v(384, TOK), v(384, TOK),
        v(576, TOK), v(D, TOK, dtype=F32),
        v(D, TOK), v(16, SHARE, TOK),
        v(2, 768, TOK), v(4, 2, HEAD, TOK), v(HEAD, TOK), v(HEAD, TOK), v(HEAD, TOK, dtype=F32), v(SHARE, TOK), v(SHARE, TOK),
        v(768, D, dtype=F32), v(4, SHARE, D), v(4, SHARE, D), v(4, SHARE, D),
        v(4, 4, SHARE, 384), v(4, 48, 384), v(4, 48, 384), v(48, D), v(48, D), v(4, 48, 384), v(4, 48, 384),
        v(576, WIDE), v(2, 256, CIN),
        v(4, 2, 64, 384), v(64, 384), v(64, 384), v(256, 384), v(256, 384), v(4, 64, 384), v(2, 64, 384),
        pltpu.SemaphoreType.DMA((SEMS,)), pltpu.SemaphoreType.DMA((SEMS,)), pltpu.SemaphoreType.DMA((8,)),
    ]


def widen(layer, conv, grads, o_layer, o_conv, o_bias, o_q, o_k, o_v, o_o, cin, gin, cout, gout, lsem, osem):
    loads = [pltpu.make_async_copy(grads.at[k], gin.at[k], lsem.at[k]) for k in range(4)]
    loads.append(pltpu.make_async_copy(conv, cin, lsem.at[4]))
    for load in loads:
        load.start()
    through = pltpu.make_async_copy(layer, o_layer, lsem.at[5])
    through.start()
    stores = [through]
    for k, o in enumerate((o_q, o_k, o_v, o_o)):
        loads[k].wait()
        gout[k] = gin[k].astype(F32)
        stores.append(pltpu.make_async_copy(gout.at[k], o, osem.at[k]))
        stores[-1].start()
    loads[4].wait()
    for t in range(TAPS):
        cout[t] = cin[SHARE * t : SHARE * t + SHARE, :].astype(F32)
        stores.append(pltpu.make_async_copy(cout.at[t], o_conv.at[t], osem.at[4 + t]))
        stores[-1].start()
    o_bias[...] = cin[TAPS * SHARE : TAPS * SHARE + 16, 0:SHARE].astype(F32)[0:1]
    for store in stores:
        store.wait()


def body(features, base_tokens, base_proj, conv_weight, conv_bias, w_query, w_key, w_value, w_out, cotangent):
    vmem = pl.BlockSpec(memory_space=pltpu.VMEM)
    hbm = pl.BlockSpec(memory_space=pl.ANY)
    layer = jax.ShapeDtypeStruct((SHARE, PAIRS), BF)
    narrow = pl.pallas_call(
        kernel,
        out_shape=(layer, jax.ShapeDtypeStruct((2, 256, CIN), BF), jax.ShapeDtypeStruct((4, SHARE, D), BF)),
        in_specs=[hbm, hbm, vmem, hbm, vmem, hbm, hbm, hbm, hbm, hbm],
        out_specs=(vmem,) * 3,
        scratch_shapes=scratch(),
        compiler_params=pltpu.CompilerParams(
            collective_id=0, has_side_effects=True, vmem_limit_bytes=60 * 1024 * 1024
        ),
        cost_estimate=pl.CostEstimate(flops=8_000_000_000, bytes_accessed=8_000_000, transcendentals=1_300_000),
        name="section",
    )(
        features, base_tokens.reshape(PAIRS, 128), base_proj, conv_weight, conv_bias.reshape(1, SHARE),
        w_query, w_key, w_value, w_out, cotangent.T,
    )
    square = jax.ShapeDtypeStruct((SHARE, D), F32)
    layer, conv, bias, gq, gk, gv, go = pl.pallas_call(
        widen,
        out_shape=(
            layer, jax.ShapeDtypeStruct((TAPS, SHARE, CIN), F32), jax.ShapeDtypeStruct((1, SHARE), F32),
            square, square, square, square,
        ),
        in_specs=[hbm] * 3,
        out_specs=(hbm, hbm, vmem, hbm, hbm, hbm, hbm),
        scratch_shapes=[
            pltpu.VMEM((512, CIN), BF), pltpu.VMEM((4, SHARE, D), BF),
            pltpu.VMEM((TAPS, SHARE, CIN), F32), pltpu.VMEM((4, SHARE, D), F32),
            pltpu.SemaphoreType.DMA((6,)), pltpu.SemaphoreType.DMA((9,)),
        ],
        compiler_params=pltpu.CompilerParams(vmem_limit_bytes=32 * 1024 * 1024),
        name="widen",
    )(narrow[0], narrow[1].reshape(512, CIN), narrow[2])
    return layer.T, conv, bias.reshape(SHARE), gq, gk, gv, go


def solution(mesh):
    placed = (
        P("seq", None), P("seq"), P(), P(None, "mp", None), P("mp"),
        P("mp", None), P("mp", None), P("mp", None), P("mp", None), P("seq", "mp"),
    )
    return jax.shard_map(
        body,
        mesh=mesh,
        in_specs=placed,
        out_specs=(
            P("seq", "mp"), P(None, "mp", None), P("mp"),
            P("mp", None), P("mp", None), P("mp", None), P("mp", None),
        ),
        check_vma=False,
    )
```

```python
import functools

import jax
import jax.numpy as jnp
from jax import lax
from jax.experimental import pallas as pl
from jax.experimental.pallas import tpu as pltpu
from jax.sharding import PartitionSpec as P

D = 1536
CIN = 768
TAPS = 5
BIN_WIDTH = 64
EPS = 1e-06
HEAD = 192
SHARE = 96
TOK = 256
PAIRS = 512
WIDE = 640
BF = jnp.bfloat16
F32 = jnp.float32
MESH = pl.DeviceIdType.MESH
SCALE = HEAD ** (-0.5)
ROOT2PI = 0.7978845608028654

(
    COT_AG, TOK_AG, W_SIB, HALO, Q_X, DO_X, ST_X, O_X, DQ_X, KV_Z, KV_SIB, KV_FWD, DKV_FAR, DKV_SIB, DKV_Z,
    OUT_Y, OUT_Z, OUT_SIB, NORM_RS,
) = range(19)
G_SIB = 19
G_STEP = G_SIB + 4
C_STEP = G_STEP + 16
SEMS = C_STEP + 8


def mm(a, b):
    return jnp.dot(a, b, preferred_element_type=F32)


def nt(a, b):
    return lax.dot_general(a, b, (((1,), (1,)), ((), ())), preferred_element_type=F32)


def tn(a, b):
    return lax.dot_general(a, b, (((0,), (0,)), ((), ())), preferred_element_type=F32)


def kernel(
    feat_hbm, toks_hbm, bproj, cw_hbm, cbias, wq, wk, wv, wo, cot_hbm,
    o_layer, c_all, g_all,
    feat, toks, cw, w_t, wo_t, xf, r3, xe, halo, wt, w4, z, slope, tok_own, cot_own, tok_t, cot_t, norm_t,
    q, kv, kn, vn, do, et, dp, st, st_in, o_f, o_send, o_in, ot, fac,
    dq_f, dq_send, dq_in, dk, dv, qn, don, norm_n, cot_n, dkv_send, dkv_in, z_send, z_in, dqkv, ng,
    n_send, n_in, a_send, ay_in, az_send, az_in, az_own, as_send, as_in,
    g_part, g_send, g_sib, g_acc, gx_in, gz_send, gz_in, gbz_in, gb_held, gx_b, g_red,
    pgs, c_send, cx_in, cz_send, cz_in, cbz_in, cb_held, cx_b, c_red, ssem, rsem, lsem,
):
    s = lax.axis_index("seq")
    m = lax.axis_index("mp")
    zl = s // 4
    x = s % 4
    c = m % 2
    sib = (s, m + 1 - 2 * c)
    zpart = ((1 - zl) * 4 + x, m)
    sent = {}

    def xpeer(r):
        return (zl * 4 + (x + r) % 4, m)

    def seqpeer(r):
        return ((s + r) % 8, m)

    def mppeer(r):
        return (s, (m + r) % 16)

    def push(src, dst, sem, dev):
        pltpu.make_async_remote_copy(
            src_ref=src, dst_ref=dst, send_sem=ssem.at[sem], recv_sem=rsem.at[sem],
            device_id=dev, device_id_type=MESH,
        ).start()

    def land(whole, sem):
        copy = pltpu.make_async_remote_copy(
            src_ref=whole, dst_ref=whole, send_sem=ssem.at[sem], recv_sem=rsem.at[sem],
            device_id=sib, device_id_type=MESH,
        )
        copy.wait_recv()
        sent[sem] = copy

    def al(v, n):
        return pl.multiple_of(v, n)

    barrier = pltpu.get_barrier_semaphore()
    for r in range(1, 16):
        pl.semaphore_signal(barrier, inc=1, device_id=mppeer(r), device_id_type=MESH)
    for r in range(1, 8):
        pl.semaphore_signal(barrier, inc=1, device_id=seqpeer(r), device_id_type=MESH)

    loads = [
        pltpu.make_async_copy(toks_hbm, toks, lsem.at[0]),
        pltpu.make_async_copy(feat_hbm, feat, lsem.at[1]),
        pltpu.make_async_copy(cw_hbm, cw, lsem.at[2]),
        pltpu.make_async_copy(cot_hbm, cot_own, lsem.at[3]),
    ]
    for k, w in enumerate((wq, wk, wv, wo)):
        rows = pl.ds(al(HEAD * k + SHARE * c, 32), SHARE)
        loads.append(pltpu.make_async_copy(w, w4.at[rows], lsem.at[4 + k]))
    for load in loads:
        load.start()
    mine = pl.ds(al(SHARE * m, 32), SHARE)

    def spread(own, full, base):
        for r in range(1, 16):
            cols = pl.ds(al(TOK * ((m + r) % 2), TOK), TOK)
            push(own.at[:, cols], full.at[mine], base, mppeer(r))

    def keep(own, full):
        full[mine, :] = own[:, pl.ds(al(TOK * c, TOK), TOK)]

    def gathered(full, base):
        land(full.at[0 : 15 * SHARE], base)

    pl.semaphore_wait(barrier, 22)
    spread(cot_hbm, cot_t, COT_AG)
    for k, w in enumerate((wo, wq, wk, wv)):
        rows = pl.ds(al(HEAD * ((k + 3) % 4) + SHARE * c, 32), SHARE)
        push(w, w4.at[rows], W_SIB, sib)

    bp = bproj[...]
    hi = bp.astype(BF).astype(F32)
    mid = (bp - hi).astype(BF).astype(F32)
    low = (bp - hi - mid).astype(BF).astype(F32)
    r3[...] = jnp.zeros_like(r3)
    for k, part in enumerate((hi, mid, low)):
        r3[8 * k : 8 * k + 4, 0:CIN] = part
        r3[8 * k + 4 : 8 * k + 8, CIN:D] = part
    lane = lax.broadcasted_iota(jnp.int32, (128, 32), 0)
    col = lax.broadcasted_iota(jnp.int32, (128, 32), 1)
    group = jnp.where(lane >= BIN_WIDTH, 4, 0)
    counts = jnp.zeros((PAIRS, 32), F32)
    loads[0].wait()
    for b in range(4):
        pick = jnp.where((col < 24) & (col % 8 == group + b), 1.0, 0.0).astype(BF)
        match = jnp.where(toks[...] == b, 1.0, 0.0).astype(BF)
        counts = counts + mm(match, pick)
    comp = (counts * (1.0 / BIN_WIDTH)).astype(BF)
    loads[1].wait()
    for k in range(0, 6, 2):
        for i in range(2):
            xf[i] = feat[:, 128 * (k + i) : 128 * (k + i) + 128].astype(F32)
        for half in range(2):
            lo = CIN * half + 128 * k
            extra = mm(comp, r3[:, lo : lo + 256].astype(BF))
            for i in range(2):
                own = xf[i, pl.ds(half, PAIRS, stride=2), :]
                xe[0:PAIRS, lo + 128 * i : lo + 128 * i + 128] = (own + extra[:, 128 * i : 128 * i + 128]).astype(BF)

    push(xe.at[pl.ds(PAIRS - 16, 16)], halo.at[0], HALO, seqpeer(1))
    push(xe.at[pl.ds(0, 16)], halo.at[1], HALO, seqpeer(7))
    loads[2].wait()
    zero = jnp.zeros((SHARE, CIN), BF)
    left = (cw[0], zero, cw[2], cw[1], cw[4], cw[3])
    right = (cw[1], cw[0], cw[3], cw[2], zero, cw[4])
    for g in range(6):
        wt[SHARE * g : SHARE * g + SHARE, 0:CIN] = left[g]
        wt[SHARE * g : SHARE * g + SHARE, CIN:D] = right[g]

    @pl.loop(0, 2)
    def _(i):
        rows = pl.ds(al(i * 256, 256), 256)
        z[:, rows] = nt(wt[...], xe[rows, :])

    land(halo, HALO)
    at = lax.broadcasted_iota(jnp.int32, (16, D), 0)
    after = halo[1].astype(F32)
    before = halo[0].astype(F32)
    after = jnp.where((at == 0) & (s < 7), after, 0.0)
    before = jnp.where((at == 15) & (s > 0), before, 0.0)
    xe[PAIRS:WIDE, :] = jnp.zeros((WIDE - PAIRS, D), BF)
    xe[PAIRS : PAIRS + 16, :] = after.astype(BF)
    xe[WIDE - 16 : WIDE, :] = before.astype(BF)
    z[:, PAIRS:WIDE] = nt(wt[...], xe[PAIRS:WIDE, :])

    offset = jnp.transpose(jnp.broadcast_to(cbias[...], (128, SHARE)))[:, 0:1]
    total = jnp.zeros((SHARE, PAIRS), F32)
    for half in range(2):
        r0, r1, r2 = (SHARE * (2 * d + half) for d in range(3))
        pre = pltpu.roll(z[r0 : r0 + SHARE, :], 1, 1)[:, 0:PAIRS]
        pre = pre + z[r1 : r1 + SHARE, 0:PAIRS]
        pre = pre + pltpu.roll(z[r2 : r2 + SHARE, :], WIDE - 1, 1)[:, 0:PAIRS]
        pre = pre + offset
        square = pre * pre
        bend = jnp.tanh(ROOT2PI * (pre + 0.044715 * (square * pre)))
        total = total + pre * (0.5 * (1.0 + bend))
        slope[half] = 0.5 * (1.0 + bend) + (0.5 * pre) * (1.0 - bend * bend) * (
            ROOT2PI * (1.0 + (3.0 * 0.044715) * square)
        )
    tok_own[...] = (0.5 * total).astype(BF)
    spread(tok_own, tok_t, TOK_AG)
    keep(tok_own, tok_t)
    for load in loads[3:]:
        load.wait()
    land(w4.at[0 : 4 * SHARE], W_SIB)
    keep(cot_own, cot_t)
    gathered(cot_t, COT_AG)
    do[0] = mm(w4[3 * HEAD : 4 * HEAD, :], cot_t[...]).astype(BF)
    for r in range(1, 4):
        push(do.at[0], do.at[r], DO_X, xpeer(r))

    @pl.loop(0, 4)
    def _(k):
        cols = pl.ds(al(384 * k, 128), 384)
        w_t[cols, :] = jnp.transpose(w4[0 : 3 * HEAD, cols].astype(F32)).astype(BF)
        wo_t[cols, :] = jnp.transpose(w4[3 * HEAD : 4 * HEAD, cols].astype(F32)).astype(BF)
        cot_n[:, cols] = jnp.transpose(cot_t[cols, :].astype(F32)).astype(BF)

    gathered(tok_t, TOK_AG)
    wide = tok_t[...].astype(F32)
    inverse = lax.rsqrt(jnp.sum(wide * wide, axis=0, keepdims=True) * (1.0 / D) + EPS)
    norm_t[...] = (wide * inverse).astype(BF)
    qkv = mm(w4[0 : 3 * HEAD, :], norm_t[...]).astype(BF)
    q[0] = qkv[0:HEAD]
    kv[0] = qkv[HEAD : 3 * HEAD]
    push(kv.at[0], kv.at[2], KV_Z, zpart)
    push(kv.at[0], kv.at[1], KV_SIB, sib)
    for r in range(1, 4):
        push(q.at[0], q.at[r], Q_X, xpeer(r))

    don[0] = jnp.transpose(do[0].astype(F32)).astype(BF)
    qn[0] = jnp.transpose(q[0].astype(F32)).astype(BF)

    @pl.loop(0, 4)
    def _(k):
        cols = pl.ds(al(384 * k, 128), 384)
        norm_n[:, cols] = jnp.transpose(norm_t[cols, :].astype(F32)).astype(BF)

    land(kv.at[2], KV_Z)
    push(kv.at[2], kv.at[3], KV_FWD, sib)

    def turn(i):
        kn[TOK * i : TOK * i + TOK, :] = jnp.transpose(kv[i, 0:HEAD].astype(F32)).astype(BF)
        vn[TOK * i : TOK * i + TOK, :] = jnp.transpose(kv[i, HEAD : 2 * HEAD].astype(F32)).astype(BF)

    turn(0)
    land(kv.at[1], KV_SIB)
    turn(1)
    turn(2)
    land(q.at[1:4], Q_X)
    land(do.at[1:4], DO_X)
    for j in range(1, 4):
        qn[j] = jnp.transpose(q[j].astype(F32)).astype(BF)
        don[j] = jnp.transpose(do[j].astype(F32)).astype(BF)
    land(kv.at[3], KV_FWD)
    turn(3)
    @pl.loop(0, 4)
    def _(j):
        scores = mm(kn[...], q[j]) * SCALE
        top = jnp.max(scores, axis=0, keepdims=True)
        e = jnp.exp(scores - top)
        et[j] = e
        norm = jnp.sum(e, axis=0, keepdims=True)
        grad = mm(vn[...], do[j])
        dp[j] = grad
        delta = jnp.sum(e * grad, axis=0, keepdims=True)
        short = e.astype(BF)
        out = mm(kv[0, HEAD : 2 * HEAD, :], short[0:TOK])
        for i in range(1, 4):
            out = out + mm(kv[i, HEAD : 2 * HEAD, :], short[TOK * i : TOK * i + TOK])
        o_f[j] = out
        st[j, 0:1, :] = top
        st[j, 1:2, :] = norm
        st[j, 2:3, :] = delta
        st[j, 3:8, :] = jnp.zeros((5, TOK), F32)
        for r in range(1, 4):
            push(st.at[j], st_in.at[r, (j + r) % 4], ST_X, xpeer(r))

    land(st_in.at[1:4], ST_X)

    factors = []
    deltas = []
    for j in range(4):
        every = [st[j]] + [st_in[r, j] for r in range(1, 4)]
        top = functools.reduce(jnp.maximum, [e[0:1] for e in every])
        norm = sum(e[1:2] * jnp.exp(e[0:1] - top) for e in every)
        log_total = jnp.log(norm) + top
        factors.append(jnp.exp(every[0][0:1] - log_total))
        deltas.append(sum(e[2:3] * jnp.exp(e[0:1] - log_total) for e in every))
    for j in range(4):
        fac[j, 0:1, :] = factors[j]
        fac[j, 1:2, :] = deltas[j]
    for r in range(1, 4):
        o_send[r] = (o_f[r] * factors[r]).astype(BF)
        push(o_send.at[r], o_in.at[4 - r], O_X, xpeer(4 - r))

    def backward(first, j):
        rows = slice(TOK * first, TOK * first + 2 * TOK)
        p = et[j, rows, :] * fac[j, 0:1, :]
        ds = (p * (dp[j, rows, :] - fac[j, 1:2, :]) * SCALE).astype(BF)
        part = mm(kv[first, 0:HEAD, :], ds[0:TOK]) + mm(kv[first + 1, 0:HEAD, :], ds[TOK : 2 * TOK])
        dk[rows, :] += mm(ds, qn[j])
        dv[rows, :] += mm(p.astype(BF), don[j])
        return part

    dk[...] = jnp.zeros_like(dk)
    dv[...] = jnp.zeros_like(dv)

    @pl.loop(0, 4)
    def _(j):
        dq_f[j] = backward(2, j)

    def key_rows(i):
        return slice(TOK * i, TOK * i + TOK)

    def pack(buf, i):
        buf[:, 0:HEAD] = dk[key_rows(i), :].astype(BF)
        buf[:, HEAD : 2 * HEAD] = dv[key_rows(i), :].astype(BF)

    pack(dkv_send.at[0], 3)
    push(dkv_send.at[0], dkv_in.at[0], DKV_FAR, sib)

    @pl.loop(1, 4)
    def _(j):
        dq_send[j] = (dq_f[j] + backward(0, j)).astype(BF)
        push(dq_send.at[j], dq_in.at[4 - j], DQ_X, xpeer(4 - j))

    land(dkv_in.at[0], DKV_FAR)
    z_send[:, 0:HEAD] = (dk[key_rows(2), :] + dkv_in[0, :, 0:HEAD].astype(F32)).astype(BF)
    z_send[:, HEAD : 2 * HEAD] = (dv[key_rows(2), :] + dkv_in[0, :, HEAD : 2 * HEAD].astype(F32)).astype(BF)
    push(z_send, z_in, DKV_Z, zpart)
    dq_f[0] = dq_f[0] + backward(0, 0)
    pack(dkv_send.at[1], 1)
    push(dkv_send.at[1], dkv_in.at[1], DKV_SIB, sib)

    def grad_w(k, grads, inputs):
        g_part[...] = mm(grads[...], inputs[...])
        g_send[k] = g_part[pl.ds(al(SHARE * (1 - c), 32), SHARE), :].astype(BF)
        g_acc[k] = g_part[pl.ds(al(SHARE * c, 32), SHARE), :].astype(BF)
        push(g_send.at[k], g_sib.at[k], G_SIB + k, sib)

    def grad_sum(k):
        land(g_sib.at[k], G_SIB + k)
        g_acc[k] = (g_acc[k].astype(F32) + g_sib[k].astype(F32)).astype(BF)

    def g_col(k):
        return lambda buf, at: buf.at[k, :, pl.ds(al(384 * at, 128), 384)]

    def g_row(k):
        return lambda buf, at: buf.at[k, pl.ds(al(48 * at, 16), 48), :]

    def g_piece(k):
        return lambda buf, z, at: buf.at[k, pl.ds(al(48 * z, 16), 48), pl.ds(al(384 * at, 128), 384)]

    def c_col(buf, at):
        return buf.at[:, pl.ds(al(64 * at, 64), 64), 0:384]

    def c_row(buf, at):
        return buf.at[at, :, 384:CIN]

    def c_piece(lanes):
        return lambda buf, z, at: buf.at[z, pl.ds(al(64 * at, 64), 64), lanes]

    def a_first(src, col, into, sem):
        for r in range(1, 4):
            push(col(src, (x + r) % 4), into.at[r], sem, xpeer(r))

    def a_second(src, piece, into, part, send, into_z, sem):
        land(into.at[1:4], sem)

        def total(z):
            own = piece(src, z, x)[...].astype(F32)
            return own + sum(part(into, r, z)[...].astype(F32) for r in range(1, 4))

        send[...] = total(1 - zl).astype(BF)
        push(send, into_z, sem + 1, zpart)
        return total(zl)

    def a_third(held, piece, full, red, into_z, sem):
        land(into_z, sem + 1)
        red[...] = (held + into_z[...].astype(F32)).astype(BF)
        push(red, piece(full, zl, x), sem + 2, zpart)
        piece(full, zl, x)[...] = red[...]

    def a_fourth(col, full, red, sem):
        land(red, sem + 2)
        for r in range(1, 4):
            push(col(full, x), col(full, x), sem + 3, xpeer(r))

    def b_first(src, row, into_z, sem):
        push(row(src, 1 - zl), into_z, sem, zpart)

    def b_second(src, row, part, held, into_z, into, sem):
        land(into_z, sem)
        held[...] = (row(src, zl)[...].astype(F32) + into_z[...].astype(F32)).astype(BF)
        for r in range(1, 4):
            push(part(held, (x + r) % 4), into.at[r], sem + 1, xpeer(r))

    def b_third(part, piece, full, held, into, red, sem):
        land(into.at[1:4], sem + 1)
        red[...] = (part(held, x)[...].astype(F32) + sum(into[r].astype(F32) for r in range(1, 4))).astype(BF)
        for r in range(1, 4):
            push(red, piece(full, zl, x), sem + 2, xpeer(r))
        piece(full, zl, x)[...] = red[...]

    def b_fourth(row, full, into, sem):
        land(into.at[1:4], sem + 2)
        push(row(full, zl), row(full, zl), sem + 3, zpart)

    def ga_part(buf, r, z):
        return buf.at[r, pl.ds(al(48 * z, 16), 48), :]

    def ca_part(buf, r, z):
        return buf.at[r, z]

    def gb_part(buf, at):
        return buf.at[:, pl.ds(al(384 * at, 128), 384)]

    def cb_part(buf, at):
        return buf.at[pl.ds(al(64 * at, 64), 64)]

    def scatter(send, into, base):
        for r in range(1, 16):
            rows = pl.ds(al(SHARE * ((m + r) % 16), 32), SHARE)
            push(send.at[rows], into.at[r], base, mppeer(r))
        into[0] = send[mine, :]

    def reduced(into, base):
        land(into.at[1:16], base)
        same = sum(into[r].astype(F32) for r in range(0, 16, 2))
        other = sum(into[r].astype(F32) for r in range(1, 16, 2))
        first = jnp.where(c == 0, same, other)
        second = jnp.where(c == 0, other, same)
        return first, second

    land(o_in.at[1:4], O_X)
    ot[...] = (o_f[0] * factors[0] + sum(o_in[r].astype(F32) for r in range(1, 4))).astype(BF)
    grad_w(3, ot, cot_n)

    @pl.loop(0, 4)
    def _(k):
        cols = pl.ds(al(384 * k, 128), 384)
        a_send[k // 2, pl.ds(al(384 * (k % 2), 128), 384), :] = mm(wo_t[cols, :], ot[...]).astype(BF)

    y = (m // 2) % 4
    zh = m // 8
    for r in range(1, 4):
        rows = pl.ds(al(HEAD * ((y + r) % 4), 64), HEAD)
        push(a_send.at[:, rows], ay_in.at[r], OUT_Y, (s, zh * 8 + ((y + r) % 4) * 2 + c))
    grad_sum(3)
    a_first(g_acc, g_col(3), gx_in.at[3], G_STEP + 12)

    land(dkv_in.at[1], DKV_SIB)
    land(z_in, DKV_Z)
    grad_k = dk[key_rows(0), :] + (dkv_in[1, :, 0:HEAD].astype(F32) + z_in[:, 0:HEAD].astype(F32))
    grad_v = dv[key_rows(0), :] + (dkv_in[1, :, HEAD : 2 * HEAD].astype(F32) + z_in[:, HEAD : 2 * HEAD].astype(F32))
    dqkv[HEAD : 2 * HEAD, :] = jnp.transpose(grad_k).astype(BF)
    dqkv[2 * HEAD : 3 * HEAD, :] = jnp.transpose(grad_v).astype(BF)
    land(dq_in.at[1:4], DQ_X)
    grad_q = dq_f[0] + sum(dq_in[r].astype(F32) for r in range(1, 4))
    dqkv[0:HEAD, :] = grad_q.astype(BF)

    @pl.loop(0, 4)
    def _(k):
        cols = pl.ds(al(384 * k, 128), 384)
        ng[cols, :] = mm(w_t[cols, :], dqkv[...])

    wide = tok_t[...].astype(F32)
    inverse = lax.rsqrt(jnp.sum(wide * wide, axis=0, keepdims=True) * (1.0 / D) + EPS)
    unit = wide * inverse
    row_stat = jnp.sum(ng[...] * unit, axis=0, keepdims=True) * (1.0 / D)
    n_send[...] = (inverse * (ng[...] - unit * row_stat)).astype(BF)
    scatter(n_send, n_in, NORM_RS)

    for k in range(3):
        grad_w(k, dqkv.at[HEAD * k : HEAD * k + HEAD], norm_n)
    for k in range(3):
        grad_sum(k)
        if k == 1:
            b_first(g_acc, g_row(1), gbz_in, G_STEP + 4)
        else:
            a_first(g_acc, g_col(k), gx_in.at[k], G_STEP + 4 * k)
    held = {}
    held[3] = a_second(g_acc, g_piece(3), gx_in.at[3], ga_part, gz_send.at[3], gz_in.at[3], G_STEP + 12)
    first, second = reduced(n_in, NORM_RS)
    tok_grad = cot_own[...].astype(F32) + jnp.concatenate([first, second], axis=1)
    pad = jnp.zeros((SHARE, WIDE - PAIRS), F32)
    for half in range(2):
        pg = jnp.concatenate([0.5 * tok_grad * slope[half], pad], axis=1)
        for d in range(3):
            shift = (WIDE - 1, 0, 1)[d]
            moved = pltpu.roll(pg, shift, 1) if shift else pg
            row = SHARE * (2 * d + half)
            pgs[row : row + SHARE, :] = moved.astype(BF)
    both = pgs[2 * SHARE : 3 * SHARE, 0:PAIRS], pgs[3 * SHARE : 4 * SHARE, 0:PAIRS]
    ones = jnp.ones((16, PAIRS), BF)
    bias = nt(ones, both[0]) + nt(ones, both[1])
    c_send[1, 224:256, :] = jnp.zeros((32, CIN), BF)
    c_send[1, 224:240, 0:SHARE] = bias.astype(BF)

    @pl.loop(0, 3)
    def _(k):
        cols = pl.ds(al(256 * k, 256), 256)
        odd_cols = pl.ds(al(CIN + 256 * k, 256), 256)
        me = mm(pgs[...], xe[:, cols])
        mo = mm(pgs[...], xe[:, odd_cols])

        def part(arr, d, half):
            row = SHARE * (2 * (d + 1) + half)
            return arr[row : row + SHARE]

        taps = (
            part(me, -1, 0) + part(mo, -1, 1),
            part(mo, -1, 0) + part(me, 0, 1),
            part(me, 0, 0) + part(mo, 0, 1),
            part(mo, 0, 0) + part(me, 1, 1),
            part(me, 1, 0) + part(mo, 1, 1),
        )
        for t in range(TAPS):
            tap = taps[t].astype(BF)
            if t < 2:
                c_send[0, SHARE * t : SHARE * t + SHARE, cols] = tap
            elif t == 2:
                c_send[0, 192:256, cols] = tap[0:64]
                c_send[1, 0:32, cols] = tap[64:96]
            else:
                c_send[1, SHARE * t - 256 : SHARE * t - 160, cols] = tap

    low, high = slice(0, 384), slice(384, CIN)
    a_first(c_send, c_col, cx_in, C_STEP)
    b_first(c_send, c_row, cbz_in, C_STEP + 4)

    land(ay_in.at[1:4], OUT_Y)
    rows = pl.ds(al(HEAD * y, 64), HEAD)

    def over_y(z):
        return a_send[z, rows, :].astype(F32) + sum(ay_in[r, z].astype(F32) for r in range(1, 4))

    az_send[...] = over_y(1 - zh).astype(BF)
    push(az_send, az_in, OUT_Z, (s, (m + 8) % 16))
    az_own[...] = over_y(zh)
    a_third(held[3], g_piece(3), g_all, g_red.at[3], gz_in.at[3], G_STEP + 12)
    for k in (0, 2):
        held[k] = a_second(g_acc, g_piece(k), gx_in.at[k], ga_part, gz_send.at[k], gz_in.at[k], G_STEP + 4 * k)
    b_second(g_acc, g_row(1), gb_part, gb_held, gbz_in, gx_b, G_STEP + 4)
    a_fourth(g_col(3), g_all, g_red.at[3], G_STEP + 12)
    held_c = a_second(c_send, c_piece(low), cx_in, ca_part, cz_send, cz_in, C_STEP)
    b_second(c_send, c_row, cb_part, cb_held, cbz_in, cx_b, C_STEP + 4)
    for k in (0, 2):
        a_third(held[k], g_piece(k), g_all, g_red.at[k], gz_in.at[k], G_STEP + 4 * k)
    b_third(gb_part, g_piece(1), g_all, gb_held, gx_b, g_red.at[1], G_STEP + 4)
    a_third(held_c, c_piece(low), c_all, c_red.at[0], cz_in, C_STEP)
    b_third(cb_part, c_piece(high), c_all, cb_held, cx_b, c_red.at[1], C_STEP + 4)
    for k in (0, 2):
        a_fourth(g_col(k), g_all, g_red.at[k], G_STEP + 4 * k)
    a_fourth(c_col, c_all, c_red.at[0], C_STEP)
    b_fourth(g_row(1), g_all, gx_b, G_STEP + 4)
    b_fourth(c_row, c_all, cx_b, C_STEP + 4)

    land(az_in, OUT_Z)
    az_own[...] = az_own[...] + az_in[...].astype(F32)
    as_send[...] = az_own[pl.ds(al(SHARE * (1 - c), 32), SHARE), :].astype(BF)
    push(as_send, as_in, OUT_SIB, sib)
    own = az_own[pl.ds(al(SHARE * c, 32), SHARE), :]
    land(as_in, OUT_SIB)
    other = as_in[...].astype(F32)
    out = jnp.concatenate([jnp.where(c == 0, own, other), jnp.where(c == 0, other, own)], axis=1)
    o_layer[...] = (out + tok_own[...].astype(F32)).astype(BF)

    for k in (3, 0, 2):
        land(gx_in.at[k, 1:4], G_STEP + 4 * k + 3)
    land(gbz_in, G_STEP + 7)
    land(cx_in.at[1:4], C_STEP + 3)
    land(cbz_in, C_STEP + 7)
    for copy in sent.values():
        copy.wait_send()


def scratch():
    def v(*shape, dtype=BF):
        return pltpu.VMEM(shape, dtype)

    return [
        v(1024, CIN), v(PAIRS, 128, dtype=jnp.int32), v(TAPS, SHARE, CIN), v(D, 3 * HEAD), v(D, HEAD),
        v(2, 1024, 128, dtype=F32), v(32, D, dtype=F32), v(WIDE, D), v(2, 16, D), v(576, D), v(768, D),
        v(576, WIDE, dtype=F32), v(2, SHARE, PAIRS, dtype=F32), v(SHARE, PAIRS), v(SHARE, PAIRS),
        v(D, TOK), v(D, TOK), v(D, TOK),
        v(4, HEAD, TOK), v(4, 384, TOK), v(1024, HEAD), v(1024, HEAD), v(4, HEAD, TOK),
        v(4, 1024, TOK, dtype=F32), v(4, 1024, TOK, dtype=F32),
        v(4, 8, TOK, dtype=F32), v(4, 4, 8, TOK, dtype=F32),
        v(4, HEAD, TOK, dtype=F32), v(4, HEAD, TOK), v(4, HEAD, TOK), v(HEAD, TOK),
        v(4, 8, TOK, dtype=F32),
        v(4, HEAD, TOK, dtype=F32), v(4, HEAD, TOK), v(4, HEAD, TOK),
        v(1024, HEAD, dtype=F32), v(1024, HEAD, dtype=F32), v(4, TOK, HEAD), v(4, TOK, HEAD), v(TOK, D), v(TOK, D),
        v(2, TOK, 384), v(2, TOK, 384), v(TOK, 384), v(TOK, 384),
        v(576, TOK), v(D, TOK, dtype=F32),
        v(D, TOK), v(16, SHARE, TOK),
        v(2, 768, TOK), v(4, 2, HEAD, TOK), v(HEAD, TOK), v(HEAD, TOK), v(HEAD, TOK, dtype=F32), v(SHARE, TOK), v(SHARE, TOK),
        v(HEAD, D, dtype=F32), v(4, SHARE, D), v(4, SHARE, D), v(4, SHARE, D),
        v(4, 4, SHARE, 384), v(4, 48, 384), v(4, 48, 384), v(48, D), v(48, D), v(4, 48, 384), v(4, 48, 384),
        v(576, WIDE), v(2, 256, CIN),
        v(4, 2, 64, 384), v(64, 384), v(64, 384), v(256, 384), v(256, 384), v(4, 64, 384), v(2, 64, 384),
        pltpu.SemaphoreType.DMA((SEMS,)), pltpu.SemaphoreType.DMA((SEMS,)), pltpu.SemaphoreType.DMA((8,)),
    ]


def widen(layer, conv, grads, o_layer, o_conv, o_bias, o_q, o_k, o_v, o_o, cin, gin, cout, gout, lsem, osem):
    loads = [pltpu.make_async_copy(grads.at[k], gin.at[k], lsem.at[k]) for k in range(4)]
    loads.append(pltpu.make_async_copy(conv, cin, lsem.at[4]))
    for load in loads:
        load.start()
    through = pltpu.make_async_copy(layer, o_layer, lsem.at[5])
    through.start()
    stores = [through]
    for k, o in enumerate((o_q, o_k, o_v, o_o)):
        loads[k].wait()
        gout[k] = gin[k].astype(F32)
        stores.append(pltpu.make_async_copy(gout.at[k], o, osem.at[k]))
        stores[-1].start()
    loads[4].wait()
    for t in range(TAPS):
        cout[t] = cin[SHARE * t : SHARE * t + SHARE, :].astype(F32)
        stores.append(pltpu.make_async_copy(cout.at[t], o_conv.at[t], osem.at[4 + t]))
        stores[-1].start()
    o_bias[...] = cin[TAPS * SHARE : TAPS * SHARE + 16, 0:SHARE].astype(F32)[0:1]
    for store in stores:
        store.wait()


def body(features, base_tokens, base_proj, conv_weight, conv_bias, w_query, w_key, w_value, w_out, cotangent):
    vmem = pl.BlockSpec(memory_space=pltpu.VMEM)
    hbm = pl.BlockSpec(memory_space=pl.ANY)
    layer = jax.ShapeDtypeStruct((SHARE, PAIRS), BF)
    narrow = pl.pallas_call(
        kernel,
        out_shape=(layer, jax.ShapeDtypeStruct((2, 256, CIN), BF), jax.ShapeDtypeStruct((4, SHARE, D), BF)),
        in_specs=[hbm, hbm, vmem, hbm, vmem, hbm, hbm, hbm, hbm, hbm],
        out_specs=(vmem,) * 3,
        scratch_shapes=scratch(),
        compiler_params=pltpu.CompilerParams(
            collective_id=0, has_side_effects=True, vmem_limit_bytes=60 * 1024 * 1024
        ),
        cost_estimate=pl.CostEstimate(flops=8_000_000_000, bytes_accessed=8_000_000, transcendentals=1_300_000),
        name="section",
    )(
        features, base_tokens.reshape(PAIRS, 128), base_proj, conv_weight, conv_bias.reshape(1, SHARE),
        w_query, w_key, w_value, w_out, cotangent.T,
    )
    square = jax.ShapeDtypeStruct((SHARE, D), F32)
    layer, conv, bias, gq, gk, gv, go = pl.pallas_call(
        widen,
        out_shape=(
            layer, jax.ShapeDtypeStruct((TAPS, SHARE, CIN), F32), jax.ShapeDtypeStruct((1, SHARE), F32),
            square, square, square, square,
        ),
        in_specs=[hbm] * 3,
        out_specs=(hbm, hbm, vmem, hbm, hbm, hbm, hbm),
        scratch_shapes=[
            pltpu.VMEM((512, CIN), BF), pltpu.VMEM((4, SHARE, D), BF),
            pltpu.VMEM((TAPS, SHARE, CIN), F32), pltpu.VMEM((4, SHARE, D), F32),
            pltpu.SemaphoreType.DMA((6,)), pltpu.SemaphoreType.DMA((9,)),
        ],
        compiler_params=pltpu.CompilerParams(vmem_limit_bytes=60 * 1024 * 1024),
        name="widen",
    )(narrow[0], narrow[1].reshape(512, CIN), narrow[2])
    return layer.T, conv, bias.reshape(SHARE), gq, gk, gv, go


def solution(mesh):
    placed = (
        P("seq", None), P("seq"), P(), P(None, "mp", None), P("mp"),
        P("mp", None), P("mp", None), P("mp", None), P("mp", None), P("seq", "mp"),
    )
    return jax.shard_map(
        body,
        mesh=mesh,
        in_specs=placed,
        out_specs=(
            P("seq", "mp"), P(None, "mp", None), P("mp"),
            P("mp", None), P("mp", None), P("mp", None), P("mp", None),
        ),
        check_vma=False,
    )
```

```python
import functools

import jax
import jax.numpy as jnp
from jax import lax
from jax.experimental import pallas as pl
from jax.experimental.pallas import tpu as pltpu
from jax.sharding import PartitionSpec as P

D = 1536
CIN = 768
TAPS = 5
BIN_WIDTH = 64
EPS = 1e-06
HEAD = 192
SHARE = 96
TOK = 256
PAIRS = 512
WIDE = 640
BF = jnp.bfloat16
F32 = jnp.float32
MESH = pl.DeviceIdType.MESH
SCALE = HEAD ** (-0.5)
ROOT2PI = 0.7978845608028654

(
    COT_AG, TOK_AG, W_SIB, HALO, Q_X, DO_X, ST_X, O_X, DQ_X, KV_Z, KV_SIB, KV_FWD, DKV_FAR, DKV_SIB, DKV_Z,
    OUT_Y, OUT_Z, OUT_SIB, NORM_RS,
) = range(19)
G_SIB = 19
G_STEP = G_SIB + 4
C_STEP = G_STEP + 24
SEMS = C_STEP + 8


def mm(a, b):
    return jnp.dot(a, b, preferred_element_type=F32)


def nt(a, b):
    return lax.dot_general(a, b, (((1,), (1,)), ((), ())), preferred_element_type=F32)


def tn(a, b):
    return lax.dot_general(a, b, (((0,), (0,)), ((), ())), preferred_element_type=F32)


def kernel(
    feat_hbm, toks_hbm, bproj, cw_hbm, cbias, wq, wk, wv, wo, cot_hbm,
    o_layer, c_all, g_all,
    feat, toks, cw, w_t, wo_t, xf, r3, xe, halo, wt, w4, z, slope, tok_own, cot_own, tok_t, cot_t, norm_t,
    q, kv, kn, vn, do, et, dp, st, st_in, o_f, o_send, o_in, ot, fac,
    dq_f, dq_send, dq_in, dk, dv, qn, don, norm_n, cot_n, dkv_send, dkv_in, z_send, z_in, dqkv, ng,
    n_send, n_in, a_send, ay_in, az_send, az_in, az_own, as_send, as_in,
    g_part, g_send, g_sib, g_acc, gr_in, gr_send, gz_send, gz_in, g_red,
    pgs, c_send, cx_in, cz_send, cz_in, cbz_in, cb_held, cx_b, c_red, ssem, rsem, lsem,
):
    s = lax.axis_index("seq")
    m = lax.axis_index("mp")
    zl = s // 4
    x = s % 4
    c = m % 2
    sib = (s, m + 1 - 2 * c)
    zpart = ((1 - zl) * 4 + x, m)
    sent = {}

    def xpeer(r):
        return (zl * 4 + (x + r) % 4, m)

    def seqpeer(r):
        return ((s + r) % 8, m)

    def mppeer(r):
        return (s, (m + r) % 16)

    def push(src, dst, sem, dev):
        pltpu.make_async_remote_copy(
            src_ref=src, dst_ref=dst, send_sem=ssem.at[sem], recv_sem=rsem.at[sem],
            device_id=dev, device_id_type=MESH,
        ).start()

    def land(whole, sem):
        copy = pltpu.make_async_remote_copy(
            src_ref=whole, dst_ref=whole, send_sem=ssem.at[sem], recv_sem=rsem.at[sem],
            device_id=sib, device_id_type=MESH,
        )
        copy.wait_recv()
        sent[sem] = copy

    def al(v, n):
        return pl.multiple_of(v, n)

    barrier = pltpu.get_barrier_semaphore()
    for r in range(1, 16):
        pl.semaphore_signal(barrier, inc=1, device_id=mppeer(r), device_id_type=MESH)
    for r in range(1, 8):
        pl.semaphore_signal(barrier, inc=1, device_id=seqpeer(r), device_id_type=MESH)

    loads = [
        pltpu.make_async_copy(toks_hbm, toks, lsem.at[0]),
        pltpu.make_async_copy(feat_hbm, feat, lsem.at[1]),
        pltpu.make_async_copy(cw_hbm, cw, lsem.at[2]),
        pltpu.make_async_copy(cot_hbm, cot_own, lsem.at[3]),
    ]
    for k, w in enumerate((wq, wk, wv, wo)):
        rows = pl.ds(al(HEAD * k + SHARE * c, 32), SHARE)
        loads.append(pltpu.make_async_copy(w, w4.at[rows], lsem.at[4 + k]))
    for load in loads:
        load.start()
    mine = pl.ds(al(SHARE * m, 32), SHARE)

    def spread(own, full, base):
        for r in range(1, 16):
            cols = pl.ds(al(TOK * ((m + r) % 2), TOK), TOK)
            push(own.at[:, cols], full.at[mine], base, mppeer(r))

    def keep(own, full):
        full[mine, :] = own[:, pl.ds(al(TOK * c, TOK), TOK)]

    def gathered(full, base):
        land(full.at[0 : 15 * SHARE], base)

    pl.semaphore_wait(barrier, 22)
    spread(cot_hbm, cot_t, COT_AG)
    for k, w in enumerate((wo, wq, wk, wv)):
        rows = pl.ds(al(HEAD * ((k + 3) % 4) + SHARE * c, 32), SHARE)
        push(w, w4.at[rows], W_SIB, sib)

    bp = bproj[...]
    hi = bp.astype(BF).astype(F32)
    mid = (bp - hi).astype(BF).astype(F32)
    low = (bp - hi - mid).astype(BF).astype(F32)
    r3[...] = jnp.zeros_like(r3)
    for k, part in enumerate((hi, mid, low)):
        r3[8 * k : 8 * k + 4, 0:CIN] = part
        r3[8 * k + 4 : 8 * k + 8, CIN:D] = part
    lane = lax.broadcasted_iota(jnp.int32, (128, 32), 0)
    col = lax.broadcasted_iota(jnp.int32, (128, 32), 1)
    group = jnp.where(lane >= BIN_WIDTH, 4, 0)
    counts = jnp.zeros((PAIRS, 32), F32)
    loads[0].wait()
    for b in range(4):
        pick = jnp.where((col < 24) & (col % 8 == group + b), 1.0, 0.0).astype(BF)
        match = jnp.where(toks[...] == b, 1.0, 0.0).astype(BF)
        counts = counts + mm(match, pick)
    comp = (counts * (1.0 / BIN_WIDTH)).astype(BF)
    loads[1].wait()
    for k in range(0, 6, 2):
        for i in range(2):
            xf[i] = feat[:, 128 * (k + i) : 128 * (k + i) + 128].astype(F32)
        for half in range(2):
            lo = CIN * half + 128 * k
            extra = mm(comp, r3[:, lo : lo + 256].astype(BF))
            for i in range(2):
                own = xf[i, pl.ds(half, PAIRS, stride=2), :]
                xe[0:PAIRS, lo + 128 * i : lo + 128 * i + 128] = (own + extra[:, 128 * i : 128 * i + 128]).astype(BF)

    push(xe.at[pl.ds(PAIRS - 16, 16)], halo.at[0], HALO, seqpeer(1))
    push(xe.at[pl.ds(0, 16)], halo.at[1], HALO, seqpeer(7))
    loads[2].wait()
    zero = jnp.zeros((SHARE, CIN), BF)
    left = (cw[0], zero, cw[2], cw[1], cw[4], cw[3])
    right = (cw[1], cw[0], cw[3], cw[2], zero, cw[4])
    for g in range(6):
        wt[SHARE * g : SHARE * g + SHARE, 0:CIN] = left[g]
        wt[SHARE * g : SHARE * g + SHARE, CIN:D] = right[g]

    @pl.loop(0, 2)
    def _(i):
        rows = pl.ds(al(i * 256, 256), 256)
        z[:, rows] = nt(wt[...], xe[rows, :])

    land(halo, HALO)
    at = lax.broadcasted_iota(jnp.int32, (16, D), 0)
    after = halo[1].astype(F32)
    before = halo[0].astype(F32)
    after = jnp.where((at == 0) & (s < 7), after, 0.0)
    before = jnp.where((at == 15) & (s > 0), before, 0.0)
    xe[PAIRS:WIDE, :] = jnp.zeros((WIDE - PAIRS, D), BF)
    xe[PAIRS : PAIRS + 16, :] = after.astype(BF)
    xe[WIDE - 16 : WIDE, :] = before.astype(BF)
    z[:, PAIRS:WIDE] = nt(wt[...], xe[PAIRS:WIDE, :])

    offset = jnp.transpose(jnp.broadcast_to(cbias[...], (128, SHARE)))[:, 0:1]
    total = jnp.zeros((SHARE, PAIRS), F32)
    for half in range(2):
        r0, r1, r2 = (SHARE * (2 * d + half) for d in range(3))
        pre = pltpu.roll(z[r0 : r0 + SHARE, :], 1, 1)[:, 0:PAIRS]
        pre = pre + z[r1 : r1 + SHARE, 0:PAIRS]
        pre = pre + pltpu.roll(z[r2 : r2 + SHARE, :], WIDE - 1, 1)[:, 0:PAIRS]
        pre = pre + offset
        square = pre * pre
        bend = jnp.tanh(ROOT2PI * (pre + 0.044715 * (square * pre)))
        total = total + pre * (0.5 * (1.0 + bend))
        slope[half] = 0.5 * (1.0 + bend) + (0.5 * pre) * (1.0 - bend * bend) * (
            ROOT2PI * (1.0 + (3.0 * 0.044715) * square)
        )
    tok_own[...] = (0.5 * total).astype(BF)
    spread(tok_own, tok_t, TOK_AG)
    keep(tok_own, tok_t)
    for load in loads[3:]:
        load.wait()
    land(w4.at[0 : 4 * SHARE], W_SIB)
    keep(cot_own, cot_t)
    gathered(cot_t, COT_AG)
    do[0] = mm(w4[3 * HEAD : 4 * HEAD, :], cot_t[...]).astype(BF)
    for r in range(1, 4):
        push(do.at[0], do.at[r], DO_X, xpeer(r))

    @pl.loop(0, 4)
    def _(k):
        cols = pl.ds(al(384 * k, 128), 384)
        w_t[cols, :] = jnp.transpose(w4[0 : 3 * HEAD, cols].astype(F32)).astype(BF)
        wo_t[cols, :] = jnp.transpose(w4[3 * HEAD : 4 * HEAD, cols].astype(F32)).astype(BF)
        cot_n[:, cols] = jnp.transpose(cot_t[cols, :].astype(F32)).astype(BF)

    gathered(tok_t, TOK_AG)
    wide = tok_t[...].astype(F32)
    inverse = lax.rsqrt(jnp.sum(wide * wide, axis=0, keepdims=True) * (1.0 / D) + EPS)
    norm_t[...] = (wide * inverse).astype(BF)
    qkv = mm(w4[0 : 3 * HEAD, :], norm_t[...]).astype(BF)
    q[0] = qkv[0:HEAD]
    kv[0] = qkv[HEAD : 3 * HEAD]
    push(kv.at[0], kv.at[2], KV_Z, zpart)
    push(kv.at[0], kv.at[1], KV_SIB, sib)
    for r in range(1, 4):
        push(q.at[0], q.at[r], Q_X, xpeer(r))

    don[0] = jnp.transpose(do[0].astype(F32)).astype(BF)
    qn[0] = jnp.transpose(q[0].astype(F32)).astype(BF)

    @pl.loop(0, 4)
    def _(k):
        cols = pl.ds(al(384 * k, 128), 384)
        norm_n[:, cols] = jnp.transpose(norm_t[cols, :].astype(F32)).astype(BF)

    land(kv.at[2], KV_Z)
    push(kv.at[2], kv.at[3], KV_FWD, sib)

    def turn(i):
        kn[TOK * i : TOK * i + TOK, :] = jnp.transpose(kv[i, 0:HEAD].astype(F32)).astype(BF)
        vn[TOK * i : TOK * i + TOK, :] = jnp.transpose(kv[i, HEAD : 2 * HEAD].astype(F32)).astype(BF)

    turn(0)
    land(kv.at[1], KV_SIB)
    turn(1)
    turn(2)
    land(q.at[1:4], Q_X)
    land(do.at[1:4], DO_X)
    for j in range(1, 4):
        qn[j] = jnp.transpose(q[j].astype(F32)).astype(BF)
        don[j] = jnp.transpose(do[j].astype(F32)).astype(BF)
    land(kv.at[3], KV_FWD)
    turn(3)
    @pl.loop(0, 4)
    def _(j):
        scores = mm(kn[...], q[j]) * SCALE
        top = jnp.max(scores, axis=0, keepdims=True)
        e = jnp.exp(scores - top)
        et[j] = e
        norm = jnp.sum(e, axis=0, keepdims=True)
        grad = mm(vn[...], do[j])
        dp[j] = grad
        delta = jnp.sum(e * grad, axis=0, keepdims=True)
        short = e.astype(BF)
        out = mm(kv[0, HEAD : 2 * HEAD, :], short[0:TOK])
        for i in range(1, 4):
            out = out + mm(kv[i, HEAD : 2 * HEAD, :], short[TOK * i : TOK * i + TOK])
        o_f[j] = out
        st[j, 0:1, :] = top
        st[j, 1:2, :] = norm
        st[j, 2:3, :] = delta
        st[j, 3:8, :] = jnp.zeros((5, TOK), F32)
        for r in range(1, 4):
            push(st.at[j], st_in.at[r, (j + r) % 4], ST_X, xpeer(r))

    land(st_in.at[1:4], ST_X)

    factors = []
    deltas = []
    for j in range(4):
        every = [st[j]] + [st_in[r, j] for r in range(1, 4)]
        top = functools.reduce(jnp.maximum, [e[0:1] for e in every])
        norm = sum(e[1:2] * jnp.exp(e[0:1] - top) for e in every)
        log_total = jnp.log(norm) + top
        factors.append(jnp.exp(every[0][0:1] - log_total))
        deltas.append(sum(e[2:3] * jnp.exp(e[0:1] - log_total) for e in every))
    for j in range(4):
        fac[j, 0:1, :] = factors[j]
        fac[j, 1:2, :] = deltas[j]
    for r in range(1, 4):
        o_send[r] = (o_f[r] * factors[r]).astype(BF)
        push(o_send.at[r], o_in.at[4 - r], O_X, xpeer(4 - r))

    def backward(first, j):
        rows = slice(TOK * first, TOK * first + 2 * TOK)
        p = et[j, rows, :] * fac[j, 0:1, :]
        ds = (p * (dp[j, rows, :] - fac[j, 1:2, :]) * SCALE).astype(BF)
        part = mm(kv[first, 0:HEAD, :], ds[0:TOK]) + mm(kv[first + 1, 0:HEAD, :], ds[TOK : 2 * TOK])
        dk[rows, :] += mm(ds, qn[j])
        dv[rows, :] += mm(p.astype(BF), don[j])
        return part

    dk[...] = jnp.zeros_like(dk)
    dv[...] = jnp.zeros_like(dv)

    @pl.loop(0, 4)
    def _(j):
        dq_f[j] = backward(2, j)

    def key_rows(i):
        return slice(TOK * i, TOK * i + TOK)

    def pack(buf, i):
        buf[:, 0:HEAD] = dk[key_rows(i), :].astype(BF)
        buf[:, HEAD : 2 * HEAD] = dv[key_rows(i), :].astype(BF)

    pack(dkv_send.at[0], 3)
    push(dkv_send.at[0], dkv_in.at[0], DKV_FAR, sib)

    def query_block(j):
        dq_send[j] = (dq_f[j] + backward(0, j)).astype(BF)
        push(dq_send.at[j], dq_in.at[4 - j], DQ_X, xpeer(4 - j))

    query_block(2)
    land(dkv_in.at[0], DKV_FAR)
    z_send[:, 0:HEAD] = (dk[key_rows(2), :] + dkv_in[0, :, 0:HEAD].astype(F32)).astype(BF)
    z_send[:, HEAD : 2 * HEAD] = (dv[key_rows(2), :] + dkv_in[0, :, HEAD : 2 * HEAD].astype(F32)).astype(BF)
    push(z_send, z_in, DKV_Z, zpart)

    @pl.loop(0, 2)
    def _(i):
        query_block(1 + 2 * i)

    dq_f[0] = dq_f[0] + backward(0, 0)
    pack(dkv_send.at[1], 1)
    push(dkv_send.at[1], dkv_in.at[1], DKV_SIB, sib)

    def grad_w(k, grads, inputs):
        g_part[...] = mm(grads[...], inputs[...])
        g_send[k] = g_part[pl.ds(al(SHARE * (1 - c), 32), SHARE), :].astype(BF)
        g_acc[k] = g_part[pl.ds(al(SHARE * c, 32), SHARE), :].astype(BF)
        push(g_send.at[k], g_sib.at[k], G_SIB + k, sib)

    def grad_sum(k):
        land(g_sib.at[k], G_SIB + k)
        g_acc[k] = (g_acc[k].astype(F32) + g_sib[k].astype(F32)).astype(BF)

    def g_piece(k):
        return lambda buf, z, at: buf.at[k, pl.ds(al(48 * z, 16), 48), pl.ds(al(384 * at, 128), 384)]

    def c_col(buf, at):
        return buf.at[:, pl.ds(al(64 * at, 64), 64), 0:384]

    def c_row(buf, at):
        return buf.at[at, :, 384:CIN]

    def c_piece(lanes):
        return lambda buf, z, at: buf.at[z, pl.ds(al(64 * at, 64), 64), lanes]

    def a_first(src, col, into, sem):
        for r in range(1, 4):
            push(col(src, (x + r) % 4), into.at[r], sem, xpeer(r))

    def a_second(src, piece, into, part, send, into_z, sem):
        land(into.at[1:4], sem)

        def total(z):
            own = piece(src, z, x)[...].astype(F32)
            return own + sum(part(into, r, z)[...].astype(F32) for r in range(1, 4))

        send[...] = total(1 - zl).astype(BF)
        push(send, into_z, sem + 1, zpart)
        return total(zl)

    def a_third(held, piece, full, red, into_z, sem):
        land(into_z, sem + 1)
        red[...] = (held + into_z[...].astype(F32)).astype(BF)
        push(red, piece(full, zl, x), sem + 2, zpart)
        piece(full, zl, x)[...] = red[...]

    right, left = xpeer(1), xpeer(3)

    def r_first(src, piece, into, sem):
        push(piece(src, 0, (x + 2) % 4), into.at[0], sem, right)
        push(piece(src, 1, (x + 2) % 4), into.at[1], sem, left)
        push(piece(src, 1, (x + 1) % 4), into.at[3], sem + 1, right)
        push(piece(src, 0, (x + 3) % 4), into.at[4], sem + 1, left)

    def r_second(src, piece, into, send, sem):
        land(into.at[0:2], sem)
        send[0] = (piece(src, 0, (x + 1) % 4)[...].astype(F32) + into[0].astype(F32)).astype(BF)
        send[1] = (piece(src, 1, (x + 3) % 4)[...].astype(F32) + into[1].astype(F32)).astype(BF)
        push(send.at[0], into.at[2], sem + 1, right)
        push(send.at[1], into.at[5], sem + 1, left)

    def r_third(src, piece, into, send, into_z, sem):
        land(into.at[2:6], sem + 1)

        def total(z):
            own = piece(src, z, x)[...].astype(F32)
            return own + into[2 + z].astype(F32) + into[4 + z].astype(F32)

        send[...] = total(1 - zl).astype(BF)
        push(send, into_z, sem + 2, zpart)
        return total(zl)

    def r_fourth(held, piece, full, red, into_z, sem):
        land(into_z, sem + 2)
        red[...] = (held + into_z[...].astype(F32)).astype(BF)
        push(red, piece(full, zl, x), sem + 3, zpart)
        for dev in (right, left):
            push(red, piece(full, zl, x), sem + 4, dev)
        piece(full, zl, x)[...] = red[...]

    def r_fifth(piece, full, red, sem):
        land(red, sem + 3)
        for dev in (right, left):
            push(piece(full, 1 - zl, x), piece(full, 1 - zl, x), sem + 4, dev)

    def r_sixth(piece, full, into, sem):
        land(into.at[0:4], sem + 4)
        push(piece(full, 0, (x + 3) % 4), piece(full, 0, (x + 3) % 4), sem + 5, right)
        push(piece(full, 1, (x + 1) % 4), piece(full, 1, (x + 1) % 4), sem + 5, left)

    def a_fourth(col, full, red, sem):
        land(red, sem + 2)
        for r in range(1, 4):
            push(col(full, x), col(full, x), sem + 3, xpeer(r))

    def b_first(src, row, into_z, sem):
        push(row(src, 1 - zl), into_z, sem, zpart)

    def b_second(src, row, part, held, into_z, into, sem):
        land(into_z, sem)
        held[...] = (row(src, zl)[...].astype(F32) + into_z[...].astype(F32)).astype(BF)
        for r in range(1, 4):
            push(part(held, (x + r) % 4), into.at[r], sem + 1, xpeer(r))

    def b_third(part, piece, full, held, into, red, sem):
        land(into.at[1:4], sem + 1)
        red[...] = (part(held, x)[...].astype(F32) + sum(into[r].astype(F32) for r in range(1, 4))).astype(BF)
        for r in range(1, 4):
            push(red, piece(full, zl, x), sem + 2, xpeer(r))
        piece(full, zl, x)[...] = red[...]

    def b_fourth(row, full, into, sem):
        land(into.at[1:4], sem + 2)
        push(row(full, zl), row(full, zl), sem + 3, zpart)

    def ca_part(buf, r, z):
        return buf.at[r, z]

    def cb_part(buf, at):
        return buf.at[pl.ds(al(64 * at, 64), 64)]

    def scatter(send, into, base):
        for r in range(1, 16):
            rows = pl.ds(al(SHARE * ((m + r) % 16), 32), SHARE)
            push(send.at[rows], into.at[r], base, mppeer(r))
        into[0] = send[mine, :]

    def reduced(into, base):
        land(into.at[1:16], base)
        same = sum(into[r].astype(F32) for r in range(0, 16, 2))
        other = sum(into[r].astype(F32) for r in range(1, 16, 2))
        first = jnp.where(c == 0, same, other)
        second = jnp.where(c == 0, other, same)
        return first, second

    land(o_in.at[1:4], O_X)
    ot[...] = (o_f[0] * factors[0] + sum(o_in[r].astype(F32) for r in range(1, 4))).astype(BF)
    grad_w(3, ot, cot_n)

    @pl.loop(0, 4)
    def _(k):
        cols = pl.ds(al(384 * k, 128), 384)
        a_send[k // 2, pl.ds(al(384 * (k % 2), 128), 384), :] = mm(wo_t[cols, :], ot[...]).astype(BF)

    y = (m // 2) % 4
    zh = m // 8
    grad_sum(3)
    r_first(g_acc, g_piece(3), gr_in.at[3], G_STEP + 18)

    land(dkv_in.at[1], DKV_SIB)
    land(z_in, DKV_Z)
    grad_k = dk[key_rows(0), :] + (dkv_in[1, :, 0:HEAD].astype(F32) + z_in[:, 0:HEAD].astype(F32))
    grad_v = dv[key_rows(0), :] + (dkv_in[1, :, HEAD : 2 * HEAD].astype(F32) + z_in[:, HEAD : 2 * HEAD].astype(F32))
    dqkv[HEAD : 2 * HEAD, :] = jnp.transpose(grad_k).astype(BF)
    dqkv[2 * HEAD : 3 * HEAD, :] = jnp.transpose(grad_v).astype(BF)
    land(dq_in.at[1:4], DQ_X)
    grad_q = dq_f[0] + sum(dq_in[r].astype(F32) for r in range(1, 4))
    dqkv[0:HEAD, :] = grad_q.astype(BF)

    @pl.loop(0, 4)
    def _(k):
        cols = pl.ds(al(384 * k, 128), 384)
        ng[cols, :] = mm(w_t[cols, :], dqkv[...])

    wide = tok_t[...].astype(F32)
    inverse = lax.rsqrt(jnp.sum(wide * wide, axis=0, keepdims=True) * (1.0 / D) + EPS)
    unit = wide * inverse
    row_stat = jnp.sum(ng[...] * unit, axis=0, keepdims=True) * (1.0 / D)
    n_send[...] = (inverse * (ng[...] - unit * row_stat)).astype(BF)
    scatter(n_send, n_in, NORM_RS)
    for r in range(1, 4):
        rows = pl.ds(al(HEAD * ((y + r) % 4), 64), HEAD)
        push(a_send.at[:, rows], ay_in.at[r], OUT_Y, (s, zh * 8 + ((y + r) % 4) * 2 + c))

    for k in range(3):
        grad_w(k, dqkv.at[HEAD * k : HEAD * k + HEAD], norm_n)
    for k in range(3):
        grad_sum(k)
        r_first(g_acc, g_piece(k), gr_in.at[k], G_STEP + 6 * k)
    r_second(g_acc, g_piece(3), gr_in.at[3], gr_send.at[3], G_STEP + 18)
    first, second = reduced(n_in, NORM_RS)
    for k in range(3):
        r_second(g_acc, g_piece(k), gr_in.at[k], gr_send.at[k], G_STEP + 6 * k)
    tok_grad = cot_own[...].astype(F32) + jnp.concatenate([first, second], axis=1)
    pad = jnp.zeros((SHARE, WIDE - PAIRS), F32)
    for half in range(2):
        pg = jnp.concatenate([0.5 * tok_grad * slope[half], pad], axis=1)
        for d in range(3):
            shift = (WIDE - 1, 0, 1)[d]
            moved = pltpu.roll(pg, shift, 1) if shift else pg
            row = SHARE * (2 * d + half)
            pgs[row : row + SHARE, :] = moved.astype(BF)
    both = pgs[2 * SHARE : 3 * SHARE, 0:PAIRS], pgs[3 * SHARE : 4 * SHARE, 0:PAIRS]
    ones = jnp.ones((16, PAIRS), BF)
    bias = nt(ones, both[0]) + nt(ones, both[1])
    c_send[1, 224:256, :] = jnp.zeros((32, CIN), BF)
    c_send[1, 224:240, 0:SHARE] = bias.astype(BF)

    @pl.loop(0, 3)
    def _(k):
        cols = pl.ds(al(256 * k, 256), 256)
        odd_cols = pl.ds(al(CIN + 256 * k, 256), 256)
        me = mm(pgs[...], xe[:, cols])
        mo = mm(pgs[...], xe[:, odd_cols])

        def part(arr, d, half):
            row = SHARE * (2 * (d + 1) + half)
            return arr[row : row + SHARE]

        taps = (
            part(me, -1, 0) + part(mo, -1, 1),
            part(mo, -1, 0) + part(me, 0, 1),
            part(me, 0, 0) + part(mo, 0, 1),
            part(mo, 0, 0) + part(me, 1, 1),
            part(me, 1, 0) + part(mo, 1, 1),
        )
        for t in range(TAPS):
            tap = taps[t].astype(BF)
            if t < 2:
                c_send[0, SHARE * t : SHARE * t + SHARE, cols] = tap
            elif t == 2:
                c_send[0, 192:256, cols] = tap[0:64]
                c_send[1, 0:32, cols] = tap[64:96]
            else:
                c_send[1, SHARE * t - 256 : SHARE * t - 160, cols] = tap

    low, high = slice(0, 384), slice(384, CIN)
    a_first(c_send, c_col, cx_in, C_STEP)
    b_first(c_send, c_row, cbz_in, C_STEP + 4)

    land(ay_in.at[1:4], OUT_Y)
    rows = pl.ds(al(HEAD * y, 64), HEAD)

    def over_y(z):
        return a_send[z, rows, :].astype(F32) + sum(ay_in[r, z].astype(F32) for r in range(1, 4))

    az_send[...] = over_y(1 - zh).astype(BF)
    push(az_send, az_in, OUT_Z, (s, (m + 8) % 16))
    az_own[...] = over_y(zh)
    held = {}
    order = (3, 0, 1, 2)
    for k in order:
        held[k] = r_third(g_acc, g_piece(k), gr_in.at[k], gz_send.at[k], gz_in.at[k], G_STEP + 6 * k)
    held_c = a_second(c_send, c_piece(low), cx_in, ca_part, cz_send, cz_in, C_STEP)
    b_second(c_send, c_row, cb_part, cb_held, cbz_in, cx_b, C_STEP + 4)
    for k in order:
        r_fourth(held[k], g_piece(k), g_all, g_red.at[k], gz_in.at[k], G_STEP + 6 * k)
    a_third(held_c, c_piece(low), c_all, c_red.at[0], cz_in, C_STEP)
    b_third(cb_part, c_piece(high), c_all, cb_held, cx_b, c_red.at[1], C_STEP + 4)
    for k in order:
        r_fifth(g_piece(k), g_all, g_red.at[k], G_STEP + 6 * k)
    a_fourth(c_col, c_all, c_red.at[0], C_STEP)
    b_fourth(c_row, c_all, cx_b, C_STEP + 4)
    for k in order:
        r_sixth(g_piece(k), g_all, gr_in.at[k], G_STEP + 6 * k)

    land(az_in, OUT_Z)
    az_own[...] = az_own[...] + az_in[...].astype(F32)
    as_send[...] = az_own[pl.ds(al(SHARE * (1 - c), 32), SHARE), :].astype(BF)
    push(as_send, as_in, OUT_SIB, sib)
    own = az_own[pl.ds(al(SHARE * c, 32), SHARE), :]
    land(as_in, OUT_SIB)
    other = as_in[...].astype(F32)
    out = jnp.concatenate([jnp.where(c == 0, own, other), jnp.where(c == 0, other, own)], axis=1)
    o_layer[...] = (out + tok_own[...].astype(F32)).astype(BF)

    for k in order:
        land(gr_in.at[k, 0:2], G_STEP + 6 * k + 5)
    land(cx_in.at[1:4], C_STEP + 3)
    land(cbz_in, C_STEP + 7)
    for copy in sent.values():
        copy.wait_send()


def scratch():
    def v(*shape, dtype=BF):
        return pltpu.VMEM(shape, dtype)

    return [
        v(1024, CIN), v(PAIRS, 128, dtype=jnp.int32), v(TAPS, SHARE, CIN), v(D, 3 * HEAD), v(D, HEAD),
        v(2, 1024, 128, dtype=F32), v(32, D, dtype=F32), v(WIDE, D), v(2, 16, D), v(576, D), v(768, D),
        v(576, WIDE, dtype=F32), v(2, SHARE, PAIRS, dtype=F32), v(SHARE, PAIRS), v(SHARE, PAIRS),
        v(D, TOK), v(D, TOK), v(D, TOK),
        v(4, HEAD, TOK), v(4, 384, TOK), v(1024, HEAD), v(1024, HEAD), v(4, HEAD, TOK),
        v(4, 1024, TOK, dtype=F32), v(4, 1024, TOK, dtype=F32),
        v(4, 8, TOK, dtype=F32), v(4, 4, 8, TOK, dtype=F32),
        v(4, HEAD, TOK, dtype=F32), v(4, HEAD, TOK), v(4, HEAD, TOK), v(HEAD, TOK),
        v(4, 8, TOK, dtype=F32),
        v(4, HEAD, TOK, dtype=F32), v(4, HEAD, TOK), v(4, HEAD, TOK),
        v(1024, HEAD, dtype=F32), v(1024, HEAD, dtype=F32), v(4, TOK, HEAD), v(4, TOK, HEAD), v(TOK, D), v(TOK, D),
        v(2, TOK, 384), v(2, TOK, 384), v(TOK, 384), v(TOK, 384),
        v(576, TOK), v(D, TOK, dtype=F32),
        v(D, TOK), v(16, SHARE, TOK),
        v(2, 768, TOK), v(4, 2, HEAD, TOK), v(HEAD, TOK), v(HEAD, TOK), v(HEAD, TOK, dtype=F32), v(SHARE, TOK), v(SHARE, TOK),
        v(HEAD, D, dtype=F32), v(4, SHARE, D), v(4, SHARE, D), v(4, SHARE, D),
        v(4, 6, 48, 384), v(4, 2, 48, 384), v(4, 48, 384), v(4, 48, 384), v(4, 48, 384),
        v(576, WIDE), v(2, 256, CIN),
        v(4, 2, 64, 384), v(64, 384), v(64, 384), v(256, 384), v(256, 384), v(4, 64, 384), v(2, 64, 384),
        pltpu.SemaphoreType.DMA((SEMS,)), pltpu.SemaphoreType.DMA((SEMS,)), pltpu.SemaphoreType.DMA((8,)),
    ]


def widen(layer, conv, grads, o_layer, o_conv, o_bias, o_q, o_k, o_v, o_o, cin, gin, cout, gout, lsem, osem):
    loads = [pltpu.make_async_copy(grads.at[k], gin.at[k], lsem.at[k]) for k in range(4)]
    loads.append(pltpu.make_async_copy(conv, cin, lsem.at[4]))
    for load in loads:
        load.start()
    through = pltpu.make_async_copy(layer, o_layer, lsem.at[5])
    through.start()
    stores = [through]
    for k, o in enumerate((o_q, o_k, o_v, o_o)):
        loads[k].wait()
        gout[k] = gin[k].astype(F32)
        stores.append(pltpu.make_async_copy(gout.at[k], o, osem.at[k]))
        stores[-1].start()
    loads[4].wait()
    for t in range(TAPS):
        cout[t] = cin[SHARE * t : SHARE * t + SHARE, :].astype(F32)
        stores.append(pltpu.make_async_copy(cout.at[t], o_conv.at[t], osem.at[4 + t]))
        stores[-1].start()
    o_bias[...] = cin[TAPS * SHARE : TAPS * SHARE + 16, 0:SHARE].astype(F32)[0:1]
    for store in stores:
        store.wait()


def body(features, base_tokens, base_proj, conv_weight, conv_bias, w_query, w_key, w_value, w_out, cotangent):
    vmem = pl.BlockSpec(memory_space=pltpu.VMEM)
    hbm = pl.BlockSpec(memory_space=pl.ANY)
    layer = jax.ShapeDtypeStruct((SHARE, PAIRS), BF)
    narrow = pl.pallas_call(
        kernel,
        out_shape=(layer, jax.ShapeDtypeStruct((2, 256, CIN), BF), jax.ShapeDtypeStruct((4, SHARE, D), BF)),
        in_specs=[hbm, hbm, vmem, hbm, vmem, hbm, hbm, hbm, hbm, hbm],
        out_specs=(vmem,) * 3,
        scratch_shapes=scratch(),
        compiler_params=pltpu.CompilerParams(
            collective_id=0, has_side_effects=True, vmem_limit_bytes=60 * 1024 * 1024
        ),
        cost_estimate=pl.CostEstimate(flops=8_000_000_000, bytes_accessed=8_000_000, transcendentals=1_300_000),
        name="section",
    )(
        features, base_tokens.reshape(PAIRS, 128), base_proj, conv_weight, conv_bias.reshape(1, SHARE),
        w_query, w_key, w_value, w_out, cotangent.T,
    )
    square = jax.ShapeDtypeStruct((SHARE, D), F32)
    layer, conv, bias, gq, gk, gv, go = pl.pallas_call(
        widen,
        out_shape=(
            layer, jax.ShapeDtypeStruct((TAPS, SHARE, CIN), F32), jax.ShapeDtypeStruct((1, SHARE), F32),
            square, square, square, square,
        ),
        in_specs=[hbm] * 3,
        out_specs=(hbm, hbm, vmem, hbm, hbm, hbm, hbm),
        scratch_shapes=[
            pltpu.VMEM((512, CIN), BF), pltpu.VMEM((4, SHARE, D), BF),
            pltpu.VMEM((TAPS, SHARE, CIN), F32), pltpu.VMEM((4, SHARE, D), F32),
            pltpu.SemaphoreType.DMA((6,)), pltpu.SemaphoreType.DMA((9,)),
        ],
        compiler_params=pltpu.CompilerParams(vmem_limit_bytes=60 * 1024 * 1024),
        name="widen",
    )(narrow[0], narrow[1].reshape(512, CIN), narrow[2])
    return layer.T, conv, bias.reshape(SHARE), gq, gk, gv, go


def solution(mesh):
    placed = (
        P("seq", None), P("seq"), P(), P(None, "mp", None), P("mp"),
        P("mp", None), P("mp", None), P("mp", None), P("mp", None), P("seq", "mp"),
    )
    return jax.shard_map(
        body,
        mesh=mesh,
        in_specs=placed,
        out_specs=(
            P("seq", "mp"), P(None, "mp", None), P("mp"),
            P("mp", None), P("mp", None), P("mp", None), P("mp", None),
        ),
        check_vma=False,
    )
```

```python
import functools

import jax
import jax.numpy as jnp
from jax import lax
from jax.experimental import pallas as pl
from jax.experimental.pallas import tpu as pltpu
from jax.sharding import PartitionSpec as P

D = 1536
CIN = 768
TAPS = 5
BIN_WIDTH = 64
EPS = 1e-06
HEAD = 192
SHARE = 96
TOK = 256
PAIRS = 512
WIDE = 640
BF = jnp.bfloat16
F32 = jnp.float32
MESH = pl.DeviceIdType.MESH
SCALE = HEAD ** (-0.5)
ROOT2PI = 0.7978845608028654

(
    COT_AG, TOK_AG, W_SIB, HALO, Q_X, DO_X, ST_X, O_X, DQ_X, K_Z, V_Z, KV_SIB, K_FWD, V_FWD, DKV_FAR, DKV_SIB, DKV_Z,
    OUT_Y, OUT_Z, OUT_SIB, NORM_RS,
) = range(21)
G_SIB = 21
G_STEP = G_SIB + 4
C_STEP = G_STEP + 24
SEMS = C_STEP + 8


def mm(a, b):
    return jnp.dot(a, b, preferred_element_type=F32)


def nt(a, b):
    return lax.dot_general(a, b, (((1,), (1,)), ((), ())), preferred_element_type=F32)


def tn(a, b):
    return lax.dot_general(a, b, (((0,), (0,)), ((), ())), preferred_element_type=F32)


def kernel(
    feat_hbm, toks_hbm, bproj, cw_hbm, cbias, wq, wk, wv, wo, cot_hbm,
    o_layer, c_all, g_all,
    feat, toks, cw, w_t, wo_t, xf, r3, xe, halo, wt, w4, z, slope, tok_own, cot_own, tok_t, cot_t, norm_t,
    q, kv, kn, vn, do, et, dp, st, st_in, o_f, o_send, o_in, ot, fac,
    dq_f, dq_send, dq_in, dk, dv, qn, don, norm_n, cot_n, wide_stat, dkv_send, dkv_in, z_send, z_in, dqkv,
    n_send, n_in, a_send, ay_in, az_send, az_in, az_own, as_send, as_in,
    g_part, g_send, g_sib, g_acc, gr_in, gr_send, gz_send, gz_in, g_red,
    pgs, c_send, cx_in, cz_send, cz_in, cbz_in, cb_held, cx_b, c_red, ssem, rsem, lsem,
):
    s = lax.axis_index("seq")
    m = lax.axis_index("mp")
    zl = s // 4
    x = s % 4
    c = m % 2
    sib = (s, m + 1 - 2 * c)
    zpart = ((1 - zl) * 4 + x, m)
    sent = {}

    def xpeer(r):
        return (zl * 4 + (x + r) % 4, m)

    def seqpeer(r):
        return ((s + r) % 8, m)

    def mppeer(r):
        return (s, (m + r) % 16)

    def push(src, dst, sem, dev):
        pltpu.make_async_remote_copy(
            src_ref=src, dst_ref=dst, send_sem=ssem.at[sem], recv_sem=rsem.at[sem],
            device_id=dev, device_id_type=MESH,
        ).start()

    def land(whole, sem):
        copy = pltpu.make_async_remote_copy(
            src_ref=whole, dst_ref=whole, send_sem=ssem.at[sem], recv_sem=rsem.at[sem],
            device_id=sib, device_id_type=MESH,
        )
        copy.wait_recv()
        sent[sem] = copy

    def al(v, n):
        return pl.multiple_of(v, n)

    barrier = pltpu.get_barrier_semaphore()
    for r in range(1, 16):
        pl.semaphore_signal(barrier, inc=1, device_id=mppeer(r), device_id_type=MESH)
    for r in range(1, 8):
        pl.semaphore_signal(barrier, inc=1, device_id=seqpeer(r), device_id_type=MESH)

    loads = [
        pltpu.make_async_copy(toks_hbm, toks, lsem.at[0]),
        pltpu.make_async_copy(feat_hbm, feat, lsem.at[1]),
        pltpu.make_async_copy(cw_hbm, cw, lsem.at[2]),
        pltpu.make_async_copy(cot_hbm, cot_own, lsem.at[3]),
    ]
    for k, w in enumerate((wq, wk, wv, wo)):
        rows = pl.ds(al(HEAD * k + SHARE * c, 32), SHARE)
        loads.append(pltpu.make_async_copy(w, w4.at[rows], lsem.at[4 + k]))
    for load in loads:
        load.start()
    mine = pl.ds(al(SHARE * m, 32), SHARE)

    def spread(own, full, base, steps=range(1, 16)):
        for r in steps:
            cols = pl.ds(al(TOK * ((m + r) % 2), TOK), TOK)
            push(own.at[:, cols], full.at[mine], base, mppeer(r))

    def keep(own, full):
        full[mine, :] = own[:, pl.ds(al(TOK * c, TOK), TOK)]

    def gathered(full, base):
        land(full.at[0 : 15 * SHARE], base)

    pl.semaphore_wait(barrier, 22)
    spread(cot_hbm, cot_t, COT_AG, range(1, 10))
    for k, w in enumerate((wo, wq, wk, wv)):
        rows = pl.ds(al(HEAD * ((k + 3) % 4) + SHARE * c, 32), SHARE)
        push(w, w4.at[rows], W_SIB, sib)

    bp = bproj[...]
    hi = bp.astype(BF).astype(F32)
    mid = (bp - hi).astype(BF).astype(F32)
    low = (bp - hi - mid).astype(BF).astype(F32)
    r3[...] = jnp.zeros_like(r3)
    for k, part in enumerate((hi, mid, low)):
        r3[8 * k : 8 * k + 4, 0:CIN] = part
        r3[8 * k + 4 : 8 * k + 8, CIN:D] = part
    lane = lax.broadcasted_iota(jnp.int32, (128, 32), 0)
    col = lax.broadcasted_iota(jnp.int32, (128, 32), 1)
    group = jnp.where(lane >= BIN_WIDTH, 4, 0)
    counts = jnp.zeros((PAIRS, 32), F32)
    loads[0].wait()
    for b in range(4):
        pick = jnp.where((col < 24) & (col % 8 == group + b), 1.0, 0.0).astype(BF)
        match = jnp.where(toks[...] == b, 1.0, 0.0).astype(BF)
        counts = counts + mm(match, pick)
    comp = (counts * (1.0 / BIN_WIDTH)).astype(BF)
    loads[1].wait()
    for k in range(0, 6, 2):
        for i in range(2):
            xf[i] = feat[:, 128 * (k + i) : 128 * (k + i) + 128].astype(F32)
        for half in range(2):
            lo = CIN * half + 128 * k
            extra = mm(comp, r3[:, lo : lo + 256].astype(BF))
            for i in range(2):
                own = xf[i, pl.ds(half, PAIRS, stride=2), :]
                xe[0:PAIRS, lo + 128 * i : lo + 128 * i + 128] = (own + extra[:, 128 * i : 128 * i + 128]).astype(BF)

    push(xe.at[pl.ds(PAIRS - 16, 16)], halo.at[0], HALO, seqpeer(1))
    push(xe.at[pl.ds(0, 16)], halo.at[1], HALO, seqpeer(7))
    loads[2].wait()
    zero = jnp.zeros((SHARE, CIN), BF)
    left = (cw[0], zero, cw[2], cw[1], cw[4], cw[3])
    right = (cw[1], cw[0], cw[3], cw[2], zero, cw[4])
    for g in range(6):
        wt[SHARE * g : SHARE * g + SHARE, 0:CIN] = left[g]
        wt[SHARE * g : SHARE * g + SHARE, CIN:D] = right[g]

    @pl.loop(0, 2)
    def _(i):
        rows = pl.ds(al(i * 256, 256), 256)
        z[:, rows] = nt(wt[...], xe[rows, :])

    land(halo, HALO)
    at = lax.broadcasted_iota(jnp.int32, (16, D), 0)
    after = halo[1].astype(F32)
    before = halo[0].astype(F32)
    after = jnp.where((at == 0) & (s < 7), after, 0.0)
    before = jnp.where((at == 15) & (s > 0), before, 0.0)
    xe[PAIRS:WIDE, :] = jnp.zeros((WIDE - PAIRS, D), BF)
    xe[PAIRS : PAIRS + 16, :] = after.astype(BF)
    xe[WIDE - 16 : WIDE, :] = before.astype(BF)
    z[:, PAIRS:WIDE] = nt(wt[...], xe[PAIRS:WIDE, :])

    offset = jnp.transpose(jnp.broadcast_to(cbias[...], (128, SHARE)))[:, 0:1]
    total = jnp.zeros((SHARE, PAIRS), F32)
    for half in range(2):
        r0, r1, r2 = (SHARE * (2 * d + half) for d in range(3))
        pre = pltpu.roll(z[r0 : r0 + SHARE, :], 1, 1)[:, 0:PAIRS]
        pre = pre + z[r1 : r1 + SHARE, 0:PAIRS]
        pre = pre + pltpu.roll(z[r2 : r2 + SHARE, :], WIDE - 1, 1)[:, 0:PAIRS]
        pre = pre + offset
        square = pre * pre
        bend = jnp.tanh(ROOT2PI * (pre + 0.044715 * (square * pre)))
        total = total + pre * (0.5 * (1.0 + bend))
        slope[half] = 0.5 * (1.0 + bend) + (0.5 * pre) * (1.0 - bend * bend) * (
            ROOT2PI * (1.0 + (3.0 * 0.044715) * square)
        )
    tok_own[...] = (0.5 * total).astype(BF)
    spread(tok_own, tok_t, TOK_AG)
    spread(cot_hbm, cot_t, COT_AG, range(10, 16))
    keep(tok_own, tok_t)
    for load in loads[3:]:
        load.wait()
    land(w4.at[0 : 4 * SHARE], W_SIB)

    @pl.loop(0, 4)
    def _(k):
        cols = pl.ds(al(384 * k, 128), 384)
        w_t[cols, :] = jnp.transpose(w4[0 : 3 * HEAD, cols].astype(F32)).astype(BF)
        wo_t[cols, :] = jnp.transpose(w4[3 * HEAD : 4 * HEAD, cols].astype(F32)).astype(BF)

    gathered(tok_t, TOK_AG)
    wide = tok_t[...].astype(F32)
    inverse = lax.rsqrt(jnp.sum(wide * wide, axis=0, keepdims=True) * (1.0 / D) + EPS)
    wide_stat[1:2, :] = inverse
    norm_t[...] = (wide * inverse).astype(BF)
    kv[0, 0:HEAD] = mm(w4[HEAD : 2 * HEAD, :], norm_t[...]).astype(BF)
    keys, values = slice(0, HEAD), slice(HEAD, 2 * HEAD)
    push(kv.at[0, keys], kv.at[2, keys], K_Z, zpart)
    push(kv.at[0, keys], kv.at[1, keys], KV_SIB, sib)
    q[0] = mm(w4[0:HEAD, :], norm_t[...]).astype(BF)
    for r in range(1, 4):
        push(q.at[0], q.at[r], Q_X, xpeer(r))
    kv[0, HEAD : 2 * HEAD] = mm(w4[2 * HEAD : 3 * HEAD, :], norm_t[...]).astype(BF)
    push(kv.at[0, values], kv.at[2, values], V_Z, zpart)
    push(kv.at[0, values], kv.at[1, values], KV_SIB, sib)
    keep(cot_own, cot_t)
    gathered(cot_t, COT_AG)
    do[0] = mm(w4[3 * HEAD : 4 * HEAD, :], cot_t[...]).astype(BF)
    for r in range(1, 4):
        push(do.at[0], do.at[r], DO_X, xpeer(r))

    def turn_k(i):
        kn[TOK * i : TOK * i + TOK, :] = jnp.transpose(kv[i, 0:HEAD].astype(F32)).astype(BF)

    def turn_v(i):
        vn[TOK * i : TOK * i + TOK, :] = jnp.transpose(kv[i, HEAD : 2 * HEAD].astype(F32)).astype(BF)

    land(kv.at[2, keys], K_Z)
    push(kv.at[2, keys], kv.at[3, keys], K_FWD, sib)
    turn_k(0)
    turn_v(0)
    don[0] = jnp.transpose(do[0].astype(F32)).astype(BF)
    qn[0] = jnp.transpose(q[0].astype(F32)).astype(BF)
    land(kv.at[1], KV_SIB)
    turn_k(1)
    turn_v(1)
    turn_k(2)
    land(kv.at[2, values], V_Z)
    push(kv.at[2, values], kv.at[3, values], V_FWD, sib)
    turn_v(2)
    land(kv.at[3, keys], K_FWD)
    turn_k(3)
    land(q.at[1:4], Q_X)
    land(kv.at[3, values], V_FWD)
    turn_v(3)
    @pl.loop(0, 4)
    def _(j):
        scores = mm(kn[...], q[j]) * SCALE
        top = jnp.max(scores, axis=0, keepdims=True)
        e = jnp.exp(scores - top)
        et[j] = e
        st[j, 0:1, :] = top
        st[j, 1:2, :] = jnp.sum(e, axis=0, keepdims=True)
        short = e.astype(BF)
        out = mm(kv[0, HEAD : 2 * HEAD, :], short[0:TOK])
        for i in range(1, 4):
            out = out + mm(kv[i, HEAD : 2 * HEAD, :], short[TOK * i : TOK * i + TOK])
        o_f[j] = out

    land(do.at[1:4], DO_X)

    @pl.loop(0, 4)
    def _(j):
        grad = mm(vn[...], do[j])
        dp[j] = grad
        st[j, 2:3, :] = jnp.sum(et[j] * grad, axis=0, keepdims=True)
        st[j, 3:8, :] = jnp.zeros((5, TOK), F32)
        for r in range(1, 4):
            push(st.at[j], st_in.at[r, (j + r) % 4], ST_X, xpeer(r))

    for j in range(1, 4):
        qn[j] = jnp.transpose(q[j].astype(F32)).astype(BF)
        don[j] = jnp.transpose(do[j].astype(F32)).astype(BF)

    @pl.loop(0, 4)
    def _(k):
        cols = pl.ds(al(384 * k, 128), 384)
        norm_n[:, cols] = jnp.transpose(norm_t[cols, :].astype(F32)).astype(BF)

    land(st_in.at[1:4], ST_X)

    factors = []
    deltas = []
    for j in range(4):
        every = [st[j]] + [st_in[r, j] for r in range(1, 4)]
        top = functools.reduce(jnp.maximum, [e[0:1] for e in every])
        norm = sum(e[1:2] * jnp.exp(e[0:1] - top) for e in every)
        log_total = jnp.log(norm) + top
        factors.append(jnp.exp(every[0][0:1] - log_total))
        deltas.append(sum(e[2:3] * jnp.exp(e[0:1] - log_total) for e in every))
    for j in range(4):
        fac[j, 0:1, :] = factors[j]
        fac[j, 1:2, :] = deltas[j]
    for r in range(1, 4):
        o_send[r] = (o_f[r] * factors[r]).astype(BF)
        push(o_send.at[r], o_in.at[4 - r], O_X, xpeer(4 - r))

    def backward(first, j):
        rows = slice(TOK * first, TOK * first + 2 * TOK)
        p = et[j, rows, :] * fac[j, 0:1, :]
        ds = (p * (dp[j, rows, :] - fac[j, 1:2, :]) * SCALE).astype(BF)
        part = mm(kv[first, 0:HEAD, :], ds[0:TOK]) + mm(kv[first + 1, 0:HEAD, :], ds[TOK : 2 * TOK])
        dk[rows, :] += mm(ds, qn[j])
        dv[rows, :] += mm(p.astype(BF), don[j])
        return part

    dk[...] = jnp.zeros_like(dk)
    dv[...] = jnp.zeros_like(dv)

    @pl.loop(0, 4)
    def _(j):
        dq_f[j] = backward(2, j)

    def key_rows(i):
        return slice(TOK * i, TOK * i + TOK)

    def pack(buf, i):
        buf[:, 0:HEAD] = dk[key_rows(i), :].astype(BF)
        buf[:, HEAD : 2 * HEAD] = dv[key_rows(i), :].astype(BF)

    pack(dkv_send.at[0], 3)
    push(dkv_send.at[0], dkv_in.at[0], DKV_FAR, sib)

    def query_block(j):
        dq_send[j] = (dq_f[j] + backward(0, j)).astype(BF)
        push(dq_send.at[j], dq_in.at[4 - j], DQ_X, xpeer(4 - j))

    query_block(2)
    land(dkv_in.at[0], DKV_FAR)
    z_send[:, 0:HEAD] = (dk[key_rows(2), :] + dkv_in[0, :, 0:HEAD].astype(F32)).astype(BF)
    z_send[:, HEAD : 2 * HEAD] = (dv[key_rows(2), :] + dkv_in[0, :, HEAD : 2 * HEAD].astype(F32)).astype(BF)
    push(z_send, z_in, DKV_Z, zpart)

    @pl.loop(0, 2)
    def _(i):
        query_block(1 + 2 * i)

    dq_f[0] = dq_f[0] + backward(0, 0)
    pack(dkv_send.at[1], 1)
    push(dkv_send.at[1], dkv_in.at[1], DKV_SIB, sib)

    def grad_w(k, grads, inputs):
        g_part[...] = mm(grads[...], inputs[...])
        g_send[k] = g_part[pl.ds(al(SHARE * (1 - c), 32), SHARE), :].astype(BF)
        g_acc[k] = g_part[pl.ds(al(SHARE * c, 32), SHARE), :].astype(BF)
        push(g_send.at[k], g_sib.at[k], G_SIB + k, sib)

    def grad_sum(k):
        land(g_sib.at[k], G_SIB + k)
        g_acc[k] = (g_acc[k].astype(F32) + g_sib[k].astype(F32)).astype(BF)

    def g_piece(k):
        return lambda buf, z, at: buf.at[k, pl.ds(al(48 * z, 16), 48), pl.ds(al(384 * at, 128), 384)]

    def c_col(buf, at):
        return buf.at[:, pl.ds(al(64 * at, 64), 64), 0:384]

    def c_row(buf, at):
        return buf.at[at, :, 384:CIN]

    def c_piece(lanes):
        return lambda buf, z, at: buf.at[z, pl.ds(al(64 * at, 64), 64), lanes]

    def a_first(src, col, into, sem):
        for r in range(1, 4):
            push(col(src, (x + r) % 4), into.at[r], sem, xpeer(r))

    def a_second(src, piece, into, part, send, into_z, sem):
        land(into.at[1:4], sem)

        def total(z):
            own = piece(src, z, x)[...].astype(F32)
            return own + sum(part(into, r, z)[...].astype(F32) for r in range(1, 4))

        send[...] = total(1 - zl).astype(BF)
        push(send, into_z, sem + 1, zpart)
        return total(zl)

    def a_third(held, piece, full, red, into_z, sem):
        land(into_z, sem + 1)
        red[...] = (held + into_z[...].astype(F32)).astype(BF)
        push(red, piece(full, zl, x), sem + 2, zpart)
        piece(full, zl, x)[...] = red[...]

    right, left = xpeer(1), xpeer(3)

    def r_first(src, piece, into, sem):
        push(piece(src, 0, (x + 2) % 4), into.at[0], sem, right)
        push(piece(src, 1, (x + 2) % 4), into.at[1], sem, left)
        push(piece(src, 1, (x + 1) % 4), into.at[3], sem + 1, right)
        push(piece(src, 0, (x + 3) % 4), into.at[4], sem + 1, left)

    def r_second(src, piece, into, send, sem):
        land(into.at[0:2], sem)
        send[0] = (piece(src, 0, (x + 1) % 4)[...].astype(F32) + into[0].astype(F32)).astype(BF)
        send[1] = (piece(src, 1, (x + 3) % 4)[...].astype(F32) + into[1].astype(F32)).astype(BF)
        push(send.at[0], into.at[2], sem + 1, right)
        push(send.at[1], into.at[5], sem + 1, left)

    def r_third(src, piece, into, send, into_z, sem):
        land(into.at[2:6], sem + 1)

        def total(z):
            own = piece(src, z, x)[...].astype(F32)
            return own + into[2 + z].astype(F32) + into[4 + z].astype(F32)

        send[...] = total(1 - zl).astype(BF)
        push(send, into_z, sem + 2, zpart)
        return total(zl)

    def r_fourth(held, piece, full, red, into_z, sem):
        land(into_z, sem + 2)
        red[...] = (held + into_z[...].astype(F32)).astype(BF)
        push(red, piece(full, zl, x), sem + 3, zpart)
        for dev in (right, left):
            push(red, piece(full, zl, x), sem + 4, dev)
        piece(full, zl, x)[...] = red[...]

    def r_fifth(piece, full, red, sem):
        land(red, sem + 3)
        for dev in (right, left):
            push(piece(full, 1 - zl, x), piece(full, 1 - zl, x), sem + 4, dev)

    def r_sixth(piece, full, into, sem):
        land(into.at[0:4], sem + 4)
        push(piece(full, 0, (x + 3) % 4), piece(full, 0, (x + 3) % 4), sem + 5, right)
        push(piece(full, 1, (x + 1) % 4), piece(full, 1, (x + 1) % 4), sem + 5, left)

    def a_fourth(col, full, red, sem):
        land(red, sem + 2)
        for r in range(1, 4):
            push(col(full, x), col(full, x), sem + 3, xpeer(r))

    def b_first(src, row, into_z, sem):
        push(row(src, 1 - zl), into_z, sem, zpart)

    def b_second(src, row, part, held, into_z, into, sem):
        land(into_z, sem)
        held[...] = (row(src, zl)[...].astype(F32) + into_z[...].astype(F32)).astype(BF)
        for r in range(1, 4):
            push(part(held, (x + r) % 4), into.at[r], sem + 1, xpeer(r))

    def b_third(part, piece, full, held, into, red, sem):
        land(into.at[1:4], sem + 1)
        red[...] = (part(held, x)[...].astype(F32) + sum(into[r].astype(F32) for r in range(1, 4))).astype(BF)
        for r in range(1, 4):
            push(red, piece(full, zl, x), sem + 2, xpeer(r))
        piece(full, zl, x)[...] = red[...]

    def b_fourth(row, full, into, sem):
        land(into.at[1:4], sem + 2)
        push(row(full, zl), row(full, zl), sem + 3, zpart)

    def ca_part(buf, r, z):
        return buf.at[r, z]

    def cb_part(buf, at):
        return buf.at[pl.ds(al(64 * at, 64), 64)]

    def reduced(into, base):
        land(into.at[1:16], base)
        same = sum(into[r].astype(F32) for r in range(0, 16, 2))
        other = sum(into[r].astype(F32) for r in range(1, 16, 2))
        first = jnp.where(c == 0, same, other)
        second = jnp.where(c == 0, other, same)
        return first, second

    land(o_in.at[1:4], O_X)
    ot[...] = (o_f[0] * factors[0] + sum(o_in[r].astype(F32) for r in range(1, 4))).astype(BF)

    @pl.loop(0, 4)
    def _(k):
        cols = pl.ds(al(384 * k, 128), 384)
        cot_n[:, cols] = jnp.transpose(cot_t[cols, :].astype(F32)).astype(BF)

    grad_w(3, ot, cot_n)

    @pl.loop(0, 4)
    def _(k):
        cols = pl.ds(al(384 * k, 128), 384)
        a_send[k // 2, pl.ds(al(384 * (k % 2), 128), 384), :] = mm(wo_t[cols, :], ot[...]).astype(BF)

    y = (m // 2) % 4
    zh = m // 8
    grad_sum(3)
    r_first(g_acc, g_piece(3), gr_in.at[3], G_STEP + 18)

    land(dkv_in.at[1], DKV_SIB)
    land(z_in, DKV_Z)
    grad_k = dk[key_rows(0), :] + (dkv_in[1, :, 0:HEAD].astype(F32) + z_in[:, 0:HEAD].astype(F32))
    grad_v = dv[key_rows(0), :] + (dkv_in[1, :, HEAD : 2 * HEAD].astype(F32) + z_in[:, HEAD : 2 * HEAD].astype(F32))
    dqkv[HEAD : 2 * HEAD, :] = jnp.transpose(grad_k).astype(BF)
    dqkv[2 * HEAD : 3 * HEAD, :] = jnp.transpose(grad_v).astype(BF)
    land(dq_in.at[1:4], DQ_X)
    grad_q = dq_f[0] + sum(dq_in[r].astype(F32) for r in range(1, 4))
    dqkv[0:HEAD, :] = grad_q.astype(BF)

    row_stat = jnp.sum(dqkv[0:HEAD, :].astype(F32) * q[0].astype(F32), axis=0, keepdims=True)
    row_stat = row_stat + jnp.sum(dqkv[HEAD:, :].astype(F32) * kv[0].astype(F32), axis=0, keepdims=True)
    wide_stat[0:1, :] = row_stat * (1.0 / D)

    def scatter_rows(k):
        cols = pl.ds(al(384 * k, 128), 384)
        inverse = wide_stat[1:2, :]
        unit = tok_t[cols, :].astype(F32) * inverse
        n_send[cols, :] = (inverse * (mm(w_t[cols, :], dqkv[...]) - unit * wide_stat[0:1, :])).astype(BF)
        for i in range(4):
            peer = 4 * k + i
            slot = (peer + 16 - m) % 16
            rows = pl.ds(al(SHARE * peer, 32), SHARE)

            @pl.when(slot > 0)
            def _():
                push(n_send.at[rows], n_in.at[slot], NORM_RS, (s, peer))

    @pl.loop(0, 4)
    def _(k):
        scatter_rows((k + m // 4) % 4)

    n_in[0] = n_send[mine, :]
    for r in range(1, 4):
        rows = pl.ds(al(HEAD * ((y + r) % 4), 64), HEAD)
        push(a_send.at[:, rows], ay_in.at[r], OUT_Y, (s, zh * 8 + ((y + r) % 4) * 2 + c))

    for k in range(3):
        grad_w(k, dqkv.at[HEAD * k : HEAD * k + HEAD], norm_n)
    for k in range(3):
        grad_sum(k)
        r_first(g_acc, g_piece(k), gr_in.at[k], G_STEP + 6 * k)
    held = {}
    order = (3, 0, 1, 2)
    for k in order:
        r_second(g_acc, g_piece(k), gr_in.at[k], gr_send.at[k], G_STEP + 6 * k)
    for k in order:
        held[k] = r_third(g_acc, g_piece(k), gr_in.at[k], gz_send.at[k], gz_in.at[k], G_STEP + 6 * k)
    first, second = reduced(n_in, NORM_RS)
    tok_grad = cot_own[...].astype(F32) + jnp.concatenate([first, second], axis=1)
    pad = jnp.zeros((SHARE, WIDE - PAIRS), F32)
    for half in range(2):
        pg = jnp.concatenate([0.5 * tok_grad * slope[half], pad], axis=1)
        for d in range(3):
            shift = (WIDE - 1, 0, 1)[d]
            moved = pltpu.roll(pg, shift, 1) if shift else pg
            row = SHARE * (2 * d + half)
            pgs[row : row + SHARE, :] = moved.astype(BF)
    both = pgs[2 * SHARE : 3 * SHARE, 0:PAIRS], pgs[3 * SHARE : 4 * SHARE, 0:PAIRS]
    ones = jnp.ones((16, PAIRS), BF)
    bias = nt(ones, both[0]) + nt(ones, both[1])
    c_send[1, 224:256, :] = jnp.zeros((32, CIN), BF)
    c_send[1, 224:240, 0:SHARE] = bias.astype(BF)

    @pl.loop(0, 3)
    def _(k):
        cols = pl.ds(al(256 * k, 256), 256)
        odd_cols = pl.ds(al(CIN + 256 * k, 256), 256)
        me = mm(pgs[...], xe[:, cols])
        mo = mm(pgs[...], xe[:, odd_cols])

        def part(arr, d, half):
            row = SHARE * (2 * (d + 1) + half)
            return arr[row : row + SHARE]

        taps = (
            part(me, -1, 0) + part(mo, -1, 1),
            part(mo, -1, 0) + part(me, 0, 1),
            part(me, 0, 0) + part(mo, 0, 1),
            part(mo, 0, 0) + part(me, 1, 1),
            part(me, 1, 0) + part(mo, 1, 1),
        )
        for t in range(TAPS):
            tap = taps[t].astype(BF)
            if t < 2:
                c_send[0, SHARE * t : SHARE * t + SHARE, cols] = tap
            elif t == 2:
                c_send[0, 192:256, cols] = tap[0:64]
                c_send[1, 0:32, cols] = tap[64:96]
            else:
                c_send[1, SHARE * t - 256 : SHARE * t - 160, cols] = tap

    low, high = slice(0, 384), slice(384, CIN)
    a_first(c_send, c_col, cx_in, C_STEP)
    b_first(c_send, c_row, cbz_in, C_STEP + 4)

    land(ay_in.at[1:4], OUT_Y)
    rows = pl.ds(al(HEAD * y, 64), HEAD)

    def over_y(z):
        return a_send[z, rows, :].astype(F32) + sum(ay_in[r, z].astype(F32) for r in range(1, 4))

    az_send[...] = over_y(1 - zh).astype(BF)
    push(az_send, az_in, OUT_Z, (s, (m + 8) % 16))
    az_own[...] = over_y(zh)
    held_c = a_second(c_send, c_piece(low), cx_in, ca_part, cz_send, cz_in, C_STEP)
    b_second(c_send, c_row, cb_part, cb_held, cbz_in, cx_b, C_STEP + 4)
    for k in order:
        r_fourth(held[k], g_piece(k), g_all, g_red.at[k], gz_in.at[k], G_STEP + 6 * k)
    a_third(held_c, c_piece(low), c_all, c_red.at[0], cz_in, C_STEP)
    b_third(cb_part, c_piece(high), c_all, cb_held, cx_b, c_red.at[1], C_STEP + 4)
    for k in order:
        r_fifth(g_piece(k), g_all, g_red.at[k], G_STEP + 6 * k)
    a_fourth(c_col, c_all, c_red.at[0], C_STEP)
    b_fourth(c_row, c_all, cx_b, C_STEP + 4)
    for k in order:
        r_sixth(g_piece(k), g_all, gr_in.at[k], G_STEP + 6 * k)

    land(az_in, OUT_Z)
    az_own[...] = az_own[...] + az_in[...].astype(F32)
    as_send[...] = az_own[pl.ds(al(SHARE * (1 - c), 32), SHARE), :].astype(BF)
    push(as_send, as_in, OUT_SIB, sib)
    own = az_own[pl.ds(al(SHARE * c, 32), SHARE), :]
    land(as_in, OUT_SIB)
    other = as_in[...].astype(F32)
    out = jnp.concatenate([jnp.where(c == 0, own, other), jnp.where(c == 0, other, own)], axis=1)
    o_layer[...] = (out + tok_own[...].astype(F32)).astype(BF)

    for k in order:
        land(gr_in.at[k, 0:2], G_STEP + 6 * k + 5)
    land(cx_in.at[1:4], C_STEP + 3)
    land(cbz_in, C_STEP + 7)
    for copy in sent.values():
        copy.wait_send()


def scratch():
    def v(*shape, dtype=BF):
        return pltpu.VMEM(shape, dtype)

    return [
        v(1024, CIN), v(PAIRS, 128, dtype=jnp.int32), v(TAPS, SHARE, CIN), v(D, 3 * HEAD), v(D, HEAD),
        v(2, 1024, 128, dtype=F32), v(32, D, dtype=F32), v(WIDE, D), v(2, 16, D), v(576, D), v(768, D),
        v(576, WIDE, dtype=F32), v(2, SHARE, PAIRS, dtype=F32), v(SHARE, PAIRS), v(SHARE, PAIRS),
        v(D, TOK), v(D, TOK), v(D, TOK),
        v(4, HEAD, TOK), v(4, 384, TOK), v(1024, HEAD), v(1024, HEAD), v(4, HEAD, TOK),
        v(4, 1024, TOK, dtype=F32), v(4, 1024, TOK, dtype=F32),
        v(4, 8, TOK, dtype=F32), v(4, 4, 8, TOK, dtype=F32),
        v(4, HEAD, TOK, dtype=F32), v(4, HEAD, TOK), v(4, HEAD, TOK), v(HEAD, TOK),
        v(4, 8, TOK, dtype=F32),
        v(4, HEAD, TOK, dtype=F32), v(4, HEAD, TOK), v(4, HEAD, TOK),
        v(1024, HEAD, dtype=F32), v(1024, HEAD, dtype=F32), v(4, TOK, HEAD), v(4, TOK, HEAD), v(TOK, D), v(TOK, D), v(8, TOK, dtype=F32),
        v(2, TOK, 384), v(2, TOK, 384), v(TOK, 384), v(TOK, 384),
        v(576, TOK),
        v(D, TOK), v(16, SHARE, TOK),
        v(2, 768, TOK), v(4, 2, HEAD, TOK), v(HEAD, TOK), v(HEAD, TOK), v(HEAD, TOK, dtype=F32), v(SHARE, TOK), v(SHARE, TOK),
        v(HEAD, D, dtype=F32), v(4, SHARE, D), v(4, SHARE, D), v(4, SHARE, D),
        v(4, 6, 48, 384), v(4, 2, 48, 384), v(4, 48, 384), v(4, 48, 384), v(4, 48, 384),
        v(576, WIDE), v(2, 256, CIN),
        v(4, 2, 64, 384), v(64, 384), v(64, 384), v(256, 384), v(256, 384), v(4, 64, 384), v(2, 64, 384),
        pltpu.SemaphoreType.DMA((SEMS,)), pltpu.SemaphoreType.DMA((SEMS,)), pltpu.SemaphoreType.DMA((8,)),
    ]


def widen(layer, conv, grads, o_layer, o_conv, o_bias, o_q, o_k, o_v, o_o, cin, gin, cout, gout, lsem, osem):
    loads = [pltpu.make_async_copy(grads.at[k], gin.at[k], lsem.at[k]) for k in range(4)]
    loads.append(pltpu.make_async_copy(conv, cin, lsem.at[4]))
    for load in loads:
        load.start()
    through = pltpu.make_async_copy(layer, o_layer, lsem.at[5])
    through.start()
    stores = [through]
    for k, o in enumerate((o_q, o_k, o_v, o_o)):
        loads[k].wait()
        gout[k] = gin[k].astype(F32)
        stores.append(pltpu.make_async_copy(gout.at[k], o, osem.at[k]))
        stores[-1].start()
    loads[4].wait()
    for t in range(TAPS):
        cout[t] = cin[SHARE * t : SHARE * t + SHARE, :].astype(F32)
        stores.append(pltpu.make_async_copy(cout.at[t], o_conv.at[t], osem.at[4 + t]))
        stores[-1].start()
    o_bias[...] = cin[TAPS * SHARE : TAPS * SHARE + 16, 0:SHARE].astype(F32)[0:1]
    for store in stores:
        store.wait()


def body(features, base_tokens, base_proj, conv_weight, conv_bias, w_query, w_key, w_value, w_out, cotangent):
    vmem = pl.BlockSpec(memory_space=pltpu.VMEM)
    hbm = pl.BlockSpec(memory_space=pl.ANY)
    layer = jax.ShapeDtypeStruct((SHARE, PAIRS), BF)
    narrow = pl.pallas_call(
        kernel,
        out_shape=(layer, jax.ShapeDtypeStruct((2, 256, CIN), BF), jax.ShapeDtypeStruct((4, SHARE, D), BF)),
        in_specs=[hbm, hbm, vmem, hbm, vmem, hbm, hbm, hbm, hbm, hbm],
        out_specs=(vmem,) * 3,
        scratch_shapes=scratch(),
        compiler_params=pltpu.CompilerParams(
            collective_id=0, has_side_effects=True, vmem_limit_bytes=60 * 1024 * 1024
        ),
        cost_estimate=pl.CostEstimate(flops=8_000_000_000, bytes_accessed=8_000_000, transcendentals=1_300_000),
        name="section",
    )(
        features, base_tokens.reshape(PAIRS, 128), base_proj, conv_weight, conv_bias.reshape(1, SHARE),
        w_query, w_key, w_value, w_out, cotangent.T,
    )
    square = jax.ShapeDtypeStruct((SHARE, D), F32)
    layer, conv, bias, gq, gk, gv, go = pl.pallas_call(
        widen,
        out_shape=(
            layer, jax.ShapeDtypeStruct((TAPS, SHARE, CIN), F32), jax.ShapeDtypeStruct((1, SHARE), F32),
            square, square, square, square,
        ),
        in_specs=[hbm] * 3,
        out_specs=(hbm, hbm, vmem, hbm, hbm, hbm, hbm),
        scratch_shapes=[
            pltpu.VMEM((512, CIN), BF), pltpu.VMEM((4, SHARE, D), BF),
            pltpu.VMEM((TAPS, SHARE, CIN), F32), pltpu.VMEM((4, SHARE, D), F32),
            pltpu.SemaphoreType.DMA((6,)), pltpu.SemaphoreType.DMA((9,)),
        ],
        compiler_params=pltpu.CompilerParams(vmem_limit_bytes=60 * 1024 * 1024),
        name="widen",
    )(narrow[0], narrow[1].reshape(512, CIN), narrow[2])
    return layer.T, conv, bias.reshape(SHARE), gq, gk, gv, go


def solution(mesh):
    placed = (
        P("seq", None), P("seq"), P(), P(None, "mp", None), P("mp"),
        P("mp", None), P("mp", None), P("mp", None), P("mp", None), P("seq", "mp"),
    )
    return jax.shard_map(
        body,
        mesh=mesh,
        in_specs=placed,
        out_specs=(
            P("seq", "mp"), P(None, "mp", None), P("mp"),
            P("mp", None), P("mp", None), P("mp", None), P("mp", None),
        ),
        check_vma=False,
    )
```

```python
import functools

import jax
import jax.numpy as jnp
from jax import lax
from jax.experimental import pallas as pl
from jax.experimental.pallas import tpu as pltpu
from jax.sharding import PartitionSpec as P

D = 1536
CIN = 768
TAPS = 5
BIN_WIDTH = 64
EPS = 1e-06
HEAD = 192
SHARE = 96
TOK = 256
PAIRS = 512
WIDE = 640
BF = jnp.bfloat16
F32 = jnp.float32
MESH = pl.DeviceIdType.MESH
SCALE = HEAD ** (-0.5)
ROOT2PI = 0.7978845608028654

(
    COT_AG, TOK_AG, W_SIB, HALO, Q_X, DO_X, ST_X, O_X, DQ_X, K_Z, V_Z, KV_SIB, K_FWD, V_FWD, DKV_FAR, DKV_SIB, DKV_Z,
    OUT_Y, OUT_Z, OUT_SIB, NORM_RS,
) = range(21)
G_SIB = 21
G_STEP = G_SIB + 4
C_STEP = G_STEP + 24
SEMS = C_STEP + 8


def mm(a, b):
    return jnp.dot(a, b, preferred_element_type=F32)


def nt(a, b):
    return lax.dot_general(a, b, (((1,), (1,)), ((), ())), preferred_element_type=F32)


def tn(a, b):
    return lax.dot_general(a, b, (((0,), (0,)), ((), ())), preferred_element_type=F32)


def kernel(
    feat_hbm, toks_hbm, bproj, cw_hbm, cbias, wq, wk, wv, wo, cot_hbm,
    o_layer, c_all, g_all,
    feat, toks, cw, w_t, wo_t, xf, r3, xe, halo, wt, w4, z, slope, tok_own, cot_own, tok_t, cot_t, norm_t,
    q, kv, kn, vn, do, et, dp, st, st_in, o_f, o_send, o_in, ot, fac,
    dq_f, dq_send, dq_in, dk, dv, qn, don, norm_n, cot_n, wide_stat, dkv_send, dkv_in, z_send, z_in, dqkv,
    n_send, n_in, a_send, ay_in, az_send, az_in, az_own, as_send, as_in,
    g_part, g_send, g_sib, g_acc, gr_in, gr_send, gz_send, gz_in, g_red,
    pgs, c_send, cx_in, cz_send, cz_in, cbz_in, cb_held, cx_b, c_red, ssem, rsem, lsem,
):
    s = lax.axis_index("seq")
    m = lax.axis_index("mp")
    zl = s // 4
    x = s % 4
    c = m % 2
    sib = (s, m + 1 - 2 * c)
    zpart = ((1 - zl) * 4 + x, m)
    sent = {}

    def xpeer(r):
        return (zl * 4 + (x + r) % 4, m)

    def seqpeer(r):
        return ((s + r) % 8, m)

    def mppeer(r):
        return (s, (m + r) % 16)

    def push(src, dst, sem, dev):
        pltpu.make_async_remote_copy(
            src_ref=src, dst_ref=dst, send_sem=ssem.at[sem], recv_sem=rsem.at[sem],
            device_id=dev, device_id_type=MESH,
        ).start()

    def land(whole, sem):
        copy = pltpu.make_async_remote_copy(
            src_ref=whole, dst_ref=whole, send_sem=ssem.at[sem], recv_sem=rsem.at[sem],
            device_id=sib, device_id_type=MESH,
        )
        copy.wait_recv()
        sent[sem] = copy

    def al(v, n):
        return pl.multiple_of(v, n)

    barrier = pltpu.get_barrier_semaphore()
    for r in range(1, 16):
        pl.semaphore_signal(barrier, inc=1, device_id=mppeer(r), device_id_type=MESH)
    for r in range(1, 8):
        pl.semaphore_signal(barrier, inc=1, device_id=seqpeer(r), device_id_type=MESH)

    loads = [
        pltpu.make_async_copy(toks_hbm, toks, lsem.at[0]),
        pltpu.make_async_copy(feat_hbm, feat, lsem.at[1]),
        pltpu.make_async_copy(cw_hbm, cw, lsem.at[2]),
        pltpu.make_async_copy(cot_hbm, cot_own, lsem.at[3]),
    ]
    for k, w in enumerate((wq, wk, wv, wo)):
        rows = pl.ds(al(HEAD * k + SHARE * c, 32), SHARE)
        loads.append(pltpu.make_async_copy(w, w4.at[rows], lsem.at[4 + k]))
    for load in loads:
        load.start()
    mine = pl.ds(al(SHARE * m, 32), SHARE)

    def spread(own, full, base, steps=range(1, 16)):
        for r in steps:
            cols = pl.ds(al(TOK * ((m + r) % 2), TOK), TOK)
            push(own.at[:, cols], full.at[mine], base, mppeer(r))

    def keep(own, full):
        full[mine, :] = own[:, pl.ds(al(TOK * c, TOK), TOK)]

    def gathered(full, base):
        land(full.at[0 : 15 * SHARE], base)

    pl.semaphore_wait(barrier, 22)
    spread(cot_hbm, cot_t, COT_AG, range(1, 10))
    for k, w in enumerate((wo, wq, wk, wv)):
        rows = pl.ds(al(HEAD * ((k + 3) % 4) + SHARE * c, 32), SHARE)
        push(w, w4.at[rows], W_SIB, sib)

    bp = bproj[...]
    hi = bp.astype(BF).astype(F32)
    mid = (bp - hi).astype(BF).astype(F32)
    low = (bp - hi - mid).astype(BF).astype(F32)
    r3[...] = jnp.zeros_like(r3)
    for k, part in enumerate((hi, mid, low)):
        r3[8 * k : 8 * k + 4, 0:CIN] = part
        r3[8 * k + 4 : 8 * k + 8, CIN:D] = part
    lane = lax.broadcasted_iota(jnp.int32, (128, 32), 0)
    col = lax.broadcasted_iota(jnp.int32, (128, 32), 1)
    group = jnp.where(lane >= BIN_WIDTH, 4, 0)
    counts = jnp.zeros((PAIRS, 32), F32)
    loads[0].wait()
    for b in range(4):
        pick = jnp.where((col < 24) & (col % 8 == group + b), 1.0, 0.0).astype(BF)
        match = jnp.where(toks[...] == b, 1.0, 0.0).astype(BF)
        counts = counts + mm(match, pick)
    comp = (counts * (1.0 / BIN_WIDTH)).astype(BF)
    loads[1].wait()
    for k in range(0, 6, 2):
        for i in range(2):
            xf[i] = feat[:, 128 * (k + i) : 128 * (k + i) + 128].astype(F32)
        for half in range(2):
            lo = CIN * half + 128 * k
            extra = mm(comp, r3[:, lo : lo + 256].astype(BF))
            for i in range(2):
                own = xf[i, pl.ds(half, PAIRS, stride=2), :]
                xe[0:PAIRS, lo + 128 * i : lo + 128 * i + 128] = (own + extra[:, 128 * i : 128 * i + 128]).astype(BF)

    push(xe.at[pl.ds(PAIRS - 16, 16)], halo.at[0], HALO, seqpeer(1))
    push(xe.at[pl.ds(0, 16)], halo.at[1], HALO, seqpeer(7))
    loads[2].wait()
    zero = jnp.zeros((SHARE, CIN), BF)
    left = (cw[0], zero, cw[2], cw[1], cw[4], cw[3])
    right = (cw[1], cw[0], cw[3], cw[2], zero, cw[4])
    for g in range(6):
        wt[SHARE * g : SHARE * g + SHARE, 0:CIN] = left[g]
        wt[SHARE * g : SHARE * g + SHARE, CIN:D] = right[g]

    @pl.loop(0, 2)
    def _(i):
        rows = pl.ds(al(i * 256, 256), 256)
        z[:, rows] = nt(wt[...], xe[rows, :])

    land(halo, HALO)
    at = lax.broadcasted_iota(jnp.int32, (16, D), 0)
    after = halo[1].astype(F32)
    before = halo[0].astype(F32)
    after = jnp.where((at == 0) & (s < 7), after, 0.0)
    before = jnp.where((at == 15) & (s > 0), before, 0.0)
    xe[PAIRS:WIDE, :] = jnp.zeros((WIDE - PAIRS, D), BF)
    xe[PAIRS : PAIRS + 16, :] = after.astype(BF)
    xe[WIDE - 16 : WIDE, :] = before.astype(BF)
    z[:, PAIRS:WIDE] = nt(wt[...], xe[PAIRS:WIDE, :])

    offset = jnp.transpose(jnp.broadcast_to(cbias[...], (128, SHARE)))[:, 0:1]
    total = jnp.zeros((SHARE, PAIRS), F32)
    for half in range(2):
        r0, r1, r2 = (SHARE * (2 * d + half) for d in range(3))
        pre = pltpu.roll(z[r0 : r0 + SHARE, :], 1, 1)[:, 0:PAIRS]
        pre = pre + z[r1 : r1 + SHARE, 0:PAIRS]
        pre = pre + pltpu.roll(z[r2 : r2 + SHARE, :], WIDE - 1, 1)[:, 0:PAIRS]
        pre = pre + offset
        square = pre * pre
        bend = jnp.tanh(ROOT2PI * (pre + 0.044715 * (square * pre)))
        total = total + pre * (0.5 * (1.0 + bend))
        slope[half] = 0.5 * (1.0 + bend) + (0.5 * pre) * (1.0 - bend * bend) * (
            ROOT2PI * (1.0 + (3.0 * 0.044715) * square)
        )
    tok_own[...] = (0.5 * total).astype(BF)
    spread(tok_own, tok_t, TOK_AG)
    spread(cot_hbm, cot_t, COT_AG, range(10, 16))
    keep(tok_own, tok_t)
    for load in loads[3:]:
        load.wait()
    land(w4.at[0 : 4 * SHARE], W_SIB)

    @pl.loop(0, 4)
    def _(k):
        cols = pl.ds(al(384 * k, 128), 384)
        w_t[cols, :] = jnp.transpose(w4[0 : 3 * HEAD, cols].astype(F32)).astype(BF)
        wo_t[cols, :] = jnp.transpose(w4[3 * HEAD : 4 * HEAD, cols].astype(F32)).astype(BF)

    gathered(tok_t, TOK_AG)
    wide = tok_t[...].astype(F32)
    inverse = lax.rsqrt(jnp.sum(wide * wide, axis=0, keepdims=True) * (1.0 / D) + EPS)
    wide_stat[1:2, :] = inverse
    norm_t[...] = (wide * inverse).astype(BF)
    kv[0, 0:HEAD] = mm(w4[HEAD : 2 * HEAD, :], norm_t[...]).astype(BF)
    keys, values = slice(0, HEAD), slice(HEAD, 2 * HEAD)
    push(kv.at[0, keys], kv.at[2, keys], K_Z, zpart)
    push(kv.at[0, keys], kv.at[1, keys], KV_SIB, sib)
    q[0] = mm(w4[0:HEAD, :], norm_t[...]).astype(BF)
    for r in range(1, 4):
        push(q.at[0], q.at[r], Q_X, xpeer(r))
    kv[0, HEAD : 2 * HEAD] = mm(w4[2 * HEAD : 3 * HEAD, :], norm_t[...]).astype(BF)
    push(kv.at[0, values], kv.at[2, values], V_Z, zpart)
    push(kv.at[0, values], kv.at[1, values], KV_SIB, sib)
    keep(cot_own, cot_t)
    gathered(cot_t, COT_AG)
    do[0] = mm(w4[3 * HEAD : 4 * HEAD, :], cot_t[...]).astype(BF)
    for r in range(1, 4):
        push(do.at[0], do.at[r], DO_X, xpeer(r))

    def turn_k(i):
        kn[TOK * i : TOK * i + TOK, :] = jnp.transpose(kv[i, 0:HEAD].astype(F32)).astype(BF)

    def turn_v(i):
        vn[TOK * i : TOK * i + TOK, :] = jnp.transpose(kv[i, HEAD : 2 * HEAD].astype(F32)).astype(BF)

    land(kv.at[2, keys], K_Z)
    push(kv.at[2, keys], kv.at[3, keys], K_FWD, sib)
    turn_k(0)
    turn_v(0)
    don[0] = jnp.transpose(do[0].astype(F32)).astype(BF)
    qn[0] = jnp.transpose(q[0].astype(F32)).astype(BF)
    land(kv.at[1], KV_SIB)
    turn_k(1)
    turn_v(1)
    turn_k(2)
    land(kv.at[2, values], V_Z)
    push(kv.at[2, values], kv.at[3, values], V_FWD, sib)
    turn_v(2)
    land(kv.at[3, keys], K_FWD)
    turn_k(3)
    land(q.at[1:4], Q_X)
    land(kv.at[3, values], V_FWD)
    turn_v(3)
    @pl.loop(0, 4)
    def _(j):
        scores = mm(kn[...], q[j]) * SCALE
        top = jnp.max(scores, axis=0, keepdims=True)
        e = jnp.exp(scores - top)
        et[j] = e
        st[j, 0:1, :] = top
        st[j, 1:2, :] = jnp.sum(e, axis=0, keepdims=True)
        short = e.astype(BF)
        out = mm(kv[0, HEAD : 2 * HEAD, :], short[0:TOK])
        for i in range(1, 4):
            out = out + mm(kv[i, HEAD : 2 * HEAD, :], short[TOK * i : TOK * i + TOK])
        o_f[j] = out

    land(do.at[1:4], DO_X)

    @pl.loop(0, 4)
    def _(j):
        grad = mm(vn[...], do[j])
        dp[j] = grad
        st[j, 2:3, :] = jnp.sum(et[j] * grad, axis=0, keepdims=True)
        st[j, 3:8, :] = jnp.zeros((5, TOK), F32)
        for r in range(1, 4):
            push(st.at[j], st_in.at[r, (j + r) % 4], ST_X, xpeer(r))

    for j in range(1, 4):
        qn[j] = jnp.transpose(q[j].astype(F32)).astype(BF)
        don[j] = jnp.transpose(do[j].astype(F32)).astype(BF)

    @pl.loop(0, 4)
    def _(k):
        cols = pl.ds(al(384 * k, 128), 384)
        norm_n[:, cols] = jnp.transpose(norm_t[cols, :].astype(F32)).astype(BF)

    land(st_in.at[1:4], ST_X)

    factors = []
    deltas = []
    for j in range(4):
        every = [st[j]] + [st_in[r, j] for r in range(1, 4)]
        top = functools.reduce(jnp.maximum, [e[0:1] for e in every])
        norm = sum(e[1:2] * jnp.exp(e[0:1] - top) for e in every)
        log_total = jnp.log(norm) + top
        factors.append(jnp.exp(every[0][0:1] - log_total))
        deltas.append(sum(e[2:3] * jnp.exp(e[0:1] - log_total) for e in every))
    for j in range(4):
        fac[j, 0:1, :] = factors[j]
        fac[j, 1:2, :] = deltas[j]
    for r in range(1, 4):
        o_send[r] = (o_f[r] * factors[r]).astype(BF)
        push(o_send.at[r], o_in.at[4 - r], O_X, xpeer(4 - r))

    def backward(first, j):
        rows = slice(TOK * first, TOK * first + 2 * TOK)
        p = et[j, rows, :] * fac[j, 0:1, :]
        ds = (p * (dp[j, rows, :] - fac[j, 1:2, :]) * SCALE).astype(BF)
        part = mm(kv[first, 0:HEAD, :], ds[0:TOK]) + mm(kv[first + 1, 0:HEAD, :], ds[TOK : 2 * TOK])
        dk[rows, :] += mm(ds, qn[j])
        dv[rows, :] += mm(p.astype(BF), don[j])
        return part

    dk[...] = jnp.zeros_like(dk)
    dv[...] = jnp.zeros_like(dv)

    @pl.loop(0, 4)
    def _(j):
        dq_f[j] = backward(2, j)

    def key_rows(i):
        return slice(TOK * i, TOK * i + TOK)

    def pack(buf, i):
        buf[:, 0:HEAD] = dk[key_rows(i), :].astype(BF)
        buf[:, HEAD : 2 * HEAD] = dv[key_rows(i), :].astype(BF)

    pack(dkv_send.at[0], 3)
    push(dkv_send.at[0], dkv_in.at[0], DKV_FAR, sib)

    def query_block(j):
        dq_send[j] = (dq_f[j] + backward(0, j)).astype(BF)
        push(dq_send.at[j], dq_in.at[4 - j], DQ_X, xpeer(4 - j))

    query_block(2)
    land(dkv_in.at[0], DKV_FAR)
    z_send[:, 0:HEAD] = (dk[key_rows(2), :] + dkv_in[0, :, 0:HEAD].astype(F32)).astype(BF)
    z_send[:, HEAD : 2 * HEAD] = (dv[key_rows(2), :] + dkv_in[0, :, HEAD : 2 * HEAD].astype(F32)).astype(BF)
    push(z_send, z_in, DKV_Z, zpart)

    @pl.loop(0, 2)
    def _(i):
        query_block(1 + 2 * i)

    dq_f[0] = dq_f[0] + backward(0, 0)
    pack(dkv_send.at[1], 1)
    push(dkv_send.at[1], dkv_in.at[1], DKV_SIB, sib)

    def grad_w(k, grads, inputs):
        g_part[...] = mm(grads[...], inputs[...])
        g_send[k] = g_part[pl.ds(al(SHARE * (1 - c), 32), SHARE), :].astype(BF)
        g_acc[k] = g_part[pl.ds(al(SHARE * c, 32), SHARE), :].astype(BF)
        push(g_send.at[k], g_sib.at[k], G_SIB + k, sib)

    def grad_sum(k):
        land(g_sib.at[k], G_SIB + k)
        g_acc[k] = (g_acc[k].astype(F32) + g_sib[k].astype(F32)).astype(BF)

    def g_piece(k):
        return lambda buf, z, at: buf.at[k, pl.ds(al(48 * z, 16), 48), pl.ds(al(384 * at, 128), 384)]

    def c_col(buf, at):
        return buf.at[:, pl.ds(al(64 * at, 64), 64), 0:384]

    def c_row(buf, at):
        return buf.at[at, :, 384:CIN]

    def c_piece(lanes):
        return lambda buf, z, at: buf.at[z, pl.ds(al(64 * at, 64), 64), lanes]

    def a_first(src, col, into, sem):
        for r in range(1, 4):
            push(col(src, (x + r) % 4), into.at[r], sem, xpeer(r))

    def a_second(src, piece, into, part, send, into_z, sem):
        land(into.at[1:4], sem)

        def total(z):
            own = piece(src, z, x)[...].astype(F32)
            return own + sum(part(into, r, z)[...].astype(F32) for r in range(1, 4))

        send[...] = total(1 - zl).astype(BF)
        push(send, into_z, sem + 1, zpart)
        return total(zl)

    def a_third(held, piece, full, red, into_z, sem):
        land(into_z, sem + 1)
        red[...] = (held + into_z[...].astype(F32)).astype(BF)
        push(red, piece(full, zl, x), sem + 2, zpart)
        piece(full, zl, x)[...] = red[...]

    right, left = xpeer(1), xpeer(3)

    def r_first(src, piece, into, sem):
        push(piece(src, 0, (x + 2) % 4), into.at[0], sem, right)
        push(piece(src, 1, (x + 2) % 4), into.at[1], sem, left)
        push(piece(src, 1, (x + 1) % 4), into.at[3], sem + 1, right)
        push(piece(src, 0, (x + 3) % 4), into.at[4], sem + 1, left)

    def r_second(src, piece, into, send, sem):
        land(into.at[0:2], sem)
        send[0] = (piece(src, 0, (x + 1) % 4)[...].astype(F32) + into[0].astype(F32)).astype(BF)
        send[1] = (piece(src, 1, (x + 3) % 4)[...].astype(F32) + into[1].astype(F32)).astype(BF)
        push(send.at[0], into.at[2], sem + 1, right)
        push(send.at[1], into.at[5], sem + 1, left)

    def r_third(src, piece, into, send, into_z, sem):
        land(into.at[2:6], sem + 1)

        def total(z):
            own = piece(src, z, x)[...].astype(F32)
            return own + into[2 + z].astype(F32) + into[4 + z].astype(F32)

        send[...] = total(1 - zl).astype(BF)
        push(send, into_z, sem + 2, zpart)
        return total(zl)

    def r_fourth(held, piece, full, red, into_z, sem):
        land(into_z, sem + 2)
        red[...] = (held + into_z[...].astype(F32)).astype(BF)
        push(red, piece(full, zl, x), sem + 3, zpart)
        for dev in (right, left):
            push(red, piece(full, zl, x), sem + 4, dev)
        piece(full, zl, x)[...] = red[...]

    def r_fifth(piece, full, red, sem):
        land(red, sem + 3)
        for dev in (right, left):
            push(piece(full, 1 - zl, x), piece(full, 1 - zl, x), sem + 4, dev)

    def r_sixth(piece, full, into, sem):
        land(into.at[0:4], sem + 4)
        push(piece(full, 0, (x + 3) % 4), piece(full, 0, (x + 3) % 4), sem + 5, right)
        push(piece(full, 1, (x + 1) % 4), piece(full, 1, (x + 1) % 4), sem + 5, left)

    def a_fourth(col, full, red, sem):
        land(red, sem + 2)
        for r in range(1, 4):
            push(col(full, x), col(full, x), sem + 3, xpeer(r))

    def b_first(src, row, into_z, sem):
        push(row(src, 1 - zl), into_z, sem, zpart)

    def b_second(src, row, part, held, into_z, into, sem):
        land(into_z, sem)
        held[...] = (row(src, zl)[...].astype(F32) + into_z[...].astype(F32)).astype(BF)
        for r in range(1, 4):
            push(part(held, (x + r) % 4), into.at[r], sem + 1, xpeer(r))

    def b_third(part, piece, full, held, into, red, sem):
        land(into.at[1:4], sem + 1)
        red[...] = (part(held, x)[...].astype(F32) + sum(into[r].astype(F32) for r in range(1, 4))).astype(BF)
        for r in range(1, 4):
            push(red, piece(full, zl, x), sem + 2, xpeer(r))
        piece(full, zl, x)[...] = red[...]

    def b_fourth(row, full, into, sem):
        land(into.at[1:4], sem + 2)
        push(row(full, zl), row(full, zl), sem + 3, zpart)

    def ca_part(buf, r, z):
        return buf.at[r, z]

    def cb_part(buf, at):
        return buf.at[pl.ds(al(64 * at, 64), 64)]

    def reduced(into, base):
        land(into.at[1:16], base)
        same = sum(into[r].astype(F32) for r in range(0, 16, 2))
        other = sum(into[r].astype(F32) for r in range(1, 16, 2))
        first = jnp.where(c == 0, same, other)
        second = jnp.where(c == 0, other, same)
        return first, second

    land(o_in.at[1:4], O_X)
    ot[...] = (o_f[0] * factors[0] + sum(o_in[r].astype(F32) for r in range(1, 4))).astype(BF)

    @pl.loop(0, 4)
    def _(k):
        cols = pl.ds(al(384 * k, 128), 384)
        cot_n[:, cols] = jnp.transpose(cot_t[cols, :].astype(F32)).astype(BF)

    grad_w(3, ot, cot_n)

    y = (m // 2) % 4
    zh = m // 8

    land(dkv_in.at[1], DKV_SIB)
    land(z_in, DKV_Z)
    grad_k = dk[key_rows(0), :] + (dkv_in[1, :, 0:HEAD].astype(F32) + z_in[:, 0:HEAD].astype(F32))
    grad_v = dv[key_rows(0), :] + (dkv_in[1, :, HEAD : 2 * HEAD].astype(F32) + z_in[:, HEAD : 2 * HEAD].astype(F32))
    dqkv[HEAD : 2 * HEAD, :] = jnp.transpose(grad_k).astype(BF)
    dqkv[2 * HEAD : 3 * HEAD, :] = jnp.transpose(grad_v).astype(BF)
    land(dq_in.at[1:4], DQ_X)
    grad_q = dq_f[0] + sum(dq_in[r].astype(F32) for r in range(1, 4))
    dqkv[0:HEAD, :] = grad_q.astype(BF)

    row_stat = jnp.sum(dqkv[0:HEAD, :].astype(F32) * q[0].astype(F32), axis=0, keepdims=True)
    row_stat = row_stat + jnp.sum(dqkv[HEAD:, :].astype(F32) * kv[0].astype(F32), axis=0, keepdims=True)
    wide_stat[0:1, :] = row_stat * (1.0 / D)

    def scatter_rows(k):
        cols = pl.ds(al(384 * k, 128), 384)
        inverse = wide_stat[1:2, :]
        unit = tok_t[cols, :].astype(F32) * inverse
        n_send[cols, :] = (inverse * (mm(w_t[cols, :], dqkv[...]) - unit * wide_stat[0:1, :])).astype(BF)
        for i in range(4):
            peer = 4 * k + i
            slot = (peer + 16 - m) % 16
            rows = pl.ds(al(SHARE * peer, 32), SHARE)

            @pl.when(slot > 0)
            def _():
                push(n_send.at[rows], n_in.at[slot], NORM_RS, (s, peer))

    @pl.loop(0, 4)
    def _(k):
        scatter_rows((k + m // 4) % 4)

    n_in[0] = n_send[mine, :]

    grad_sum(3)
    r_first(g_acc, g_piece(3), gr_in.at[3], G_STEP + 18)

    for k in range(3):
        grad_w(k, dqkv.at[HEAD * k : HEAD * k + HEAD], norm_n)
    for k in range(3):
        grad_sum(k)
        r_first(g_acc, g_piece(k), gr_in.at[k], G_STEP + 6 * k)
    @pl.loop(0, 4)
    def _(k):
        cols = pl.ds(al(384 * k, 128), 384)
        a_send[k // 2, pl.ds(al(384 * (k % 2), 128), 384), :] = mm(wo_t[cols, :], ot[...]).astype(BF)

    held = {}
    order = (3, 0, 1, 2)
    for k in order:
        r_second(g_acc, g_piece(k), gr_in.at[k], gr_send.at[k], G_STEP + 6 * k)
    first, second = reduced(n_in, NORM_RS)
    for r in range(1, 4):
        rows = pl.ds(al(HEAD * ((y + r) % 4), 64), HEAD)
        push(a_send.at[:, rows], ay_in.at[r], OUT_Y, (s, zh * 8 + ((y + r) % 4) * 2 + c))
    tok_grad = cot_own[...].astype(F32) + jnp.concatenate([first, second], axis=1)
    pad = jnp.zeros((SHARE, WIDE - PAIRS), F32)
    for half in range(2):
        pg = jnp.concatenate([0.5 * tok_grad * slope[half], pad], axis=1)
        for d in range(3):
            shift = (WIDE - 1, 0, 1)[d]
            moved = pltpu.roll(pg, shift, 1) if shift else pg
            row = SHARE * (2 * d + half)
            pgs[row : row + SHARE, :] = moved.astype(BF)
    both = pgs[2 * SHARE : 3 * SHARE, 0:PAIRS], pgs[3 * SHARE : 4 * SHARE, 0:PAIRS]
    ones = jnp.ones((16, PAIRS), BF)
    bias = nt(ones, both[0]) + nt(ones, both[1])
    c_send[1, 224:256, :] = jnp.zeros((32, CIN), BF)
    c_send[1, 224:240, 0:SHARE] = bias.astype(BF)

    @pl.loop(0, 3)
    def _(k):
        cols = pl.ds(al(256 * k, 256), 256)
        odd_cols = pl.ds(al(CIN + 256 * k, 256), 256)
        me = mm(pgs[...], xe[:, cols])
        mo = mm(pgs[...], xe[:, odd_cols])

        def part(arr, d, half):
            row = SHARE * (2 * (d + 1) + half)
            return arr[row : row + SHARE]

        taps = (
            part(me, -1, 0) + part(mo, -1, 1),
            part(mo, -1, 0) + part(me, 0, 1),
            part(me, 0, 0) + part(mo, 0, 1),
            part(mo, 0, 0) + part(me, 1, 1),
            part(me, 1, 0) + part(mo, 1, 1),
        )
        for t in range(TAPS):
            tap = taps[t].astype(BF)
            if t < 2:
                c_send[0, SHARE * t : SHARE * t + SHARE, cols] = tap
            elif t == 2:
                c_send[0, 192:256, cols] = tap[0:64]
                c_send[1, 0:32, cols] = tap[64:96]
            else:
                c_send[1, SHARE * t - 256 : SHARE * t - 160, cols] = tap

    low, high = slice(0, 384), slice(384, CIN)
    a_first(c_send, c_col, cx_in, C_STEP)
    b_first(c_send, c_row, cbz_in, C_STEP + 4)

    for k in order:
        held[k] = r_third(g_acc, g_piece(k), gr_in.at[k], gz_send.at[k], gz_in.at[k], G_STEP + 6 * k)
    held_c = a_second(c_send, c_piece(low), cx_in, ca_part, cz_send, cz_in, C_STEP)
    b_second(c_send, c_row, cb_part, cb_held, cbz_in, cx_b, C_STEP + 4)
    for k in order:
        r_fourth(held[k], g_piece(k), g_all, g_red.at[k], gz_in.at[k], G_STEP + 6 * k)
    a_third(held_c, c_piece(low), c_all, c_red.at[0], cz_in, C_STEP)
    b_third(cb_part, c_piece(high), c_all, cb_held, cx_b, c_red.at[1], C_STEP + 4)
    land(ay_in.at[1:4], OUT_Y)
    rows = pl.ds(al(HEAD * y, 64), HEAD)

    def over_y(z):
        return a_send[z, rows, :].astype(F32) + sum(ay_in[r, z].astype(F32) for r in range(1, 4))

    az_send[...] = over_y(1 - zh).astype(BF)
    push(az_send, az_in, OUT_Z, (s, (m + 8) % 16))
    az_own[...] = over_y(zh)
    for k in order:
        r_fifth(g_piece(k), g_all, g_red.at[k], G_STEP + 6 * k)
    a_fourth(c_col, c_all, c_red.at[0], C_STEP)
    b_fourth(c_row, c_all, cx_b, C_STEP + 4)
    for k in order:
        r_sixth(g_piece(k), g_all, gr_in.at[k], G_STEP + 6 * k)

    land(az_in, OUT_Z)
    az_own[...] = az_own[...] + az_in[...].astype(F32)
    as_send[...] = az_own[pl.ds(al(SHARE * (1 - c), 32), SHARE), :].astype(BF)
    push(as_send, as_in, OUT_SIB, sib)
    own = az_own[pl.ds(al(SHARE * c, 32), SHARE), :]
    land(as_in, OUT_SIB)
    other = as_in[...].astype(F32)
    out = jnp.concatenate([jnp.where(c == 0, own, other), jnp.where(c == 0, other, own)], axis=1)
    o_layer[...] = (out + tok_own[...].astype(F32)).astype(BF)

    for k in order:
        land(gr_in.at[k, 0:2], G_STEP + 6 * k + 5)
    land(cx_in.at[1:4], C_STEP + 3)
    land(cbz_in, C_STEP + 7)
    for copy in sent.values():
        copy.wait_send()


def scratch():
    def v(*shape, dtype=BF):
        return pltpu.VMEM(shape, dtype)

    return [
        v(1024, CIN), v(PAIRS, 128, dtype=jnp.int32), v(TAPS, SHARE, CIN), v(D, 3 * HEAD), v(D, HEAD),
        v(2, 1024, 128, dtype=F32), v(32, D, dtype=F32), v(WIDE, D), v(2, 16, D), v(576, D), v(768, D),
        v(576, WIDE, dtype=F32), v(2, SHARE, PAIRS, dtype=F32), v(SHARE, PAIRS), v(SHARE, PAIRS),
        v(D, TOK), v(D, TOK), v(D, TOK),
        v(4, HEAD, TOK), v(4, 384, TOK), v(1024, HEAD), v(1024, HEAD), v(4, HEAD, TOK),
        v(4, 1024, TOK, dtype=F32), v(4, 1024, TOK, dtype=F32),
        v(4, 8, TOK, dtype=F32), v(4, 4, 8, TOK, dtype=F32),
        v(4, HEAD, TOK, dtype=F32), v(4, HEAD, TOK), v(4, HEAD, TOK), v(HEAD, TOK),
        v(4, 8, TOK, dtype=F32),
        v(4, HEAD, TOK, dtype=F32), v(4, HEAD, TOK), v(4, HEAD, TOK),
        v(1024, HEAD, dtype=F32), v(1024, HEAD, dtype=F32), v(4, TOK, HEAD), v(4, TOK, HEAD), v(TOK, D), v(TOK, D), v(8, TOK, dtype=F32),
        v(2, TOK, 384), v(2, TOK, 384), v(TOK, 384), v(TOK, 384),
        v(576, TOK),
        v(D, TOK), v(16, SHARE, TOK),
        v(2, 768, TOK), v(4, 2, HEAD, TOK), v(HEAD, TOK), v(HEAD, TOK), v(HEAD, TOK, dtype=F32), v(SHARE, TOK), v(SHARE, TOK),
        v(HEAD, D, dtype=F32), v(4, SHARE, D), v(4, SHARE, D), v(4, SHARE, D),
        v(4, 6, 48, 384), v(4, 2, 48, 384), v(4, 48, 384), v(4, 48, 384), v(4, 48, 384),
        v(576, WIDE), v(2, 256, CIN),
        v(4, 2, 64, 384), v(64, 384), v(64, 384), v(256, 384), v(256, 384), v(4, 64, 384), v(2, 64, 384),
        pltpu.SemaphoreType.DMA((SEMS,)), pltpu.SemaphoreType.DMA((SEMS,)), pltpu.SemaphoreType.DMA((8,)),
    ]


def widen(layer, conv, grads, o_layer, o_conv, o_bias, o_q, o_k, o_v, o_o, cin, gin, cout, gout, lsem, osem):
    loads = [pltpu.make_async_copy(grads.at[k], gin.at[k], lsem.at[k]) for k in range(4)]
    loads.append(pltpu.make_async_copy(conv, cin, lsem.at[4]))
    for load in loads:
        load.start()
    through = pltpu.make_async_copy(layer, o_layer, lsem.at[5])
    through.start()
    stores = [through]
    for k, o in enumerate((o_q, o_k, o_v, o_o)):
        loads[k].wait()
        gout[k] = gin[k].astype(F32)
        stores.append(pltpu.make_async_copy(gout.at[k], o, osem.at[k]))
        stores[-1].start()
    loads[4].wait()
    for t in range(TAPS):
        cout[t] = cin[SHARE * t : SHARE * t + SHARE, :].astype(F32)
        stores.append(pltpu.make_async_copy(cout.at[t], o_conv.at[t], osem.at[4 + t]))
        stores[-1].start()
    o_bias[...] = cin[TAPS * SHARE : TAPS * SHARE + 16, 0:SHARE].astype(F32)[0:1]
    for store in stores:
        store.wait()


def body(features, base_tokens, base_proj, conv_weight, conv_bias, w_query, w_key, w_value, w_out, cotangent):
    vmem = pl.BlockSpec(memory_space=pltpu.VMEM)
    hbm = pl.BlockSpec(memory_space=pl.ANY)
    layer = jax.ShapeDtypeStruct((SHARE, PAIRS), BF)
    narrow = pl.pallas_call(
        kernel,
        out_shape=(layer, jax.ShapeDtypeStruct((2, 256, CIN), BF), jax.ShapeDtypeStruct((4, SHARE, D), BF)),
        in_specs=[hbm, hbm, vmem, hbm, vmem, hbm, hbm, hbm, hbm, hbm],
        out_specs=(vmem,) * 3,
        scratch_shapes=scratch(),
        compiler_params=pltpu.CompilerParams(
            collective_id=0, has_side_effects=True, vmem_limit_bytes=60 * 1024 * 1024
        ),
        cost_estimate=pl.CostEstimate(flops=8_000_000_000, bytes_accessed=8_000_000, transcendentals=1_300_000),
        name="section",
    )(
        features, base_tokens.reshape(PAIRS, 128), base_proj, conv_weight, conv_bias.reshape(1, SHARE),
        w_query, w_key, w_value, w_out, cotangent.T,
    )
    square = jax.ShapeDtypeStruct((SHARE, D), F32)
    layer, conv, bias, gq, gk, gv, go = pl.pallas_call(
        widen,
        out_shape=(
            layer, jax.ShapeDtypeStruct((TAPS, SHARE, CIN), F32), jax.ShapeDtypeStruct((1, SHARE), F32),
            square, square, square, square,
        ),
        in_specs=[hbm] * 3,
        out_specs=(hbm, hbm, vmem, hbm, hbm, hbm, hbm),
        scratch_shapes=[
            pltpu.VMEM((512, CIN), BF), pltpu.VMEM((4, SHARE, D), BF),
            pltpu.VMEM((TAPS, SHARE, CIN), F32), pltpu.VMEM((4, SHARE, D), F32),
            pltpu.SemaphoreType.DMA((6,)), pltpu.SemaphoreType.DMA((9,)),
        ],
        compiler_params=pltpu.CompilerParams(vmem_limit_bytes=60 * 1024 * 1024),
        name="widen",
    )(narrow[0], narrow[1].reshape(512, CIN), narrow[2])
    return layer.T, conv, bias.reshape(SHARE), gq, gk, gv, go


def solution(mesh):
    placed = (
        P("seq", None), P("seq"), P(), P(None, "mp", None), P("mp"),
        P("mp", None), P("mp", None), P("mp", None), P("mp", None), P("seq", "mp"),
    )
    return jax.shard_map(
        body,
        mesh=mesh,
        in_specs=placed,
        out_specs=(
            P("seq", "mp"), P(None, "mp", None), P("mp"),
            P("mp", None), P("mp", None), P("mp", None), P("mp", None),
        ),
        check_vma=False,
    )
```

```python
import functools

import jax
import jax.numpy as jnp
from jax import lax
from jax.experimental import pallas as pl
from jax.experimental.pallas import tpu as pltpu
from jax.sharding import PartitionSpec as P

D = 1536
CIN = 768
TAPS = 5
BIN_WIDTH = 64
EPS = 1e-06
HEAD = 192
SHARE = 96
TOK = 256
PAIRS = 512
WIDE = 640
BF = jnp.bfloat16
F32 = jnp.float32
MESH = pl.DeviceIdType.MESH
SCALE = HEAD ** (-0.5)
ROOT2PI = 0.7978845608028654

(
    COT_AG, TOK_AG, W_SIB, HALO, Q_X, DO_X, ST_X, O_X, DQ_X, K_Z, V_Z, KV_SIB, K_FWD, V_FWD, DKV_FAR, DKV_SIB, DKV_Z,
    OUT_Y, OUT_Z, OUT_SIB, NORM_RS,
) = range(21)
G_SIB = 21
G_STEP = G_SIB + 4
C_STEP = G_STEP + 24
SEMS = C_STEP + 8


def mm(a, b):
    return jnp.dot(a, b, preferred_element_type=F32)


def nt(a, b):
    return lax.dot_general(a, b, (((1,), (1,)), ((), ())), preferred_element_type=F32)


def tn(a, b):
    return lax.dot_general(a, b, (((0,), (0,)), ((), ())), preferred_element_type=F32)


def kernel(
    feat_hbm, toks_hbm, bproj, cw_hbm, cbias, wq, wk, wv, wo, cot_hbm,
    o_layer, c_all, g_all,
    feat, toks, cw, w_t, wo_t, xf, r3, xe, halo, wt, w4, z, slope, tok_own, cot_own, tok_t, cot_t, norm_t,
    q, kv, kn, vn, do, et, dp, st, st_in, o_f, o_send, o_in, ot, fac,
    dq_f, dq_send, dq_in, dk, dv, qn, don, norm_n, cot_n, wide_stat, dkv_send, dkv_in, z_send, z_in, dqkv,
    n_send, n_in, a_send, ay_in, az_send, az_in, az_own, as_send, as_in,
    g_part, g_send, g_sib, g_acc, gr_in, gr_send, gz_send, gz_in, g_red,
    pgs, c_send, cx_in, cz_send, cz_in, cbz_in, cb_held, cx_b, c_red, ssem, rsem, lsem,
):
    s = lax.axis_index("seq")
    m = lax.axis_index("mp")
    zl = s // 4
    x = s % 4
    c = m % 2
    sib = (s, m + 1 - 2 * c)
    zpart = ((1 - zl) * 4 + x, m)
    sent = {}

    def xpeer(r):
        return (zl * 4 + (x + r) % 4, m)

    def seqpeer(r):
        return ((s + r) % 8, m)

    def mppeer(r):
        return (s, (m + r) % 16)

    def push(src, dst, sem, dev):
        pltpu.make_async_remote_copy(
            src_ref=src, dst_ref=dst, send_sem=ssem.at[sem], recv_sem=rsem.at[sem],
            device_id=dev, device_id_type=MESH,
        ).start()

    def land(whole, sem):
        copy = pltpu.make_async_remote_copy(
            src_ref=whole, dst_ref=whole, send_sem=ssem.at[sem], recv_sem=rsem.at[sem],
            device_id=sib, device_id_type=MESH,
        )
        copy.wait_recv()
        sent[sem] = copy

    def al(v, n):
        return pl.multiple_of(v, n)

    barrier = pltpu.get_barrier_semaphore()
    for r in range(1, 16):
        pl.semaphore_signal(barrier, inc=1, device_id=mppeer(r), device_id_type=MESH)
    for r in range(1, 8):
        pl.semaphore_signal(barrier, inc=1, device_id=seqpeer(r), device_id_type=MESH)

    loads = [
        pltpu.make_async_copy(toks_hbm, toks, lsem.at[0]),
        pltpu.make_async_copy(feat_hbm, feat, lsem.at[1]),
        pltpu.make_async_copy(cw_hbm, cw, lsem.at[2]),
        pltpu.make_async_copy(cot_hbm, cot_own, lsem.at[3]),
    ]
    for k, w in enumerate((wq, wk, wv, wo)):
        rows = pl.ds(al(HEAD * k + SHARE * c, 32), SHARE)
        loads.append(pltpu.make_async_copy(w, w4.at[rows], lsem.at[4 + k]))
    for load in loads:
        load.start()
    mine = pl.ds(al(SHARE * m, 32), SHARE)

    y = (m // 2) % 4
    zh = m // 8
    around = (
        (1, 0, 0), (0, 1, 0), (0, 3, 0), (1, 2, 0), (0, 2, 1), (1, 1, 1), (1, 3, 1), (1, 0, 1),
        (0, 1, 1), (0, 3, 1), (1, 2, 1), (0, 2, 0), (1, 1, 0), (1, 3, 0), (0, 0, 1),
    )

    def around_mp(step):
        dz, dy, dc = step
        return ((zh + dz) % 2) * 8 + ((y + dy) % 4) * 2 + (c + dc) % 2

    def spread(own, full, base, steps=around):
        for step in steps:
            cols = pl.ds(al(TOK * ((c + step[2]) % 2), TOK), TOK)
            push(own.at[:, cols], full.at[mine], base, (s, around_mp(step)))

    def keep(own, full):
        full[mine, :] = own[:, pl.ds(al(TOK * c, TOK), TOK)]

    def gathered(full, base):
        land(full.at[0 : 15 * SHARE], base)

    pl.semaphore_wait(barrier, 22)
    spread(cot_hbm, cot_t, COT_AG, around[:9])
    for k, w in enumerate((wo, wq, wk, wv)):
        rows = pl.ds(al(HEAD * ((k + 3) % 4) + SHARE * c, 32), SHARE)
        push(w, w4.at[rows], W_SIB, sib)

    bp = bproj[...]
    hi = bp.astype(BF).astype(F32)
    mid = (bp - hi).astype(BF).astype(F32)
    low = (bp - hi - mid).astype(BF).astype(F32)
    r3[...] = jnp.zeros_like(r3)
    for k, part in enumerate((hi, mid, low)):
        r3[8 * k : 8 * k + 4, 0:CIN] = part
        r3[8 * k + 4 : 8 * k + 8, CIN:D] = part
    lane = lax.broadcasted_iota(jnp.int32, (128, 32), 0)
    col = lax.broadcasted_iota(jnp.int32, (128, 32), 1)
    group = jnp.where(lane >= BIN_WIDTH, 4, 0)
    counts = jnp.zeros((PAIRS, 32), F32)
    loads[0].wait()
    for b in range(4):
        pick = jnp.where((col < 24) & (col % 8 == group + b), 1.0, 0.0).astype(BF)
        match = jnp.where(toks[...] == b, 1.0, 0.0).astype(BF)
        counts = counts + mm(match, pick)
    comp = (counts * (1.0 / BIN_WIDTH)).astype(BF)
    loads[1].wait()
    for k in range(0, 6, 2):
        for i in range(2):
            xf[i] = feat[:, 128 * (k + i) : 128 * (k + i) + 128].astype(F32)
        for half in range(2):
            lo = CIN * half + 128 * k
            extra = mm(comp, r3[:, lo : lo + 256].astype(BF))
            for i in range(2):
                own = xf[i, pl.ds(half, PAIRS, stride=2), :]
                xe[0:PAIRS, lo + 128 * i : lo + 128 * i + 128] = (own + extra[:, 128 * i : 128 * i + 128]).astype(BF)

    push(xe.at[pl.ds(PAIRS - 16, 16)], halo.at[0], HALO, seqpeer(1))
    push(xe.at[pl.ds(0, 16)], halo.at[1], HALO, seqpeer(7))
    loads[2].wait()
    zero = jnp.zeros((SHARE, CIN), BF)
    left = (cw[0], zero, cw[2], cw[1], cw[4], cw[3])
    right = (cw[1], cw[0], cw[3], cw[2], zero, cw[4])
    for g in range(6):
        wt[SHARE * g : SHARE * g + SHARE, 0:CIN] = left[g]
        wt[SHARE * g : SHARE * g + SHARE, CIN:D] = right[g]

    @pl.loop(0, 2)
    def _(i):
        rows = pl.ds(al(i * 256, 256), 256)
        z[:, rows] = nt(wt[...], xe[rows, :])

    land(halo, HALO)
    at = lax.broadcasted_iota(jnp.int32, (16, D), 0)
    after = halo[1].astype(F32)
    before = halo[0].astype(F32)
    after = jnp.where((at == 0) & (s < 7), after, 0.0)
    before = jnp.where((at == 15) & (s > 0), before, 0.0)
    xe[PAIRS:WIDE, :] = jnp.zeros((WIDE - PAIRS, D), BF)
    xe[PAIRS : PAIRS + 16, :] = after.astype(BF)
    xe[WIDE - 16 : WIDE, :] = before.astype(BF)
    z[:, PAIRS:WIDE] = nt(wt[...], xe[PAIRS:WIDE, :])

    offset = jnp.transpose(jnp.broadcast_to(cbias[...], (128, SHARE)))[:, 0:1]
    total = jnp.zeros((SHARE, PAIRS), F32)
    for half in range(2):
        r0, r1, r2 = (SHARE * (2 * d + half) for d in range(3))
        pre = pltpu.roll(z[r0 : r0 + SHARE, :], 1, 1)[:, 0:PAIRS]
        pre = pre + z[r1 : r1 + SHARE, 0:PAIRS]
        pre = pre + pltpu.roll(z[r2 : r2 + SHARE, :], WIDE - 1, 1)[:, 0:PAIRS]
        pre = pre + offset
        square = pre * pre
        bend = jnp.tanh(ROOT2PI * (pre + 0.044715 * (square * pre)))
        total = total + pre * (0.5 * (1.0 + bend))
        slope[half] = 0.5 * (1.0 + bend) + (0.5 * pre) * (1.0 - bend * bend) * (
            ROOT2PI * (1.0 + (3.0 * 0.044715) * square)
        )
    tok_own[...] = (0.5 * total).astype(BF)
    spread(tok_own, tok_t, TOK_AG)
    spread(cot_hbm, cot_t, COT_AG, around[9:])
    keep(tok_own, tok_t)
    for load in loads[3:]:
        load.wait()
    land(w4.at[0 : 4 * SHARE], W_SIB)

    @pl.loop(0, 4)
    def _(k):
        cols = pl.ds(al(384 * k, 128), 384)
        w_t[cols, :] = jnp.transpose(w4[0 : 3 * HEAD, cols].astype(F32)).astype(BF)
        wo_t[cols, :] = jnp.transpose(w4[3 * HEAD : 4 * HEAD, cols].astype(F32)).astype(BF)

    gathered(tok_t, TOK_AG)
    wide = tok_t[...].astype(F32)
    inverse = lax.rsqrt(jnp.sum(wide * wide, axis=0, keepdims=True) * (1.0 / D) + EPS)
    wide_stat[1:2, :] = inverse
    norm_t[...] = (wide * inverse).astype(BF)
    kv[0, 0:HEAD] = mm(w4[HEAD : 2 * HEAD, :], norm_t[...]).astype(BF)
    keys, values = slice(0, HEAD), slice(HEAD, 2 * HEAD)
    push(kv.at[0, keys], kv.at[2, keys], K_Z, zpart)
    push(kv.at[0, keys], kv.at[1, keys], KV_SIB, sib)
    q[0] = mm(w4[0:HEAD, :], norm_t[...]).astype(BF)
    for r in range(1, 4):
        push(q.at[0], q.at[r], Q_X, xpeer(r))
    kv[0, HEAD : 2 * HEAD] = mm(w4[2 * HEAD : 3 * HEAD, :], norm_t[...]).astype(BF)
    push(kv.at[0, values], kv.at[2, values], V_Z, zpart)
    push(kv.at[0, values], kv.at[1, values], KV_SIB, sib)
    keep(cot_own, cot_t)
    gathered(cot_t, COT_AG)
    do[0] = mm(w4[3 * HEAD : 4 * HEAD, :], cot_t[...]).astype(BF)
    for r in range(1, 4):
        push(do.at[0], do.at[r], DO_X, xpeer(r))

    def turn_k(i):
        kn[TOK * i : TOK * i + TOK, :] = jnp.transpose(kv[i, 0:HEAD].astype(F32)).astype(BF)

    def turn_v(i):
        vn[TOK * i : TOK * i + TOK, :] = jnp.transpose(kv[i, HEAD : 2 * HEAD].astype(F32)).astype(BF)

    land(kv.at[2, keys], K_Z)
    push(kv.at[2, keys], kv.at[3, keys], K_FWD, sib)
    turn_k(0)
    turn_v(0)
    don[0] = jnp.transpose(do[0].astype(F32)).astype(BF)
    qn[0] = jnp.transpose(q[0].astype(F32)).astype(BF)
    land(kv.at[1], KV_SIB)
    turn_k(1)
    turn_v(1)
    turn_k(2)
    land(kv.at[2, values], V_Z)
    push(kv.at[2, values], kv.at[3, values], V_FWD, sib)
    turn_v(2)
    land(kv.at[3, keys], K_FWD)
    turn_k(3)
    land(q.at[1:4], Q_X)
    land(kv.at[3, values], V_FWD)
    turn_v(3)
    @pl.loop(0, 4)
    def _(j):
        scores = mm(kn[...], q[j]) * SCALE
        top = jnp.max(scores, axis=0, keepdims=True)
        e = jnp.exp(scores - top)
        et[j] = e
        st[j, 0:1, :] = top
        st[j, 1:2, :] = jnp.sum(e, axis=0, keepdims=True)
        short = e.astype(BF)
        out = mm(kv[0, HEAD : 2 * HEAD, :], short[0:TOK])
        for i in range(1, 4):
            out = out + mm(kv[i, HEAD : 2 * HEAD, :], short[TOK * i : TOK * i + TOK])
        o_f[j] = out

    land(do.at[1:4], DO_X)

    @pl.loop(0, 4)
    def _(j):
        grad = mm(vn[...], do[j])
        dp[j] = grad
        st[j, 2:3, :] = jnp.sum(et[j] * grad, axis=0, keepdims=True)
        st[j, 3:8, :] = jnp.zeros((5, TOK), F32)
        for r in range(1, 4):
            push(st.at[j], st_in.at[r, (j + r) % 4], ST_X, xpeer(r))

    for j in range(1, 4):
        qn[j] = jnp.transpose(q[j].astype(F32)).astype(BF)
        don[j] = jnp.transpose(do[j].astype(F32)).astype(BF)

    @pl.loop(0, 4)
    def _(k):
        cols = pl.ds(al(384 * k, 128), 384)
        norm_n[:, cols] = jnp.transpose(norm_t[cols, :].astype(F32)).astype(BF)

    land(st_in.at[1:4], ST_X)

    factors = []
    deltas = []
    for j in range(4):
        every = [st[j]] + [st_in[r, j] for r in range(1, 4)]
        top = functools.reduce(jnp.maximum, [e[0:1] for e in every])
        norm = sum(e[1:2] * jnp.exp(e[0:1] - top) for e in every)
        log_total = jnp.log(norm) + top
        factors.append(jnp.exp(every[0][0:1] - log_total))
        deltas.append(sum(e[2:3] * jnp.exp(e[0:1] - log_total) for e in every))
    for j in range(4):
        fac[j, 0:1, :] = factors[j]
        fac[j, 1:2, :] = deltas[j]
    for r in range(1, 4):
        o_send[r] = (o_f[r] * factors[r]).astype(BF)
        push(o_send.at[r], o_in.at[4 - r], O_X, xpeer(4 - r))

    def backward(first, j):
        rows = slice(TOK * first, TOK * first + 2 * TOK)
        p = et[j, rows, :] * fac[j, 0:1, :]
        ds = (p * (dp[j, rows, :] - fac[j, 1:2, :]) * SCALE).astype(BF)
        part = mm(kv[first, 0:HEAD, :], ds[0:TOK]) + mm(kv[first + 1, 0:HEAD, :], ds[TOK : 2 * TOK])
        dk[rows, :] += mm(ds, qn[j])
        dv[rows, :] += mm(p.astype(BF), don[j])
        return part

    dk[...] = jnp.zeros_like(dk)
    dv[...] = jnp.zeros_like(dv)

    @pl.loop(0, 4)
    def _(j):
        dq_f[j] = backward(2, j)

    def key_rows(i):
        return slice(TOK * i, TOK * i + TOK)

    def pack(buf, i):
        buf[:, 0:HEAD] = dk[key_rows(i), :].astype(BF)
        buf[:, HEAD : 2 * HEAD] = dv[key_rows(i), :].astype(BF)

    pack(dkv_send.at[0], 3)
    push(dkv_send.at[0], dkv_in.at[0], DKV_FAR, sib)

    def query_block(j):
        dq_send[j] = (dq_f[j] + backward(0, j)).astype(BF)
        push(dq_send.at[j], dq_in.at[4 - j], DQ_X, xpeer(4 - j))

    query_block(2)
    land(dkv_in.at[0], DKV_FAR)
    z_send[:, 0:HEAD] = (dk[key_rows(2), :] + dkv_in[0, :, 0:HEAD].astype(F32)).astype(BF)
    z_send[:, HEAD : 2 * HEAD] = (dv[key_rows(2), :] + dkv_in[0, :, HEAD : 2 * HEAD].astype(F32)).astype(BF)
    push(z_send, z_in, DKV_Z, zpart)

    @pl.loop(0, 2)
    def _(i):
        query_block(1 + 2 * i)

    dq_f[0] = dq_f[0] + backward(0, 0)
    pack(dkv_send.at[1], 1)
    push(dkv_send.at[1], dkv_in.at[1], DKV_SIB, sib)

    def grad_w(k, grads, inputs):
        g_part[...] = mm(grads[...], inputs[...])
        g_send[k] = g_part[pl.ds(al(SHARE * (1 - c), 32), SHARE), :].astype(BF)
        g_acc[k] = g_part[pl.ds(al(SHARE * c, 32), SHARE), :].astype(BF)
        push(g_send.at[k], g_sib.at[k], G_SIB + k, sib)

    def grad_sum(k):
        land(g_sib.at[k], G_SIB + k)
        g_acc[k] = (g_acc[k].astype(F32) + g_sib[k].astype(F32)).astype(BF)

    def g_piece(k):
        return lambda buf, z, at: buf.at[k, pl.ds(al(48 * z, 16), 48), pl.ds(al(384 * at, 128), 384)]

    def c_col(buf, at):
        return buf.at[:, pl.ds(al(64 * at, 64), 64), 0:384]

    def c_row(buf, at):
        return buf.at[at, :, 384:CIN]

    def c_piece(lanes):
        return lambda buf, z, at: buf.at[z, pl.ds(al(64 * at, 64), 64), lanes]

    def a_first(src, col, into, sem):
        for r in range(1, 4):
            push(col(src, (x + r) % 4), into.at[r], sem, xpeer(r))

    def a_second(src, piece, into, part, send, into_z, sem):
        land(into.at[1:4], sem)

        def total(z):
            own = piece(src, z, x)[...].astype(F32)
            return own + sum(part(into, r, z)[...].astype(F32) for r in range(1, 4))

        send[...] = total(1 - zl).astype(BF)
        push(send, into_z, sem + 1, zpart)
        return total(zl)

    def a_third(held, piece, full, red, into_z, sem):
        land(into_z, sem + 1)
        red[...] = (held + into_z[...].astype(F32)).astype(BF)
        push(red, piece(full, zl, x), sem + 2, zpart)
        piece(full, zl, x)[...] = red[...]

    right, left = xpeer(1), xpeer(3)

    def r_first(src, piece, into, sem):
        push(piece(src, 0, (x + 2) % 4), into.at[0], sem, right)
        push(piece(src, 1, (x + 2) % 4), into.at[1], sem, left)
        push(piece(src, 1, (x + 1) % 4), into.at[3], sem + 1, right)
        push(piece(src, 0, (x + 3) % 4), into.at[4], sem + 1, left)

    def r_second(src, piece, into, send, sem):
        land(into.at[0:2], sem)
        send[0] = (piece(src, 0, (x + 1) % 4)[...].astype(F32) + into[0].astype(F32)).astype(BF)
        send[1] = (piece(src, 1, (x + 3) % 4)[...].astype(F32) + into[1].astype(F32)).astype(BF)
        push(send.at[0], into.at[2], sem + 1, right)
        push(send.at[1], into.at[5], sem + 1, left)

    def r_third(src, piece, into, send, into_z, sem):
        land(into.at[2:6], sem + 1)

        def total(z):
            own = piece(src, z, x)[...].astype(F32)
            return own + into[2 + z].astype(F32) + into[4 + z].astype(F32)

        send[...] = total(1 - zl).astype(BF)
        push(send, into_z, sem + 2, zpart)
        return total(zl)

    def r_fourth(held, piece, full, red, into_z, sem):
        land(into_z, sem + 2)
        red[...] = (held + into_z[...].astype(F32)).astype(BF)
        push(red, piece(full, zl, x), sem + 3, zpart)
        for dev in (right, left):
            push(red, piece(full, zl, x), sem + 4, dev)
        piece(full, zl, x)[...] = red[...]

    def s_fourth(held, piece, full, red, into_z, sem):
        land(into_z, sem + 2)
        red[...] = (held + into_z[...].astype(F32)).astype(BF)
        for r in range(1, 4):
            push(red, piece(full, zl, x), sem + 3, xpeer(r))
        piece(full, zl, x)[...] = red[...]

    def s_fifth(row, full, into, sem):
        land(into.at[0:3], sem + 3)
        push(row(full, zl), row(full, zl), sem + 4, zpart)

    def g_row(k):
        return lambda buf, at: buf.at[k, pl.ds(al(48 * at, 16), 48), :]

    def r_fifth(piece, full, red, sem):
        land(red, sem + 3)
        for dev in (right, left):
            push(piece(full, 1 - zl, x), piece(full, 1 - zl, x), sem + 4, dev)

    def r_sixth(piece, full, into, sem):
        land(into.at[0:4], sem + 4)
        push(piece(full, 0, (x + 3) % 4), piece(full, 0, (x + 3) % 4), sem + 5, right)
        push(piece(full, 1, (x + 1) % 4), piece(full, 1, (x + 1) % 4), sem + 5, left)

    def a_fourth(col, full, red, sem):
        land(red, sem + 2)
        for r in range(1, 4):
            push(col(full, x), col(full, x), sem + 3, xpeer(r))

    def b_first(src, row, into_z, sem):
        push(row(src, 1 - zl), into_z, sem, zpart)

    def b_second(src, row, part, held, into_z, into, sem):
        land(into_z, sem)
        held[...] = (row(src, zl)[...].astype(F32) + into_z[...].astype(F32)).astype(BF)
        for r in range(1, 4):
            push(part(held, (x + r) % 4), into.at[r], sem + 1, xpeer(r))

    def b_third(part, piece, full, held, into, red, sem):
        land(into.at[1:4], sem + 1)
        red[...] = (part(held, x)[...].astype(F32) + sum(into[r].astype(F32) for r in range(1, 4))).astype(BF)
        for r in range(1, 4):
            push(red, piece(full, zl, x), sem + 2, xpeer(r))
        piece(full, zl, x)[...] = red[...]

    def b_fourth(row, full, into, sem):
        land(into.at[1:4], sem + 2)
        push(row(full, zl), row(full, zl), sem + 3, zpart)

    def ca_part(buf, r, z):
        return buf.at[r, z]

    def cb_part(buf, at):
        return buf.at[pl.ds(al(64 * at, 64), 64)]

    def reduced(into, base):
        land(into.at[1:16], base)
        same = sum(into[r].astype(F32) for r in range(0, 16, 2))
        other = sum(into[r].astype(F32) for r in range(1, 16, 2))
        first = jnp.where(c == 0, same, other)
        second = jnp.where(c == 0, other, same)
        return first, second

    land(o_in.at[1:4], O_X)
    ot[...] = (o_f[0] * factors[0] + sum(o_in[r].astype(F32) for r in range(1, 4))).astype(BF)

    @pl.loop(0, 4)
    def _(k):
        cols = pl.ds(al(384 * k, 128), 384)
        cot_n[:, cols] = jnp.transpose(cot_t[cols, :].astype(F32)).astype(BF)

    grad_w(3, ot, cot_n)


    land(dkv_in.at[1], DKV_SIB)
    land(z_in, DKV_Z)
    grad_k = dk[key_rows(0), :] + (dkv_in[1, :, 0:HEAD].astype(F32) + z_in[:, 0:HEAD].astype(F32))
    grad_v = dv[key_rows(0), :] + (dkv_in[1, :, HEAD : 2 * HEAD].astype(F32) + z_in[:, HEAD : 2 * HEAD].astype(F32))
    dqkv[HEAD : 2 * HEAD, :] = jnp.transpose(grad_k).astype(BF)
    dqkv[2 * HEAD : 3 * HEAD, :] = jnp.transpose(grad_v).astype(BF)
    land(dq_in.at[1:4], DQ_X)
    grad_q = dq_f[0] + sum(dq_in[r].astype(F32) for r in range(1, 4))
    dqkv[0:HEAD, :] = grad_q.astype(BF)

    row_stat = jnp.sum(dqkv[0:HEAD, :].astype(F32) * q[0].astype(F32), axis=0, keepdims=True)
    row_stat = row_stat + jnp.sum(dqkv[HEAD:, :].astype(F32) * kv[0].astype(F32), axis=0, keepdims=True)
    wide_stat[0:1, :] = row_stat * (1.0 / D)

    def scatter_rows(k):
        cols = pl.ds(al(384 * k, 128), 384)
        inverse = wide_stat[1:2, :]
        unit = tok_t[cols, :].astype(F32) * inverse
        n_send[cols, :] = (inverse * (mm(w_t[cols, :], dqkv[...]) - unit * wide_stat[0:1, :])).astype(BF)

    @pl.loop(0, 4)
    def _(k):
        scatter_rows(k)

    for step in around:
        peer = around_mp(step)
        slot = step[0] * 8 + step[1] * 2 + step[2]
        push(n_send.at[pl.ds(al(SHARE * peer, 32), SHARE)], n_in.at[slot], NORM_RS, (s, peer))
    n_in[0] = n_send[mine, :]

    grad_sum(3)
    r_first(g_acc, g_piece(3), gr_in.at[3], G_STEP + 18)

    for k in range(3):
        grad_w(k, dqkv.at[HEAD * k : HEAD * k + HEAD], norm_n)
    for k in range(3):
        grad_sum(k)
        r_first(g_acc, g_piece(k), gr_in.at[k], G_STEP + 6 * k)
    @pl.loop(0, 4)
    def _(k):
        cols = pl.ds(al(384 * k, 128), 384)
        a_send[k // 2, pl.ds(al(384 * (k % 2), 128), 384), :] = mm(wo_t[cols, :], ot[...]).astype(BF)

    held = {}
    order = (3, 0, 1, 2)
    for k in order:
        r_second(g_acc, g_piece(k), gr_in.at[k], gr_send.at[k], G_STEP + 6 * k)
    first, second = reduced(n_in, NORM_RS)
    for r in range(1, 4):
        rows = pl.ds(al(HEAD * ((y + r) % 4), 64), HEAD)
        push(a_send.at[:, rows], ay_in.at[r], OUT_Y, (s, zh * 8 + ((y + r) % 4) * 2 + c))
    tok_grad = cot_own[...].astype(F32) + jnp.concatenate([first, second], axis=1)
    pad = jnp.zeros((SHARE, WIDE - PAIRS), F32)
    for half in range(2):
        pg = jnp.concatenate([0.5 * tok_grad * slope[half], pad], axis=1)
        for d in range(3):
            shift = (WIDE - 1, 0, 1)[d]
            moved = pltpu.roll(pg, shift, 1) if shift else pg
            row = SHARE * (2 * d + half)
            pgs[row : row + SHARE, :] = moved.astype(BF)
    both = pgs[2 * SHARE : 3 * SHARE, 0:PAIRS], pgs[3 * SHARE : 4 * SHARE, 0:PAIRS]
    ones = jnp.ones((16, PAIRS), BF)
    bias = nt(ones, both[0]) + nt(ones, both[1])
    c_send[1, 224:256, :] = jnp.zeros((32, CIN), BF)
    c_send[1, 224:240, 0:SHARE] = bias.astype(BF)

    @pl.loop(0, 3)
    def _(k):
        cols = pl.ds(al(256 * k, 256), 256)
        odd_cols = pl.ds(al(CIN + 256 * k, 256), 256)
        me = mm(pgs[...], xe[:, cols])
        mo = mm(pgs[...], xe[:, odd_cols])

        def part(arr, d, half):
            row = SHARE * (2 * (d + 1) + half)
            return arr[row : row + SHARE]

        taps = (
            part(me, -1, 0) + part(mo, -1, 1),
            part(mo, -1, 0) + part(me, 0, 1),
            part(me, 0, 0) + part(mo, 0, 1),
            part(mo, 0, 0) + part(me, 1, 1),
            part(me, 1, 0) + part(mo, 1, 1),
        )
        for t in range(TAPS):
            tap = taps[t].astype(BF)
            if t < 2:
                c_send[0, SHARE * t : SHARE * t + SHARE, cols] = tap
            elif t == 2:
                c_send[0, 192:256, cols] = tap[0:64]
                c_send[1, 0:32, cols] = tap[64:96]
            else:
                c_send[1, SHARE * t - 256 : SHARE * t - 160, cols] = tap

    low, high = slice(0, 384), slice(384, CIN)
    a_first(c_send, c_col, cx_in, C_STEP)
    b_first(c_send, c_row, cbz_in, C_STEP + 4)

    for k in order:
        held[k] = r_third(g_acc, g_piece(k), gr_in.at[k], gz_send.at[k], gz_in.at[k], G_STEP + 6 * k)
    held_c = a_second(c_send, c_piece(low), cx_in, ca_part, cz_send, cz_in, C_STEP)
    b_second(c_send, c_row, cb_part, cb_held, cbz_in, cx_b, C_STEP + 4)
    for k in order:
        fourth = r_fourth if k in (0, 3) else s_fourth
        fourth(held[k], g_piece(k), g_all, g_red.at[k], gz_in.at[k], G_STEP + 6 * k)
    a_third(held_c, c_piece(low), c_all, c_red.at[0], cz_in, C_STEP)
    b_third(cb_part, c_piece(high), c_all, cb_held, cx_b, c_red.at[1], C_STEP + 4)
    land(ay_in.at[1:4], OUT_Y)
    rows = pl.ds(al(HEAD * y, 64), HEAD)

    def over_y(z):
        return a_send[z, rows, :].astype(F32) + sum(ay_in[r, z].astype(F32) for r in range(1, 4))

    az_send[...] = over_y(1 - zh).astype(BF)
    push(az_send, az_in, OUT_Z, (s, (m + 8) % 16))
    az_own[...] = over_y(zh)
    for k in (3, 0):
        r_fifth(g_piece(k), g_all, g_red.at[k], G_STEP + 6 * k)
    a_fourth(c_col, c_all, c_red.at[0], C_STEP)
    b_fourth(c_row, c_all, cx_b, C_STEP + 4)
    for k in (1, 2):
        s_fifth(g_row(k), g_all, gr_in.at[k], G_STEP + 6 * k)
    for k in (3, 0):
        r_sixth(g_piece(k), g_all, gr_in.at[k], G_STEP + 6 * k)

    land(az_in, OUT_Z)
    az_own[...] = az_own[...] + az_in[...].astype(F32)
    as_send[...] = az_own[pl.ds(al(SHARE * (1 - c), 32), SHARE), :].astype(BF)
    push(as_send, as_in, OUT_SIB, sib)
    own = az_own[pl.ds(al(SHARE * c, 32), SHARE), :]
    land(as_in, OUT_SIB)
    other = as_in[...].astype(F32)
    out = jnp.concatenate([jnp.where(c == 0, own, other), jnp.where(c == 0, other, own)], axis=1)
    o_layer[...] = (out + tok_own[...].astype(F32)).astype(BF)

    for k in (3, 0):
        land(gr_in.at[k, 0:2], G_STEP + 6 * k + 5)
    for k in (1, 2):
        land(gr_in.at[k, 0:4], G_STEP + 6 * k + 4)
    land(cx_in.at[1:4], C_STEP + 3)
    land(cbz_in, C_STEP + 7)
    for copy in sent.values():
        copy.wait_send()


def scratch():
    def v(*shape, dtype=BF):
        return pltpu.VMEM(shape, dtype)

    return [
        v(1024, CIN), v(PAIRS, 128, dtype=jnp.int32), v(TAPS, SHARE, CIN), v(D, 3 * HEAD), v(D, HEAD),
        v(2, 1024, 128, dtype=F32), v(32, D, dtype=F32), v(WIDE, D), v(2, 16, D), v(576, D), v(768, D),
        v(576, WIDE, dtype=F32), v(2, SHARE, PAIRS, dtype=F32), v(SHARE, PAIRS), v(SHARE, PAIRS),
        v(D, TOK), v(D, TOK), v(D, TOK),
        v(4, HEAD, TOK), v(4, 384, TOK), v(1024, HEAD), v(1024, HEAD), v(4, HEAD, TOK),
        v(4, 1024, TOK, dtype=F32), v(4, 1024, TOK, dtype=F32),
        v(4, 8, TOK, dtype=F32), v(4, 4, 8, TOK, dtype=F32),
        v(4, HEAD, TOK, dtype=F32), v(4, HEAD, TOK), v(4, HEAD, TOK), v(HEAD, TOK),
        v(4, 8, TOK, dtype=F32),
        v(4, HEAD, TOK, dtype=F32), v(4, HEAD, TOK), v(4, HEAD, TOK),
        v(1024, HEAD, dtype=F32), v(1024, HEAD, dtype=F32), v(4, TOK, HEAD), v(4, TOK, HEAD), v(TOK, D), v(TOK, D), v(8, TOK, dtype=F32),
        v(2, TOK, 384), v(2, TOK, 384), v(TOK, 384), v(TOK, 384),
        v(576, TOK),
        v(D, TOK), v(16, SHARE, TOK),
        v(2, 768, TOK), v(4, 2, HEAD, TOK), v(HEAD, TOK), v(HEAD, TOK), v(HEAD, TOK, dtype=F32), v(SHARE, TOK), v(SHARE, TOK),
        v(HEAD, D, dtype=F32), v(4, SHARE, D), v(4, SHARE, D), v(4, SHARE, D),
        v(4, 6, 48, 384), v(4, 2, 48, 384), v(4, 48, 384), v(4, 48, 384), v(4, 48, 384),
        v(576, WIDE), v(2, 256, CIN),
        v(4, 2, 64, 384), v(64, 384), v(64, 384), v(256, 384), v(256, 384), v(4, 64, 384), v(2, 64, 384),
        pltpu.SemaphoreType.DMA((SEMS,)), pltpu.SemaphoreType.DMA((SEMS,)), pltpu.SemaphoreType.DMA((8,)),
    ]


def widen(layer, conv, grads, o_layer, o_conv, o_bias, o_q, o_k, o_v, o_o, cin, gin, cout, gout, lsem, osem):
    loads = [pltpu.make_async_copy(grads.at[k], gin.at[k], lsem.at[k]) for k in range(4)]
    loads.append(pltpu.make_async_copy(conv, cin, lsem.at[4]))
    for load in loads:
        load.start()
    through = pltpu.make_async_copy(layer, o_layer, lsem.at[5])
    through.start()
    stores = [through]
    for k, o in enumerate((o_q, o_k, o_v, o_o)):
        loads[k].wait()
        gout[k] = gin[k].astype(F32)
        stores.append(pltpu.make_async_copy(gout.at[k], o, osem.at[k]))
        stores[-1].start()
    loads[4].wait()
    for t in range(TAPS):
        cout[t] = cin[SHARE * t : SHARE * t + SHARE, :].astype(F32)
        stores.append(pltpu.make_async_copy(cout.at[t], o_conv.at[t], osem.at[4 + t]))
        stores[-1].start()
    o_bias[...] = cin[TAPS * SHARE : TAPS * SHARE + 16, 0:SHARE].astype(F32)[0:1]
    for store in stores:
        store.wait()


def body(features, base_tokens, base_proj, conv_weight, conv_bias, w_query, w_key, w_value, w_out, cotangent):
    vmem = pl.BlockSpec(memory_space=pltpu.VMEM)
    hbm = pl.BlockSpec(memory_space=pl.ANY)
    layer = jax.ShapeDtypeStruct((SHARE, PAIRS), BF)
    narrow = pl.pallas_call(
        kernel,
        out_shape=(layer, jax.ShapeDtypeStruct((2, 256, CIN), BF), jax.ShapeDtypeStruct((4, SHARE, D), BF)),
        in_specs=[hbm, hbm, vmem, hbm, vmem, hbm, hbm, hbm, hbm, hbm],
        out_specs=(vmem,) * 3,
        scratch_shapes=scratch(),
        compiler_params=pltpu.CompilerParams(
            collective_id=0, has_side_effects=True, vmem_limit_bytes=60 * 1024 * 1024
        ),
        cost_estimate=pl.CostEstimate(flops=8_000_000_000, bytes_accessed=8_000_000, transcendentals=1_300_000),
        name="section",
    )(
        features, base_tokens.reshape(PAIRS, 128), base_proj, conv_weight, conv_bias.reshape(1, SHARE),
        w_query, w_key, w_value, w_out, cotangent.T,
    )
    square = jax.ShapeDtypeStruct((SHARE, D), F32)
    layer, conv, bias, gq, gk, gv, go = pl.pallas_call(
        widen,
        out_shape=(
            layer, jax.ShapeDtypeStruct((TAPS, SHARE, CIN), F32), jax.ShapeDtypeStruct((1, SHARE), F32),
            square, square, square, square,
        ),
        in_specs=[hbm] * 3,
        out_specs=(hbm, hbm, vmem, hbm, hbm, hbm, hbm),
        scratch_shapes=[
            pltpu.VMEM((512, CIN), BF), pltpu.VMEM((4, SHARE, D), BF),
            pltpu.VMEM((TAPS, SHARE, CIN), F32), pltpu.VMEM((4, SHARE, D), F32),
            pltpu.SemaphoreType.DMA((6,)), pltpu.SemaphoreType.DMA((9,)),
        ],
        compiler_params=pltpu.CompilerParams(vmem_limit_bytes=60 * 1024 * 1024),
        name="widen",
    )(narrow[0], narrow[1].reshape(512, CIN), narrow[2])
    return layer.T, conv, bias.reshape(SHARE), gq, gk, gv, go


def solution(mesh):
    placed = (
        P("seq", None), P("seq"), P(), P(None, "mp", None), P("mp"),
        P("mp", None), P("mp", None), P("mp", None), P("mp", None), P("seq", "mp"),
    )
    return jax.shard_map(
        body,
        mesh=mesh,
        in_specs=placed,
        out_specs=(
            P("seq", "mp"), P(None, "mp", None), P("mp"),
            P("mp", None), P("mp", None), P("mp", None), P("mp", None),
        ),
        check_vma=False,
    )
```

```python
import functools

import jax
import jax.numpy as jnp
from jax import lax
from jax.experimental import pallas as pl
from jax.experimental.pallas import tpu as pltpu
from jax.sharding import PartitionSpec as P

D = 1536
CIN = 768
TAPS = 5
BIN_WIDTH = 64
EPS = 1e-06
HEAD = 192
SHARE = 96
TOK = 256
PAIRS = 512
WIDE = 640
BF = jnp.bfloat16
F32 = jnp.float32
MESH = pl.DeviceIdType.MESH
SCALE = HEAD ** (-0.5)
ROOT2PI = 0.7978845608028654

(
    COT_AG, TOK_AG, W_SIB, HALO, Q_X, DO_X, ST_X, O_X, DQ_X, K_Z, V_Z, KV_SIB, K_FWD, V_FWD, DKV_FAR, DKV_SIB, DKV_Z,
    OUT_Y, OUT_Z, OUT_SIB, NORM_RS, VIA_C, VIA_T, VIA_N,
) = range(24)
G_SIB = 24
G_STEP = G_SIB + 4
C_STEP = G_STEP + 24
SEMS = C_STEP + 8


def mm(a, b):
    return jnp.dot(a, b, preferred_element_type=F32)


def nt(a, b):
    return lax.dot_general(a, b, (((1,), (1,)), ((), ())), preferred_element_type=F32)


def tn(a, b):
    return lax.dot_general(a, b, (((0,), (0,)), ((), ())), preferred_element_type=F32)


def kernel(
    feat_hbm, toks_hbm, bproj, cw_hbm, cbias, wq, wk, wv, wo, cot_hbm,
    o_layer, c_all, g_all,
    feat, toks, cw, w_t, wo_t, xf, r3, xe, halo, wt, w4, z, slope, tok_own, cot_own, tok_t, cot_t, norm_t,
    q, kv, kn, vn, do, et, dp, st, st_in, o_f, o_send, o_in, ot, fac,
    dq_f, dq_send, dq_in, dk, dv, qn, don, norm_n, cot_n, wide_stat, dkv_send, dkv_in, z_send, z_in, dqkv,
    n_send, n_in, a_send, ay_in, az_send, az_in, az_own, as_send, as_in,
    g_part, g_send, g_sib, g_acc, gr_in, gr_send, gz_send, gz_in, g_red,
    pgs, c_send, cx_in, cz_send, cz_in, cbz_in, cb_held, cx_b, c_red, via_c, via_t, via_n, ssem, rsem, lsem,
):
    s = lax.axis_index("seq")
    m = lax.axis_index("mp")
    zl = s // 4
    x = s % 4
    c = m % 2
    y = (m // 2) % 4
    zh = m // 8
    sib = (s, m + 1 - 2 * c)
    z_down, z_up = (zh * 2 + zl + 3) % 4, (zh * 2 + zl + 1) % 4

    def at_z(z4, row, core):
        return ((z4 % 2) * 4 + x, (z4 // 2) * 8 + row * 2 + core)

    relayed = ((1, 0, 0), (1, 0, 1), (1, 1, 0), (1, 3, 1))

    def far_end(step):
        return at_z(z_down, (y + step[1]) % 4, (c + step[2]) % 2)

    zpart = ((1 - zl) * 4 + x, m)
    sent = {}

    def xpeer(r):
        return (zl * 4 + (x + r) % 4, m)

    def seqpeer(r):
        return ((s + r) % 8, m)

    def mppeer(r):
        return (s, (m + r) % 16)

    def push(src, dst, sem, dev):
        pltpu.make_async_remote_copy(
            src_ref=src, dst_ref=dst, send_sem=ssem.at[sem], recv_sem=rsem.at[sem],
            device_id=dev, device_id_type=MESH,
        ).start()

    def land(whole, sem):
        copy = pltpu.make_async_remote_copy(
            src_ref=whole, dst_ref=whole, send_sem=ssem.at[sem], recv_sem=rsem.at[sem],
            device_id=sib, device_id_type=MESH,
        )
        copy.wait_recv()
        sent[sem] = copy

    def al(v, n):
        return pl.multiple_of(v, n)

    barrier = pltpu.get_barrier_semaphore()
    for r in range(1, 16):
        pl.semaphore_signal(barrier, inc=1, device_id=mppeer(r), device_id_type=MESH)
    for r in range(1, 8):
        pl.semaphore_signal(barrier, inc=1, device_id=seqpeer(r), device_id_type=MESH)
    for step in relayed:
        source = at_z(z_up, (y + 4 - step[1]) % 4, (c + step[2]) % 2)
        pl.semaphore_signal(barrier, inc=1, device_id=source, device_id_type=MESH)

    loads = [
        pltpu.make_async_copy(toks_hbm, toks, lsem.at[0]),
        pltpu.make_async_copy(feat_hbm, feat, lsem.at[1]),
        pltpu.make_async_copy(cw_hbm, cw, lsem.at[2]),
        pltpu.make_async_copy(cot_hbm, cot_own, lsem.at[3]),
    ]
    for k, w in enumerate((wq, wk, wv, wo)):
        rows = pl.ds(al(HEAD * k + SHARE * c, 32), SHARE)
        loads.append(pltpu.make_async_copy(w, w4.at[rows], lsem.at[4 + k]))
    for load in loads:
        load.start()
    mine = pl.ds(al(SHARE * m, 32), SHARE)

    around = (
        (1, 1, 0), (1, 2, 0), (0, 1, 0), (0, 3, 0), (1, 3, 1), (1, 1, 1), (1, 0, 1), (0, 2, 1), (1, 0, 0),
        (1, 2, 1), (0, 1, 1), (0, 3, 1), (1, 3, 0), (0, 2, 0), (0, 0, 1),
    )

    def around_mp(step):
        dz, dy, dc = step
        return ((zh + dz) % 2) * 8 + ((y + dy) % 4) * 2 + (c + dc) % 2

    def spread(own, full, base, via, via_sem, steps=around):
        for step in steps:
            cols = pl.ds(al(TOK * ((c + step[2]) % 2), TOK), TOK)
            if step in relayed:
                push(own.at[:, cols], via.at[relayed.index(step)], via_sem, at_z(z_down, y, c))
            else:
                push(own.at[:, cols], full.at[mine], base, (s, around_mp(step)))

    def pass_on(full, base, via, via_sem):
        land(via, via_sem)
        rows = pl.ds(al(SHARE * ((z_up // 2) * 8 + y * 2 + c), 32), SHARE)
        for i, step in enumerate(relayed):
            push(via.at[i], full.at[rows], base, far_end(step))

    def keep(own, full):
        full[mine, :] = own[:, pl.ds(al(TOK * c, TOK), TOK)]

    def gathered(full, base):
        land(full.at[0 : 15 * SHARE], base)

    pl.semaphore_wait(barrier, 26)
    spread(cot_hbm, cot_t, COT_AG, via_c, VIA_C, around[:9])
    for k, w in enumerate((wo, wq, wk, wv)):
        rows = pl.ds(al(HEAD * ((k + 3) % 4) + SHARE * c, 32), SHARE)
        push(w, w4.at[rows], W_SIB, sib)

    bp = bproj[...]
    hi = bp.astype(BF).astype(F32)
    mid = (bp - hi).astype(BF).astype(F32)
    low = (bp - hi - mid).astype(BF).astype(F32)
    r3[...] = jnp.zeros_like(r3)
    for k, part in enumerate((hi, mid, low)):
        r3[8 * k : 8 * k + 4, 0:CIN] = part
        r3[8 * k + 4 : 8 * k + 8, CIN:D] = part
    lane = lax.broadcasted_iota(jnp.int32, (128, 32), 0)
    col = lax.broadcasted_iota(jnp.int32, (128, 32), 1)
    group = jnp.where(lane >= BIN_WIDTH, 4, 0)
    counts = jnp.zeros((PAIRS, 32), F32)
    loads[0].wait()
    for b in range(4):
        pick = jnp.where((col < 24) & (col % 8 == group + b), 1.0, 0.0).astype(BF)
        match = jnp.where(toks[...] == b, 1.0, 0.0).astype(BF)
        counts = counts + mm(match, pick)
    comp = (counts * (1.0 / BIN_WIDTH)).astype(BF)
    loads[1].wait()
    for k in range(0, 6, 2):
        for i in range(2):
            xf[i] = feat[:, 128 * (k + i) : 128 * (k + i) + 128].astype(F32)
        for half in range(2):
            lo = CIN * half + 128 * k
            extra = mm(comp, r3[:, lo : lo + 256].astype(BF))
            for i in range(2):
                own = xf[i, pl.ds(half, PAIRS, stride=2), :]
                xe[0:PAIRS, lo + 128 * i : lo + 128 * i + 128] = (own + extra[:, 128 * i : 128 * i + 128]).astype(BF)

    push(xe.at[pl.ds(PAIRS - 16, 16)], halo.at[0], HALO, seqpeer(1))
    push(xe.at[pl.ds(0, 16)], halo.at[1], HALO, seqpeer(7))
    loads[2].wait()
    zero = jnp.zeros((SHARE, CIN), BF)
    left = (cw[0], zero, cw[2], cw[1], cw[4], cw[3])
    right = (cw[1], cw[0], cw[3], cw[2], zero, cw[4])
    for g in range(6):
        wt[SHARE * g : SHARE * g + SHARE, 0:CIN] = left[g]
        wt[SHARE * g : SHARE * g + SHARE, CIN:D] = right[g]

    @pl.loop(0, 2)
    def _(i):
        rows = pl.ds(al(i * 256, 256), 256)
        z[:, rows] = nt(wt[...], xe[rows, :])

    pass_on(cot_t, COT_AG, via_c, VIA_C)
    land(halo, HALO)
    at = lax.broadcasted_iota(jnp.int32, (16, D), 0)
    after = halo[1].astype(F32)
    before = halo[0].astype(F32)
    after = jnp.where((at == 0) & (s < 7), after, 0.0)
    before = jnp.where((at == 15) & (s > 0), before, 0.0)
    xe[PAIRS:WIDE, :] = jnp.zeros((WIDE - PAIRS, D), BF)
    xe[PAIRS : PAIRS + 16, :] = after.astype(BF)
    xe[WIDE - 16 : WIDE, :] = before.astype(BF)
    z[:, PAIRS:WIDE] = nt(wt[...], xe[PAIRS:WIDE, :])

    offset = jnp.transpose(jnp.broadcast_to(cbias[...], (128, SHARE)))[:, 0:1]
    total = jnp.zeros((SHARE, PAIRS), F32)
    for half in range(2):
        r0, r1, r2 = (SHARE * (2 * d + half) for d in range(3))
        pre = pltpu.roll(z[r0 : r0 + SHARE, :], 1, 1)[:, 0:PAIRS]
        pre = pre + z[r1 : r1 + SHARE, 0:PAIRS]
        pre = pre + pltpu.roll(z[r2 : r2 + SHARE, :], WIDE - 1, 1)[:, 0:PAIRS]
        pre = pre + offset
        square = pre * pre
        bend = jnp.tanh(ROOT2PI * (pre + 0.044715 * (square * pre)))
        total = total + pre * (0.5 * (1.0 + bend))
        slope[half] = 0.5 * (1.0 + bend) + (0.5 * pre) * (1.0 - bend * bend) * (
            ROOT2PI * (1.0 + (3.0 * 0.044715) * square)
        )
    tok_own[...] = (0.5 * total).astype(BF)
    spread(tok_own, tok_t, TOK_AG, via_t, VIA_T)
    spread(cot_hbm, cot_t, COT_AG, via_c, VIA_C, around[9:])
    keep(tok_own, tok_t)
    pass_on(tok_t, TOK_AG, via_t, VIA_T)
    for load in loads[3:]:
        load.wait()
    land(w4.at[0 : 4 * SHARE], W_SIB)

    @pl.loop(0, 4)
    def _(k):
        cols = pl.ds(al(384 * k, 128), 384)
        w_t[cols, :] = jnp.transpose(w4[0 : 3 * HEAD, cols].astype(F32)).astype(BF)
        wo_t[cols, :] = jnp.transpose(w4[3 * HEAD : 4 * HEAD, cols].astype(F32)).astype(BF)

    gathered(tok_t, TOK_AG)
    wide = tok_t[...].astype(F32)
    inverse = lax.rsqrt(jnp.sum(wide * wide, axis=0, keepdims=True) * (1.0 / D) + EPS)
    wide_stat[1:2, :] = inverse
    norm_t[...] = (wide * inverse).astype(BF)
    kv[0, 0:HEAD] = mm(w4[HEAD : 2 * HEAD, :], norm_t[...]).astype(BF)
    keys, values = slice(0, HEAD), slice(HEAD, 2 * HEAD)
    push(kv.at[0, keys], kv.at[2, keys], K_Z, zpart)
    push(kv.at[0, keys], kv.at[1, keys], KV_SIB, sib)
    q[0] = mm(w4[0:HEAD, :], norm_t[...]).astype(BF)
    for r in range(1, 4):
        push(q.at[0], q.at[r], Q_X, xpeer(r))
    kv[0, HEAD : 2 * HEAD] = mm(w4[2 * HEAD : 3 * HEAD, :], norm_t[...]).astype(BF)
    push(kv.at[0, values], kv.at[2, values], V_Z, zpart)
    push(kv.at[0, values], kv.at[1, values], KV_SIB, sib)
    keep(cot_own, cot_t)
    gathered(cot_t, COT_AG)
    do[0] = mm(w4[3 * HEAD : 4 * HEAD, :], cot_t[...]).astype(BF)
    for r in range(1, 4):
        push(do.at[0], do.at[r], DO_X, xpeer(r))

    def turn_k(i):
        kn[TOK * i : TOK * i + TOK, :] = jnp.transpose(kv[i, 0:HEAD].astype(F32)).astype(BF)

    def turn_v(i):
        vn[TOK * i : TOK * i + TOK, :] = jnp.transpose(kv[i, HEAD : 2 * HEAD].astype(F32)).astype(BF)

    land(kv.at[2, keys], K_Z)
    push(kv.at[2, keys], kv.at[3, keys], K_FWD, sib)
    turn_k(0)
    turn_v(0)
    don[0] = jnp.transpose(do[0].astype(F32)).astype(BF)
    qn[0] = jnp.transpose(q[0].astype(F32)).astype(BF)
    land(kv.at[1], KV_SIB)
    turn_k(1)
    turn_v(1)
    turn_k(2)
    land(kv.at[2, values], V_Z)
    push(kv.at[2, values], kv.at[3, values], V_FWD, sib)
    turn_v(2)
    land(kv.at[3, keys], K_FWD)
    turn_k(3)
    land(q.at[1:4], Q_X)
    land(kv.at[3, values], V_FWD)
    turn_v(3)
    @pl.loop(0, 4)
    def _(j):
        scores = mm(kn[...], q[j]) * SCALE
        top = jnp.max(scores, axis=0, keepdims=True)
        e = jnp.exp(scores - top)
        et[j] = e
        st[j, 0:1, :] = top
        st[j, 1:2, :] = jnp.sum(e, axis=0, keepdims=True)
        short = e.astype(BF)
        out = mm(kv[0, HEAD : 2 * HEAD, :], short[0:TOK])
        for i in range(1, 4):
            out = out + mm(kv[i, HEAD : 2 * HEAD, :], short[TOK * i : TOK * i + TOK])
        o_f[j] = out

    land(do.at[1:4], DO_X)

    @pl.loop(0, 4)
    def _(j):
        grad = mm(vn[...], do[j])
        dp[j] = grad
        st[j, 2:3, :] = jnp.sum(et[j] * grad, axis=0, keepdims=True)
        st[j, 3:8, :] = jnp.zeros((5, TOK), F32)
        for r in range(1, 4):
            push(st.at[j], st_in.at[r, (j + r) % 4], ST_X, xpeer(r))

    for j in range(1, 4):
        qn[j] = jnp.transpose(q[j].astype(F32)).astype(BF)
        don[j] = jnp.transpose(do[j].astype(F32)).astype(BF)

    @pl.loop(0, 4)
    def _(k):
        cols = pl.ds(al(384 * k, 128), 384)
        norm_n[:, cols] = jnp.transpose(norm_t[cols, :].astype(F32)).astype(BF)

    land(st_in.at[1:4], ST_X)

    factors = []
    deltas = []
    for j in range(4):
        every = [st[j]] + [st_in[r, j] for r in range(1, 4)]
        top = functools.reduce(jnp.maximum, [e[0:1] for e in every])
        norm = sum(e[1:2] * jnp.exp(e[0:1] - top) for e in every)
        log_total = jnp.log(norm) + top
        factors.append(jnp.exp(every[0][0:1] - log_total))
        deltas.append(sum(e[2:3] * jnp.exp(e[0:1] - log_total) for e in every))
    for j in range(4):
        fac[j, 0:1, :] = factors[j]
        fac[j, 1:2, :] = deltas[j]
    for r in range(1, 4):
        o_send[r] = (o_f[r] * factors[r]).astype(BF)
        push(o_send.at[r], o_in.at[4 - r], O_X, xpeer(4 - r))

    def backward(first, j):
        rows = slice(TOK * first, TOK * first + 2 * TOK)
        p = et[j, rows, :] * fac[j, 0:1, :]
        ds = (p * (dp[j, rows, :] - fac[j, 1:2, :]) * SCALE).astype(BF)
        part = mm(kv[first, 0:HEAD, :], ds[0:TOK]) + mm(kv[first + 1, 0:HEAD, :], ds[TOK : 2 * TOK])
        dk[rows, :] += mm(ds, qn[j])
        dv[rows, :] += mm(p.astype(BF), don[j])
        return part

    dk[...] = jnp.zeros_like(dk)
    dv[...] = jnp.zeros_like(dv)

    @pl.loop(0, 4)
    def _(j):
        dq_f[j] = backward(2, j)

    def key_rows(i):
        return slice(TOK * i, TOK * i + TOK)

    def pack(buf, i):
        buf[:, 0:HEAD] = dk[key_rows(i), :].astype(BF)
        buf[:, HEAD : 2 * HEAD] = dv[key_rows(i), :].astype(BF)

    pack(dkv_send.at[0], 3)
    push(dkv_send.at[0], dkv_in.at[0], DKV_FAR, sib)

    def query_block(j):
        dq_send[j] = (dq_f[j] + backward(0, j)).astype(BF)
        push(dq_send.at[j], dq_in.at[4 - j], DQ_X, xpeer(4 - j))

    query_block(2)
    land(dkv_in.at[0], DKV_FAR)
    z_send[:, 0:HEAD] = (dk[key_rows(2), :] + dkv_in[0, :, 0:HEAD].astype(F32)).astype(BF)
    z_send[:, HEAD : 2 * HEAD] = (dv[key_rows(2), :] + dkv_in[0, :, HEAD : 2 * HEAD].astype(F32)).astype(BF)
    push(z_send, z_in, DKV_Z, zpart)

    @pl.loop(0, 2)
    def _(i):
        query_block(1 + 2 * i)

    dq_f[0] = dq_f[0] + backward(0, 0)
    pack(dkv_send.at[1], 1)
    push(dkv_send.at[1], dkv_in.at[1], DKV_SIB, sib)

    def grad_w(k, grads, inputs):
        g_part[...] = mm(grads[...], inputs[...])
        g_send[k] = g_part[pl.ds(al(SHARE * (1 - c), 32), SHARE), :].astype(BF)
        g_acc[k] = g_part[pl.ds(al(SHARE * c, 32), SHARE), :].astype(BF)
        push(g_send.at[k], g_sib.at[k], G_SIB + k, sib)

    def grad_sum(k):
        land(g_sib.at[k], G_SIB + k)
        g_acc[k] = (g_acc[k].astype(F32) + g_sib[k].astype(F32)).astype(BF)

    def g_piece(k):
        return lambda buf, z, at: buf.at[k, pl.ds(al(48 * z, 16), 48), pl.ds(al(384 * at, 128), 384)]

    def c_col(buf, at):
        return buf.at[:, pl.ds(al(64 * at, 64), 64), 0:384]

    def c_row(buf, at):
        return buf.at[at, :, 384:CIN]

    def c_piece(lanes):
        return lambda buf, z, at: buf.at[z, pl.ds(al(64 * at, 64), 64), lanes]

    def a_first(src, col, into, sem):
        for r in range(1, 4):
            push(col(src, (x + r) % 4), into.at[r], sem, xpeer(r))

    def a_second(src, piece, into, part, send, into_z, sem):
        land(into.at[1:4], sem)

        def total(z):
            own = piece(src, z, x)[...].astype(F32)
            return own + sum(part(into, r, z)[...].astype(F32) for r in range(1, 4))

        send[...] = total(1 - zl).astype(BF)
        push(send, into_z, sem + 1, zpart)
        return total(zl)

    def a_third(held, piece, full, red, into_z, sem):
        land(into_z, sem + 1)
        red[...] = (held + into_z[...].astype(F32)).astype(BF)
        push(red, piece(full, zl, x), sem + 2, zpart)
        piece(full, zl, x)[...] = red[...]

    right, left = xpeer(1), xpeer(3)

    def r_first(src, piece, into, sem):
        push(piece(src, 0, (x + 2) % 4), into.at[0], sem, right)
        push(piece(src, 1, (x + 2) % 4), into.at[1], sem, left)
        push(piece(src, 1, (x + 1) % 4), into.at[3], sem + 1, right)
        push(piece(src, 0, (x + 3) % 4), into.at[4], sem + 1, left)

    def r_second(src, piece, into, send, sem):
        land(into.at[0:2], sem)
        send[0] = (piece(src, 0, (x + 1) % 4)[...].astype(F32) + into[0].astype(F32)).astype(BF)
        send[1] = (piece(src, 1, (x + 3) % 4)[...].astype(F32) + into[1].astype(F32)).astype(BF)
        push(send.at[0], into.at[2], sem + 1, right)
        push(send.at[1], into.at[5], sem + 1, left)

    def r_third(src, piece, into, send, into_z, sem):
        land(into.at[2:6], sem + 1)

        def total(z):
            own = piece(src, z, x)[...].astype(F32)
            return own + into[2 + z].astype(F32) + into[4 + z].astype(F32)

        send[...] = total(1 - zl).astype(BF)
        push(send, into_z, sem + 2, zpart)
        return total(zl)

    def r_fourth(held, piece, full, red, into_z, sem):
        land(into_z, sem + 2)
        red[...] = (held + into_z[...].astype(F32)).astype(BF)
        push(red, piece(full, zl, x), sem + 3, zpart)
        for dev in (right, left):
            push(red, piece(full, zl, x), sem + 4, dev)
        piece(full, zl, x)[...] = red[...]

    def s_fourth(held, piece, full, red, into_z, sem):
        land(into_z, sem + 2)
        red[...] = (held + into_z[...].astype(F32)).astype(BF)
        for r in range(1, 4):
            push(red, piece(full, zl, x), sem + 3, xpeer(r))
        piece(full, zl, x)[...] = red[...]

    def s_fifth(row, full, into, sem):
        land(into.at[0:3], sem + 3)
        push(row(full, zl), row(full, zl), sem + 4, zpart)

    def g_row(k):
        return lambda buf, at: buf.at[k, pl.ds(al(48 * at, 16), 48), :]

    def r_fifth(piece, full, red, sem):
        land(red, sem + 3)
        for dev in (right, left):
            push(piece(full, 1 - zl, x), piece(full, 1 - zl, x), sem + 4, dev)

    def r_sixth(piece, full, into, sem):
        land(into.at[0:4], sem + 4)
        push(piece(full, 0, (x + 3) % 4), piece(full, 0, (x + 3) % 4), sem + 5, right)
        push(piece(full, 1, (x + 1) % 4), piece(full, 1, (x + 1) % 4), sem + 5, left)

    def a_fourth(col, full, red, sem):
        land(red, sem + 2)
        for r in range(1, 4):
            push(col(full, x), col(full, x), sem + 3, xpeer(r))

    def b_first(src, row, into_z, sem):
        push(row(src, 1 - zl), into_z, sem, zpart)

    def b_second(src, row, part, held, into_z, into, sem):
        land(into_z, sem)
        held[...] = (row(src, zl)[...].astype(F32) + into_z[...].astype(F32)).astype(BF)
        for r in range(1, 4):
            push(part(held, (x + r) % 4), into.at[r], sem + 1, xpeer(r))

    def b_third(part, piece, full, held, into, red, sem):
        land(into.at[1:4], sem + 1)
        red[...] = (part(held, x)[...].astype(F32) + sum(into[r].astype(F32) for r in range(1, 4))).astype(BF)
        for r in range(1, 4):
            push(red, piece(full, zl, x), sem + 2, xpeer(r))
        piece(full, zl, x)[...] = red[...]

    def b_fourth(row, full, into, sem):
        land(into.at[1:4], sem + 2)
        push(row(full, zl), row(full, zl), sem + 3, zpart)

    def ca_part(buf, r, z):
        return buf.at[r, z]

    def cb_part(buf, at):
        return buf.at[pl.ds(al(64 * at, 64), 64)]

    def reduced(into, base):
        land(into.at[1:16], base)
        same = sum(into[r].astype(F32) for r in range(0, 16, 2))
        other = sum(into[r].astype(F32) for r in range(1, 16, 2))
        first = jnp.where(c == 0, same, other)
        second = jnp.where(c == 0, other, same)
        return first, second

    land(o_in.at[1:4], O_X)
    ot[...] = (o_f[0] * factors[0] + sum(o_in[r].astype(F32) for r in range(1, 4))).astype(BF)

    @pl.loop(0, 4)
    def _(k):
        cols = pl.ds(al(384 * k, 128), 384)
        cot_n[:, cols] = jnp.transpose(cot_t[cols, :].astype(F32)).astype(BF)

    grad_w(3, ot, cot_n)


    land(dkv_in.at[1], DKV_SIB)
    land(z_in, DKV_Z)
    grad_k = dk[key_rows(0), :] + (dkv_in[1, :, 0:HEAD].astype(F32) + z_in[:, 0:HEAD].astype(F32))
    grad_v = dv[key_rows(0), :] + (dkv_in[1, :, HEAD : 2 * HEAD].astype(F32) + z_in[:, HEAD : 2 * HEAD].astype(F32))
    dqkv[HEAD : 2 * HEAD, :] = jnp.transpose(grad_k).astype(BF)
    dqkv[2 * HEAD : 3 * HEAD, :] = jnp.transpose(grad_v).astype(BF)
    land(dq_in.at[1:4], DQ_X)
    grad_q = dq_f[0] + sum(dq_in[r].astype(F32) for r in range(1, 4))
    dqkv[0:HEAD, :] = grad_q.astype(BF)

    row_stat = jnp.sum(dqkv[0:HEAD, :].astype(F32) * q[0].astype(F32), axis=0, keepdims=True)
    row_stat = row_stat + jnp.sum(dqkv[HEAD:, :].astype(F32) * kv[0].astype(F32), axis=0, keepdims=True)
    wide_stat[0:1, :] = row_stat * (1.0 / D)

    def scatter_rows(k):
        cols = pl.ds(al(384 * k, 128), 384)
        inverse = wide_stat[1:2, :]
        unit = tok_t[cols, :].astype(F32) * inverse
        n_send[cols, :] = (inverse * (mm(w_t[cols, :], dqkv[...]) - unit * wide_stat[0:1, :])).astype(BF)

    @pl.loop(0, 4)
    def _(k):
        scatter_rows(k)

    for step in around:
        peer = around_mp(step)
        slot = step[0] * 8 + step[1] * 2 + step[2]
        piece = n_send.at[pl.ds(al(SHARE * peer, 32), SHARE)]
        if step in relayed:
            push(piece, via_n.at[relayed.index(step)], VIA_N, at_z(z_down, y, c))
        else:
            push(piece, n_in.at[slot], NORM_RS, (s, peer))
    n_in[0] = n_send[mine, :]

    grad_sum(3)
    r_first(g_acc, g_piece(3), gr_in.at[3], G_STEP + 18)

    for k in range(3):
        grad_w(k, dqkv.at[HEAD * k : HEAD * k + HEAD], norm_n)
    land(via_n, VIA_N)
    for i, step in enumerate(relayed):
        push(via_n.at[i], n_in.at[step[0] * 8 + step[1] * 2 + step[2]], NORM_RS, far_end(step))
    for k in range(3):
        grad_sum(k)
        r_first(g_acc, g_piece(k), gr_in.at[k], G_STEP + 6 * k)
    @pl.loop(0, 4)
    def _(k):
        cols = pl.ds(al(384 * k, 128), 384)
        a_send[k // 2, pl.ds(al(384 * (k % 2), 128), 384), :] = mm(wo_t[cols, :], ot[...]).astype(BF)

    held = {}
    order = (3, 0, 1, 2)
    for k in order:
        r_second(g_acc, g_piece(k), gr_in.at[k], gr_send.at[k], G_STEP + 6 * k)
    first, second = reduced(n_in, NORM_RS)
    for r in range(1, 4):
        rows = pl.ds(al(HEAD * ((y + r) % 4), 64), HEAD)
        push(a_send.at[:, rows], ay_in.at[r], OUT_Y, (s, zh * 8 + ((y + r) % 4) * 2 + c))
    tok_grad = cot_own[...].astype(F32) + jnp.concatenate([first, second], axis=1)
    pad = jnp.zeros((SHARE, WIDE - PAIRS), F32)
    for half in range(2):
        pg = jnp.concatenate([0.5 * tok_grad * slope[half], pad], axis=1)
        for d in range(3):
            shift = (WIDE - 1, 0, 1)[d]
            moved = pltpu.roll(pg, shift, 1) if shift else pg
            row = SHARE * (2 * d + half)
            pgs[row : row + SHARE, :] = moved.astype(BF)
    both = pgs[2 * SHARE : 3 * SHARE, 0:PAIRS], pgs[3 * SHARE : 4 * SHARE, 0:PAIRS]
    ones = jnp.ones((16, PAIRS), BF)
    bias = nt(ones, both[0]) + nt(ones, both[1])
    c_send[1, 224:256, :] = jnp.zeros((32, CIN), BF)
    c_send[1, 224:240, 0:SHARE] = bias.astype(BF)

    @pl.loop(0, 3)
    def _(k):
        cols = pl.ds(al(256 * k, 256), 256)
        odd_cols = pl.ds(al(CIN + 256 * k, 256), 256)
        me = mm(pgs[...], xe[:, cols])
        mo = mm(pgs[...], xe[:, odd_cols])

        def part(arr, d, half):
            row = SHARE * (2 * (d + 1) + half)
            return arr[row : row + SHARE]

        taps = (
            part(me, -1, 0) + part(mo, -1, 1),
            part(mo, -1, 0) + part(me, 0, 1),
            part(me, 0, 0) + part(mo, 0, 1),
            part(mo, 0, 0) + part(me, 1, 1),
            part(me, 1, 0) + part(mo, 1, 1),
        )
        for t in range(TAPS):
            tap = taps[t].astype(BF)
            if t < 2:
                c_send[0, SHARE * t : SHARE * t + SHARE, cols] = tap
            elif t == 2:
                c_send[0, 192:256, cols] = tap[0:64]
                c_send[1, 0:32, cols] = tap[64:96]
            else:
                c_send[1, SHARE * t - 256 : SHARE * t - 160, cols] = tap

    low, high = slice(0, 384), slice(384, CIN)
    a_first(c_send, c_col, cx_in, C_STEP)
    b_first(c_send, c_row, cbz_in, C_STEP + 4)

    for k in order:
        held[k] = r_third(g_acc, g_piece(k), gr_in.at[k], gz_send.at[k], gz_in.at[k], G_STEP + 6 * k)
    held_c = a_second(c_send, c_piece(low), cx_in, ca_part, cz_send, cz_in, C_STEP)
    b_second(c_send, c_row, cb_part, cb_held, cbz_in, cx_b, C_STEP + 4)
    for k in order:
        fourth = r_fourth if k in (0, 3) else s_fourth
        fourth(held[k], g_piece(k), g_all, g_red.at[k], gz_in.at[k], G_STEP + 6 * k)
    a_third(held_c, c_piece(low), c_all, c_red.at[0], cz_in, C_STEP)
    b_third(cb_part, c_piece(high), c_all, cb_held, cx_b, c_red.at[1], C_STEP + 4)
    land(ay_in.at[1:4], OUT_Y)
    rows = pl.ds(al(HEAD * y, 64), HEAD)

    def over_y(z):
        return a_send[z, rows, :].astype(F32) + sum(ay_in[r, z].astype(F32) for r in range(1, 4))

    az_send[...] = over_y(1 - zh).astype(BF)
    push(az_send, az_in, OUT_Z, (s, (m + 8) % 16))
    az_own[...] = over_y(zh)
    for k in (3, 0):
        r_fifth(g_piece(k), g_all, g_red.at[k], G_STEP + 6 * k)
    a_fourth(c_col, c_all, c_red.at[0], C_STEP)
    b_fourth(c_row, c_all, cx_b, C_STEP + 4)
    for k in (1, 2):
        s_fifth(g_row(k), g_all, gr_in.at[k], G_STEP + 6 * k)
    for k in (3, 0):
        r_sixth(g_piece(k), g_all, gr_in.at[k], G_STEP + 6 * k)

    land(az_in, OUT_Z)
    az_own[...] = az_own[...] + az_in[...].astype(F32)
    as_send[...] = az_own[pl.ds(al(SHARE * (1 - c), 32), SHARE), :].astype(BF)
    push(as_send, as_in, OUT_SIB, sib)
    own = az_own[pl.ds(al(SHARE * c, 32), SHARE), :]
    land(as_in, OUT_SIB)
    other = as_in[...].astype(F32)
    out = jnp.concatenate([jnp.where(c == 0, own, other), jnp.where(c == 0, other, own)], axis=1)
    o_layer[...] = (out + tok_own[...].astype(F32)).astype(BF)

    for k in (3, 0):
        land(gr_in.at[k, 0:2], G_STEP + 6 * k + 5)
    for k in (1, 2):
        land(gr_in.at[k, 0:4], G_STEP + 6 * k + 4)
    land(cx_in.at[1:4], C_STEP + 3)
    land(cbz_in, C_STEP + 7)
    for copy in sent.values():
        copy.wait_send()


def scratch():
    def v(*shape, dtype=BF):
        return pltpu.VMEM(shape, dtype)

    return [
        v(1024, CIN), v(PAIRS, 128, dtype=jnp.int32), v(TAPS, SHARE, CIN), v(D, 3 * HEAD), v(D, HEAD),
        v(2, 1024, 128, dtype=F32), v(32, D, dtype=F32), v(WIDE, D), v(2, 16, D), v(576, D), v(768, D),
        v(576, WIDE, dtype=F32), v(2, SHARE, PAIRS, dtype=F32), v(SHARE, PAIRS), v(SHARE, PAIRS),
        v(D, TOK), v(D, TOK), v(D, TOK),
        v(4, HEAD, TOK), v(4, 384, TOK), v(1024, HEAD), v(1024, HEAD), v(4, HEAD, TOK),
        v(4, 1024, TOK, dtype=F32), v(4, 1024, TOK, dtype=F32),
        v(4, 8, TOK, dtype=F32), v(4, 4, 8, TOK, dtype=F32),
        v(4, HEAD, TOK, dtype=F32), v(4, HEAD, TOK), v(4, HEAD, TOK), v(HEAD, TOK),
        v(4, 8, TOK, dtype=F32),
        v(4, HEAD, TOK, dtype=F32), v(4, HEAD, TOK), v(4, HEAD, TOK),
        v(1024, HEAD, dtype=F32), v(1024, HEAD, dtype=F32), v(4, TOK, HEAD), v(4, TOK, HEAD), v(TOK, D), v(TOK, D), v(8, TOK, dtype=F32),
        v(2, TOK, 384), v(2, TOK, 384), v(TOK, 384), v(TOK, 384),
        v(576, TOK),
        v(D, TOK), v(16, SHARE, TOK),
        v(2, 768, TOK), v(4, 2, HEAD, TOK), v(HEAD, TOK), v(HEAD, TOK), v(HEAD, TOK, dtype=F32), v(SHARE, TOK), v(SHARE, TOK),
        v(HEAD, D, dtype=F32), v(4, SHARE, D), v(4, SHARE, D), v(4, SHARE, D),
        v(4, 6, 48, 384), v(4, 2, 48, 384), v(4, 48, 384), v(4, 48, 384), v(4, 48, 384),
        v(576, WIDE), v(2, 256, CIN),
        v(4, 2, 64, 384), v(64, 384), v(64, 384), v(256, 384), v(256, 384), v(4, 64, 384), v(2, 64, 384),
        v(4, SHARE, TOK), v(4, SHARE, TOK), v(4, SHARE, TOK),
        pltpu.SemaphoreType.DMA((SEMS,)), pltpu.SemaphoreType.DMA((SEMS,)), pltpu.SemaphoreType.DMA((8,)),
    ]


def widen(layer, conv, grads, o_layer, o_conv, o_bias, o_q, o_k, o_v, o_o, cin, gin, cout, gout, lsem, osem):
    loads = [pltpu.make_async_copy(grads.at[k], gin.at[k], lsem.at[k]) for k in range(4)]
    loads.append(pltpu.make_async_copy(conv, cin, lsem.at[4]))
    for load in loads:
        load.start()
    through = pltpu.make_async_copy(layer, o_layer, lsem.at[5])
    through.start()
    stores = [through]
    for k, o in enumerate((o_q, o_k, o_v, o_o)):
        loads[k].wait()
        gout[k] = gin[k].astype(F32)
        stores.append(pltpu.make_async_copy(gout.at[k], o, osem.at[k]))
        stores[-1].start()
    loads[4].wait()
    for t in range(TAPS):
        cout[t] = cin[SHARE * t : SHARE * t + SHARE, :].astype(F32)
        stores.append(pltpu.make_async_copy(cout.at[t], o_conv.at[t], osem.at[4 + t]))
        stores[-1].start()
    o_bias[...] = cin[TAPS * SHARE : TAPS * SHARE + 16, 0:SHARE].astype(F32)[0:1]
    for store in stores:
        store.wait()


def body(features, base_tokens, base_proj, conv_weight, conv_bias, w_query, w_key, w_value, w_out, cotangent):
    vmem = pl.BlockSpec(memory_space=pltpu.VMEM)
    hbm = pl.BlockSpec(memory_space=pl.ANY)
    layer = jax.ShapeDtypeStruct((SHARE, PAIRS), BF)
    narrow = pl.pallas_call(
        kernel,
        out_shape=(layer, jax.ShapeDtypeStruct((2, 256, CIN), BF), jax.ShapeDtypeStruct((4, SHARE, D), BF)),
        in_specs=[hbm, hbm, vmem, hbm, vmem, hbm, hbm, hbm, hbm, hbm],
        out_specs=(vmem,) * 3,
        scratch_shapes=scratch(),
        compiler_params=pltpu.CompilerParams(
            collective_id=0, has_side_effects=True, vmem_limit_bytes=60 * 1024 * 1024
        ),
        cost_estimate=pl.CostEstimate(flops=8_000_000_000, bytes_accessed=8_000_000, transcendentals=1_300_000),
        name="section",
    )(
        features, base_tokens.reshape(PAIRS, 128), base_proj, conv_weight, conv_bias.reshape(1, SHARE),
        w_query, w_key, w_value, w_out, cotangent.T,
    )
    square = jax.ShapeDtypeStruct((SHARE, D), F32)
    layer, conv, bias, gq, gk, gv, go = pl.pallas_call(
        widen,
        out_shape=(
            layer, jax.ShapeDtypeStruct((TAPS, SHARE, CIN), F32), jax.ShapeDtypeStruct((1, SHARE), F32),
            square, square, square, square,
        ),
        in_specs=[hbm] * 3,
        out_specs=(hbm, hbm, vmem, hbm, hbm, hbm, hbm),
        scratch_shapes=[
            pltpu.VMEM((512, CIN), BF), pltpu.VMEM((4, SHARE, D), BF),
            pltpu.VMEM((TAPS, SHARE, CIN), F32), pltpu.VMEM((4, SHARE, D), F32),
            pltpu.SemaphoreType.DMA((6,)), pltpu.SemaphoreType.DMA((9,)),
        ],
        compiler_params=pltpu.CompilerParams(vmem_limit_bytes=60 * 1024 * 1024),
        name="widen",
    )(narrow[0], narrow[1].reshape(512, CIN), narrow[2])
    return layer.T, conv, bias.reshape(SHARE), gq, gk, gv, go


def solution(mesh):
    placed = (
        P("seq", None), P("seq"), P(), P(None, "mp", None), P("mp"),
        P("mp", None), P("mp", None), P("mp", None), P("mp", None), P("seq", "mp"),
    )
    return jax.shard_map(
        body,
        mesh=mesh,
        in_specs=placed,
        out_specs=(
            P("seq", "mp"), P(None, "mp", None), P("mp"),
            P("mp", None), P("mp", None), P("mp", None), P("mp", None),
        ),
        check_vma=False,
    )
```

```python
import functools

import jax
import jax.numpy as jnp
from jax import lax
from jax.experimental import pallas as pl
from jax.experimental.pallas import tpu as pltpu
from jax.sharding import PartitionSpec as P

D = 1536
CIN = 768
TAPS = 5
BIN_WIDTH = 64
EPS = 1e-06
HEAD = 192
SHARE = 96
TOK = 256
PAIRS = 512
WIDE = 640
BF = jnp.bfloat16
F32 = jnp.float32
MESH = pl.DeviceIdType.MESH
SCALE = HEAD ** (-0.5)
ROOT2PI = 0.7978845608028654

(
    COT_AG, TOK_AG, W_SIB, HALO, Q_X, DO_X, ST_X, O_X, DQ_X, K_Z, V_Z, KV_SIB, K_FWD, V_FWD, DKV_FAR, DKV_SIB, DKV_Z,
    OUT_Y, OUT_Z, OUT_SIB, NORM_RS,
) = range(21)
G_SIB = 21
G_STEP = G_SIB + 4
C_STEP = G_STEP + 24
SEMS = C_STEP + 8


def mm(a, b):
    return jnp.dot(a, b, preferred_element_type=F32)


def nt(a, b):
    return lax.dot_general(a, b, (((1,), (1,)), ((), ())), preferred_element_type=F32)


def tn(a, b):
    return lax.dot_general(a, b, (((0,), (0,)), ((), ())), preferred_element_type=F32)


def kernel(
    feat_hbm, toks_hbm, bproj, cw_hbm, cbias, wq, wk, wv, wo, cot_hbm,
    o_layer, c_all, g_all,
    feat, toks, cw, w_t, wo_t, xf, r3, xe, halo, wt, w4, z, slope, tok_own, cot_own, tok_t, cot_t, norm_t,
    q, kv, kn, vn, do, et, dp, st, st_in, o_f, o_send, o_in, ot, fac,
    dq_f, dq_send, dq_in, dk, dv, qn, don, norm_n, cot_n, wide_stat, dkv_send, dkv_in, z_send, z_in, dqkv,
    n_send, n_in, a_send, ay_in, az_send, az_in, az_own, as_send, as_in,
    g_part, g_send, g_sib, g_acc, gr_in, gr_send, gz_send, gz_in, g_red,
    pgs, c_send, cx_in, cz_send, cz_in, cbz_in, cb_held, cx_b, c_red, ssem, rsem, lsem,
):
    s = lax.axis_index("seq")
    m = lax.axis_index("mp")
    zl = s // 4
    x = s % 4
    c = m % 2
    sib = (s, m + 1 - 2 * c)
    zpart = ((1 - zl) * 4 + x, m)
    sent = {}

    def xpeer(r):
        return (zl * 4 + (x + r) % 4, m)

    def seqpeer(r):
        return ((s + r) % 8, m)

    def mppeer(r):
        return (s, (m + r) % 16)

    def push(src, dst, sem, dev):
        pltpu.make_async_remote_copy(
            src_ref=src, dst_ref=dst, send_sem=ssem.at[sem], recv_sem=rsem.at[sem],
            device_id=dev, device_id_type=MESH,
        ).start()

    def land(whole, sem):
        copy = pltpu.make_async_remote_copy(
            src_ref=whole, dst_ref=whole, send_sem=ssem.at[sem], recv_sem=rsem.at[sem],
            device_id=sib, device_id_type=MESH,
        )
        copy.wait_recv()
        sent[sem] = copy

    def al(v, n):
        return pl.multiple_of(v, n)

    barrier = pltpu.get_barrier_semaphore()
    for r in range(1, 16):
        pl.semaphore_signal(barrier, inc=1, device_id=mppeer(r), device_id_type=MESH)
    for r in range(1, 8):
        pl.semaphore_signal(barrier, inc=1, device_id=seqpeer(r), device_id_type=MESH)

    loads = [
        pltpu.make_async_copy(toks_hbm, toks, lsem.at[0]),
        pltpu.make_async_copy(feat_hbm, feat, lsem.at[1]),
        pltpu.make_async_copy(cw_hbm, cw, lsem.at[2]),
        pltpu.make_async_copy(cot_hbm, cot_own, lsem.at[3]),
    ]
    for k, w in enumerate((wq, wk, wv, wo)):
        rows = pl.ds(al(HEAD * k + SHARE * c, 32), SHARE)
        loads.append(pltpu.make_async_copy(w, w4.at[rows], lsem.at[4 + k]))
    for load in loads:
        load.start()
    mine = pl.ds(al(SHARE * m, 32), SHARE)

    y = (m // 2) % 4
    zh = m // 8
    around = (
        (1, 0, 0), (0, 1, 0), (0, 3, 0), (1, 2, 0), (0, 2, 1), (1, 1, 1), (1, 3, 1), (1, 0, 1),
        (0, 1, 1), (0, 3, 1), (1, 2, 1), (0, 2, 0), (1, 1, 0), (1, 3, 0), (0, 0, 1),
    )

    def around_mp(step):
        dz, dy, dc = step
        return ((zh + dz) % 2) * 8 + ((y + dy) % 4) * 2 + (c + dc) % 2

    def spread(own, full, base, steps=around):
        for step in steps:
            cols = pl.ds(al(TOK * ((c + step[2]) % 2), TOK), TOK)
            push(own.at[:, cols], full.at[mine], base, (s, around_mp(step)))

    def keep(own, full):
        full[mine, :] = own[:, pl.ds(al(TOK * c, TOK), TOK)]

    def gathered(full, base):
        land(full.at[0 : 15 * SHARE], base)

    pl.semaphore_wait(barrier, 22)
    spread(cot_hbm, cot_t, COT_AG, around[:9])
    for k, w in enumerate((wo, wq, wk, wv)):
        rows = pl.ds(al(HEAD * ((k + 3) % 4) + SHARE * c, 32), SHARE)
        push(w, w4.at[rows], W_SIB, sib)

    bp = bproj[...]
    hi = bp.astype(BF).astype(F32)
    mid = (bp - hi).astype(BF).astype(F32)
    low = (bp - hi - mid).astype(BF).astype(F32)
    r3[...] = jnp.zeros_like(r3)
    for k, part in enumerate((hi, mid, low)):
        r3[8 * k : 8 * k + 4, 0:CIN] = part
        r3[8 * k + 4 : 8 * k + 8, CIN:D] = part
    lane = lax.broadcasted_iota(jnp.int32, (128, 32), 0)
    col = lax.broadcasted_iota(jnp.int32, (128, 32), 1)
    group = jnp.where(lane >= BIN_WIDTH, 4, 0)
    counts = jnp.zeros((PAIRS, 32), F32)
    loads[0].wait()
    for b in range(4):
        pick = jnp.where((col < 24) & (col % 8 == group + b), 1.0, 0.0).astype(BF)
        match = jnp.where(toks[...] == b, 1.0, 0.0).astype(BF)
        counts = counts + mm(match, pick)
    comp = (counts * (1.0 / BIN_WIDTH)).astype(BF)
    loads[1].wait()
    for k in range(0, 6, 2):
        for i in range(2):
            xf[i] = feat[:, 128 * (k + i) : 128 * (k + i) + 128].astype(F32)
        for half in range(2):
            lo = CIN * half + 128 * k
            extra = mm(comp, r3[:, lo : lo + 256].astype(BF))
            for i in range(2):
                own = xf[i, pl.ds(half, PAIRS, stride=2), :]
                xe[0:PAIRS, lo + 128 * i : lo + 128 * i + 128] = (own + extra[:, 128 * i : 128 * i + 128]).astype(BF)

    push(xe.at[pl.ds(PAIRS - 16, 16)], halo.at[0], HALO, seqpeer(1))
    push(xe.at[pl.ds(0, 16)], halo.at[1], HALO, seqpeer(7))
    loads[2].wait()
    zero = jnp.zeros((SHARE, CIN), BF)
    left = (cw[0], zero, cw[2], cw[1], cw[4], cw[3])
    right = (cw[1], cw[0], cw[3], cw[2], zero, cw[4])
    for g in range(6):
        wt[SHARE * g : SHARE * g + SHARE, 0:CIN] = left[g]
        wt[SHARE * g : SHARE * g + SHARE, CIN:D] = right[g]

    @pl.loop(0, 2)
    def _(i):
        rows = pl.ds(al(i * 256, 256), 256)
        z[:, rows] = nt(wt[...], xe[rows, :])

    land(halo, HALO)
    at = lax.broadcasted_iota(jnp.int32, (16, D), 0)
    after = halo[1].astype(F32)
    before = halo[0].astype(F32)
    after = jnp.where((at == 0) & (s < 7), after, 0.0)
    before = jnp.where((at == 15) & (s > 0), before, 0.0)
    xe[PAIRS:WIDE, :] = jnp.zeros((WIDE - PAIRS, D), BF)
    xe[PAIRS : PAIRS + 16, :] = after.astype(BF)
    xe[WIDE - 16 : WIDE, :] = before.astype(BF)
    z[:, PAIRS:WIDE] = nt(wt[...], xe[PAIRS:WIDE, :])

    offset = jnp.transpose(jnp.broadcast_to(cbias[...], (128, SHARE)))[:, 0:1]
    total = jnp.zeros((SHARE, PAIRS), F32)
    for half in range(2):
        r0, r1, r2 = (SHARE * (2 * d + half) for d in range(3))
        pre = pltpu.roll(z[r0 : r0 + SHARE, :], 1, 1)[:, 0:PAIRS]
        pre = pre + z[r1 : r1 + SHARE, 0:PAIRS]
        pre = pre + pltpu.roll(z[r2 : r2 + SHARE, :], WIDE - 1, 1)[:, 0:PAIRS]
        pre = pre + offset
        square = pre * pre
        bend = jnp.tanh(ROOT2PI * (pre + 0.044715 * (square * pre)))
        total = total + pre * (0.5 * (1.0 + bend))
        slope[half] = 0.5 * (1.0 + bend) + (0.5 * pre) * (1.0 - bend * bend) * (
            ROOT2PI * (1.0 + (3.0 * 0.044715) * square)
        )
    tok_own[...] = (0.5 * total).astype(BF)
    spread(tok_own, tok_t, TOK_AG)
    spread(cot_hbm, cot_t, COT_AG, around[9:])
    keep(tok_own, tok_t)
    for load in loads[3:]:
        load.wait()
    land(w4.at[0 : 4 * SHARE], W_SIB)

    @pl.loop(0, 4)
    def _(k):
        cols = pl.ds(al(384 * k, 128), 384)
        w_t[cols, :] = jnp.transpose(w4[0 : 3 * HEAD, cols].astype(F32)).astype(BF)
        wo_t[cols, :] = jnp.transpose(w4[3 * HEAD : 4 * HEAD, cols].astype(F32)).astype(BF)

    gathered(tok_t, TOK_AG)
    wide = tok_t[...].astype(F32)
    inverse = lax.rsqrt(jnp.sum(wide * wide, axis=0, keepdims=True) * (1.0 / D) + EPS)
    wide_stat[1:2, :] = inverse
    norm_t[...] = (wide * inverse).astype(BF)
    kv[0, 0:HEAD] = mm(w4[HEAD : 2 * HEAD, :], norm_t[...]).astype(BF)
    keys, values = slice(0, HEAD), slice(HEAD, 2 * HEAD)
    push(kv.at[0, keys], kv.at[2, keys], K_Z, zpart)
    push(kv.at[0, keys], kv.at[1, keys], KV_SIB, sib)
    q[0] = mm(w4[0:HEAD, :], norm_t[...]).astype(BF)
    for r in range(1, 4):
        push(q.at[0], q.at[r], Q_X, xpeer(r))
    kv[0, HEAD : 2 * HEAD] = mm(w4[2 * HEAD : 3 * HEAD, :], norm_t[...]).astype(BF)
    push(kv.at[0, values], kv.at[2, values], V_Z, zpart)
    push(kv.at[0, values], kv.at[1, values], KV_SIB, sib)
    keep(cot_own, cot_t)
    gathered(cot_t, COT_AG)
    do[0] = mm(w4[3 * HEAD : 4 * HEAD, :], cot_t[...]).astype(BF)
    for r in range(1, 4):
        push(do.at[0], do.at[r], DO_X, xpeer(r))

    def turn_k(i):
        kn[TOK * i : TOK * i + TOK, :] = jnp.transpose(kv[i, 0:HEAD].astype(F32)).astype(BF)

    def turn_v(i):
        vn[TOK * i : TOK * i + TOK, :] = jnp.transpose(kv[i, HEAD : 2 * HEAD].astype(F32)).astype(BF)

    land(kv.at[2, keys], K_Z)
    push(kv.at[2, keys], kv.at[3, keys], K_FWD, sib)
    turn_k(0)
    turn_v(0)
    don[0] = jnp.transpose(do[0].astype(F32)).astype(BF)
    qn[0] = jnp.transpose(q[0].astype(F32)).astype(BF)
    land(kv.at[1], KV_SIB)
    turn_k(1)
    turn_v(1)
    turn_k(2)
    land(kv.at[2, values], V_Z)
    push(kv.at[2, values], kv.at[3, values], V_FWD, sib)
    turn_v(2)
    land(kv.at[3, keys], K_FWD)
    turn_k(3)
    land(q.at[1:4], Q_X)
    land(kv.at[3, values], V_FWD)
    turn_v(3)
    @pl.loop(0, 4)
    def _(j):
        scores = mm(kn[...], q[j]) * SCALE
        top = jnp.max(scores, axis=0, keepdims=True)
        e = jnp.exp(scores - top)
        et[j] = e
        st[j, 0:1, :] = top
        st[j, 1:2, :] = jnp.sum(e, axis=0, keepdims=True)
        short = e.astype(BF)
        out = mm(kv[0, HEAD : 2 * HEAD, :], short[0:TOK])
        for i in range(1, 4):
            out = out + mm(kv[i, HEAD : 2 * HEAD, :], short[TOK * i : TOK * i + TOK])
        o_f[j] = out

    land(do.at[1:4], DO_X)

    @pl.loop(0, 4)
    def _(j):
        grad = mm(vn[...], do[j])
        dp[j] = grad
        st[j, 2:3, :] = jnp.sum(et[j] * grad, axis=0, keepdims=True)
        st[j, 3:8, :] = jnp.zeros((5, TOK), F32)
        for r in range(1, 4):
            push(st.at[j], st_in.at[r, (j + r) % 4], ST_X, xpeer(r))

    for j in range(1, 4):
        qn[j] = jnp.transpose(q[j].astype(F32)).astype(BF)
        don[j] = jnp.transpose(do[j].astype(F32)).astype(BF)

    @pl.loop(0, 4)
    def _(k):
        cols = pl.ds(al(384 * k, 128), 384)
        norm_n[:, cols] = jnp.transpose(norm_t[cols, :].astype(F32)).astype(BF)

    land(st_in.at[1:4], ST_X)

    factors = []
    deltas = []
    for j in range(4):
        every = [st[j]] + [st_in[r, j] for r in range(1, 4)]
        top = functools.reduce(jnp.maximum, [e[0:1] for e in every])
        norm = sum(e[1:2] * jnp.exp(e[0:1] - top) for e in every)
        log_total = jnp.log(norm) + top
        factors.append(jnp.exp(every[0][0:1] - log_total))
        deltas.append(sum(e[2:3] * jnp.exp(e[0:1] - log_total) for e in every))
    for j in range(4):
        fac[j, 0:1, :] = factors[j]
        fac[j, 1:2, :] = deltas[j]
    for r in range(1, 4):
        o_send[r] = (o_f[r] * factors[r]).astype(BF)
        push(o_send.at[r], o_in.at[4 - r], O_X, xpeer(4 - r))

    def backward(first, j):
        rows = slice(TOK * first, TOK * first + 2 * TOK)
        p = et[j, rows, :] * fac[j, 0:1, :]
        ds = (p * (dp[j, rows, :] - fac[j, 1:2, :]) * SCALE).astype(BF)
        part = mm(kv[first, 0:HEAD, :], ds[0:TOK]) + mm(kv[first + 1, 0:HEAD, :], ds[TOK : 2 * TOK])
        dk[rows, :] += mm(ds, qn[j])
        dv[rows, :] += mm(p.astype(BF), don[j])
        return part

    dk[...] = jnp.zeros_like(dk)
    dv[...] = jnp.zeros_like(dv)

    @pl.loop(0, 4)
    def _(j):
        dq_f[j] = backward(2, j)

    def key_rows(i):
        return slice(TOK * i, TOK * i + TOK)

    def pack(buf, i):
        buf[:, 0:HEAD] = dk[key_rows(i), :].astype(BF)
        buf[:, HEAD : 2 * HEAD] = dv[key_rows(i), :].astype(BF)

    pack(dkv_send.at[0], 3)
    push(dkv_send.at[0], dkv_in.at[0], DKV_FAR, sib)

    def query_block(j):
        dq_send[j] = (dq_f[j] + backward(0, j)).astype(BF)
        push(dq_send.at[j], dq_in.at[4 - j], DQ_X, xpeer(4 - j))

    query_block(2)
    land(dkv_in.at[0], DKV_FAR)
    z_send[:, 0:HEAD] = (dk[key_rows(2), :] + dkv_in[0, :, 0:HEAD].astype(F32)).astype(BF)
    z_send[:, HEAD : 2 * HEAD] = (dv[key_rows(2), :] + dkv_in[0, :, HEAD : 2 * HEAD].astype(F32)).astype(BF)
    push(z_send, z_in, DKV_Z, zpart)

    @pl.loop(0, 2)
    def _(i):
        query_block(1 + 2 * i)

    dq_f[0] = dq_f[0] + backward(0, 0)
    pack(dkv_send.at[1], 1)
    push(dkv_send.at[1], dkv_in.at[1], DKV_SIB, sib)

    def grad_w(k, grads, inputs):
        g_part[...] = mm(grads[...], inputs[...])
        g_send[k] = g_part[pl.ds(al(SHARE * (1 - c), 32), SHARE), :].astype(BF)
        g_acc[k] = g_part[pl.ds(al(SHARE * c, 32), SHARE), :].astype(BF)
        push(g_send.at[k], g_sib.at[k], G_SIB + k, sib)

    def grad_sum(k):
        land(g_sib.at[k], G_SIB + k)
        g_acc[k] = (g_acc[k].astype(F32) + g_sib[k].astype(F32)).astype(BF)

    def g_piece(k):
        return lambda buf, z, at: buf.at[k, pl.ds(al(48 * z, 16), 48), pl.ds(al(384 * at, 128), 384)]

    def c_col(buf, at):
        return buf.at[:, pl.ds(al(64 * at, 64), 64), 0:384]

    def c_row(buf, at):
        return buf.at[at, :, 384:CIN]

    def c_piece(lanes):
        return lambda buf, z, at: buf.at[z, pl.ds(al(64 * at, 64), 64), lanes]

    def a_first(src, col, into, sem):
        for r in range(1, 4):
            push(col(src, (x + r) % 4), into.at[r], sem, xpeer(r))

    def a_second(src, piece, into, part, send, into_z, sem):
        land(into.at[1:4], sem)

        def total(z):
            own = piece(src, z, x)[...].astype(F32)
            return own + sum(part(into, r, z)[...].astype(F32) for r in range(1, 4))

        send[...] = total(1 - zl).astype(BF)
        push(send, into_z, sem + 1, zpart)
        return total(zl)

    def a_third(held, piece, full, red, into_z, sem):
        land(into_z, sem + 1)
        red[...] = (held + into_z[...].astype(F32)).astype(BF)
        push(red, piece(full, zl, x), sem + 2, zpart)
        piece(full, zl, x)[...] = red[...]

    right, left = xpeer(1), xpeer(3)

    def r_first(src, piece, into, sem):
        push(piece(src, 0, (x + 2) % 4), into.at[0], sem, right)
        push(piece(src, 1, (x + 2) % 4), into.at[1], sem, left)
        push(piece(src, 1, (x + 1) % 4), into.at[3], sem + 1, right)
        push(piece(src, 0, (x + 3) % 4), into.at[4], sem + 1, left)

    def r_second(src, piece, into, send, sem):
        land(into.at[0:2], sem)
        send[0] = (piece(src, 0, (x + 1) % 4)[...].astype(F32) + into[0].astype(F32)).astype(BF)
        send[1] = (piece(src, 1, (x + 3) % 4)[...].astype(F32) + into[1].astype(F32)).astype(BF)
        push(send.at[0], into.at[2], sem + 1, right)
        push(send.at[1], into.at[5], sem + 1, left)

    def r_third(src, piece, into, send, into_z, sem):
        land(into.at[2:6], sem + 1)

        def total(z):
            own = piece(src, z, x)[...].astype(F32)
            return own + into[2 + z].astype(F32) + into[4 + z].astype(F32)

        send[...] = total(1 - zl).astype(BF)
        push(send, into_z, sem + 2, zpart)
        return total(zl)

    def r_fourth(held, piece, full, red, into_z, sem):
        land(into_z, sem + 2)
        red[...] = (held + into_z[...].astype(F32)).astype(BF)
        push(red, piece(full, zl, x), sem + 3, zpart)
        for dev in (right, left):
            push(red, piece(full, zl, x), sem + 4, dev)
        piece(full, zl, x)[...] = red[...]

    def r_fifth(piece, full, red, sem):
        land(red, sem + 3)
        for dev in (right, left):
            push(piece(full, 1 - zl, x), piece(full, 1 - zl, x), sem + 4, dev)

    def r_sixth(piece, full, into, sem):
        land(into.at[0:4], sem + 4)
        push(piece(full, 0, (x + 3) % 4), piece(full, 0, (x + 3) % 4), sem + 5, right)
        push(piece(full, 1, (x + 1) % 4), piece(full, 1, (x + 1) % 4), sem + 5, left)

    def a_fourth(col, full, red, sem):
        land(red, sem + 2)
        for r in range(1, 4):
            push(col(full, x), col(full, x), sem + 3, xpeer(r))

    def b_first(src, row, into_z, sem):
        push(row(src, 1 - zl), into_z, sem, zpart)

    def b_second(src, row, part, held, into_z, into, sem):
        land(into_z, sem)
        held[...] = (row(src, zl)[...].astype(F32) + into_z[...].astype(F32)).astype(BF)
        for r in range(1, 4):
            push(part(held, (x + r) % 4), into.at[r], sem + 1, xpeer(r))

    def b_third(part, piece, full, held, into, red, sem):
        land(into.at[1:4], sem + 1)
        red[...] = (part(held, x)[...].astype(F32) + sum(into[r].astype(F32) for r in range(1, 4))).astype(BF)
        for r in range(1, 4):
            push(red, piece(full, zl, x), sem + 2, xpeer(r))
        piece(full, zl, x)[...] = red[...]

    def b_fourth(row, full, into, sem):
        land(into.at[1:4], sem + 2)
        push(row(full, zl), row(full, zl), sem + 3, zpart)

    def ca_part(buf, r, z):
        return buf.at[r, z]

    def cb_part(buf, at):
        return buf.at[pl.ds(al(64 * at, 64), 64)]

    def reduced(into, base):
        land(into.at[1:16], base)
        same = sum(into[r].astype(F32) for r in range(0, 16, 2))
        other = sum(into[r].astype(F32) for r in range(1, 16, 2))
        first = jnp.where(c == 0, same, other)
        second = jnp.where(c == 0, other, same)
        return first, second

    land(o_in.at[1:4], O_X)
    ot[...] = (o_f[0] * factors[0] + sum(o_in[r].astype(F32) for r in range(1, 4))).astype(BF)

    @pl.loop(0, 4)
    def _(k):
        cols = pl.ds(al(384 * k, 128), 384)
        cot_n[:, cols] = jnp.transpose(cot_t[cols, :].astype(F32)).astype(BF)

    grad_w(3, ot, cot_n)


    land(dkv_in.at[1], DKV_SIB)
    land(z_in, DKV_Z)
    grad_k = dk[key_rows(0), :] + (dkv_in[1, :, 0:HEAD].astype(F32) + z_in[:, 0:HEAD].astype(F32))
    grad_v = dv[key_rows(0), :] + (dkv_in[1, :, HEAD : 2 * HEAD].astype(F32) + z_in[:, HEAD : 2 * HEAD].astype(F32))
    dqkv[HEAD : 2 * HEAD, :] = jnp.transpose(grad_k).astype(BF)
    dqkv[2 * HEAD : 3 * HEAD, :] = jnp.transpose(grad_v).astype(BF)
    land(dq_in.at[1:4], DQ_X)
    grad_q = dq_f[0] + sum(dq_in[r].astype(F32) for r in range(1, 4))
    dqkv[0:HEAD, :] = grad_q.astype(BF)

    row_stat = jnp.sum(dqkv[0:HEAD, :].astype(F32) * q[0].astype(F32), axis=0, keepdims=True)
    row_stat = row_stat + jnp.sum(dqkv[HEAD:, :].astype(F32) * kv[0].astype(F32), axis=0, keepdims=True)
    wide_stat[0:1, :] = row_stat * (1.0 / D)

    def scatter_rows(k):
        cols = pl.ds(al(384 * k, 128), 384)
        inverse = wide_stat[1:2, :]
        unit = tok_t[cols, :].astype(F32) * inverse
        n_send[cols, :] = (inverse * (mm(w_t[cols, :], dqkv[...]) - unit * wide_stat[0:1, :])).astype(BF)

    @pl.loop(0, 4)
    def _(k):
        scatter_rows(k)

    for step in around:
        peer = around_mp(step)
        slot = step[0] * 8 + step[1] * 2 + step[2]
        push(n_send.at[pl.ds(al(SHARE * peer, 32), SHARE)], n_in.at[slot], NORM_RS, (s, peer))
    n_in[0] = n_send[mine, :]

    grad_sum(3)
    r_first(g_acc, g_piece(3), gr_in.at[3], G_STEP + 18)

    for k in range(3):
        grad_w(k, dqkv.at[HEAD * k : HEAD * k + HEAD], norm_n)
    for k in range(3):
        grad_sum(k)
        r_first(g_acc, g_piece(k), gr_in.at[k], G_STEP + 6 * k)
    @pl.loop(0, 4)
    def _(k):
        cols = pl.ds(al(384 * k, 128), 384)
        a_send[k // 2, pl.ds(al(384 * (k % 2), 128), 384), :] = mm(wo_t[cols, :], ot[...]).astype(BF)

    held = {}
    order = (3, 0, 1, 2)
    for k in order:
        r_second(g_acc, g_piece(k), gr_in.at[k], gr_send.at[k], G_STEP + 6 * k)
    first, second = reduced(n_in, NORM_RS)
    for r in range(1, 4):
        rows = pl.ds(al(HEAD * ((y + r) % 4), 64), HEAD)
        push(a_send.at[:, rows], ay_in.at[r], OUT_Y, (s, zh * 8 + ((y + r) % 4) * 2 + c))
    tok_grad = cot_own[...].astype(F32) + jnp.concatenate([first, second], axis=1)
    pad = jnp.zeros((SHARE, WIDE - PAIRS), F32)
    for half in range(2):
        pg = jnp.concatenate([0.5 * tok_grad * slope[half], pad], axis=1)
        for d in range(3):
            shift = (WIDE - 1, 0, 1)[d]
            moved = pltpu.roll(pg, shift, 1) if shift else pg
            row = SHARE * (2 * d + half)
            pgs[row : row + SHARE, :] = moved.astype(BF)
    both = pgs[2 * SHARE : 3 * SHARE, 0:PAIRS], pgs[3 * SHARE : 4 * SHARE, 0:PAIRS]
    ones = jnp.ones((16, PAIRS), BF)
    bias = nt(ones, both[0]) + nt(ones, both[1])
    c_send[1, 224:256, :] = jnp.zeros((32, CIN), BF)
    c_send[1, 224:240, 0:SHARE] = bias.astype(BF)

    @pl.loop(0, 3)
    def _(k):
        cols = pl.ds(al(256 * k, 256), 256)
        odd_cols = pl.ds(al(CIN + 256 * k, 256), 256)
        me = mm(pgs[...], xe[:, cols])
        mo = mm(pgs[...], xe[:, odd_cols])

        def part(arr, d, half):
            row = SHARE * (2 * (d + 1) + half)
            return arr[row : row + SHARE]

        taps = (
            part(me, -1, 0) + part(mo, -1, 1),
            part(mo, -1, 0) + part(me, 0, 1),
            part(me, 0, 0) + part(mo, 0, 1),
            part(mo, 0, 0) + part(me, 1, 1),
            part(me, 1, 0) + part(mo, 1, 1),
        )
        for t in range(TAPS):
            tap = taps[t].astype(BF)
            if t < 2:
                c_send[0, SHARE * t : SHARE * t + SHARE, cols] = tap
            elif t == 2:
                c_send[0, 192:256, cols] = tap[0:64]
                c_send[1, 0:32, cols] = tap[64:96]
            else:
                c_send[1, SHARE * t - 256 : SHARE * t - 160, cols] = tap

    low, high = slice(0, 384), slice(384, CIN)
    a_first(c_send, c_col, cx_in, C_STEP)
    b_first(c_send, c_row, cbz_in, C_STEP + 4)

    for k in order:
        held[k] = r_third(g_acc, g_piece(k), gr_in.at[k], gz_send.at[k], gz_in.at[k], G_STEP + 6 * k)
    held_c = a_second(c_send, c_piece(low), cx_in, ca_part, cz_send, cz_in, C_STEP)
    b_second(c_send, c_row, cb_part, cb_held, cbz_in, cx_b, C_STEP + 4)
    for k in order:
        r_fourth(held[k], g_piece(k), g_all, g_red.at[k], gz_in.at[k], G_STEP + 6 * k)
    a_third(held_c, c_piece(low), c_all, c_red.at[0], cz_in, C_STEP)
    b_third(cb_part, c_piece(high), c_all, cb_held, cx_b, c_red.at[1], C_STEP + 4)
    land(ay_in.at[1:4], OUT_Y)
    rows = pl.ds(al(HEAD * y, 64), HEAD)

    def over_y(z):
        return a_send[z, rows, :].astype(F32) + sum(ay_in[r, z].astype(F32) for r in range(1, 4))

    az_send[...] = over_y(1 - zh).astype(BF)
    push(az_send, az_in, OUT_Z, (s, (m + 8) % 16))
    az_own[...] = over_y(zh)
    for k in order:
        r_fifth(g_piece(k), g_all, g_red.at[k], G_STEP + 6 * k)
    a_fourth(c_col, c_all, c_red.at[0], C_STEP)
    b_fourth(c_row, c_all, cx_b, C_STEP + 4)
    for k in order:
        r_sixth(g_piece(k), g_all, gr_in.at[k], G_STEP + 6 * k)

    land(az_in, OUT_Z)
    az_own[...] = az_own[...] + az_in[...].astype(F32)
    as_send[...] = az_own[pl.ds(al(SHARE * (1 - c), 32), SHARE), :].astype(BF)
    push(as_send, as_in, OUT_SIB, sib)
    own = az_own[pl.ds(al(SHARE * c, 32), SHARE), :]
    land(as_in, OUT_SIB)
    other = as_in[...].astype(F32)
    out = jnp.concatenate([jnp.where(c == 0, own, other), jnp.where(c == 0, other, own)], axis=1)
    o_layer[...] = (out + tok_own[...].astype(F32)).astype(BF)

    for k in order:
        land(gr_in.at[k, 0:2], G_STEP + 6 * k + 5)
    land(cx_in.at[1:4], C_STEP + 3)
    land(cbz_in, C_STEP + 7)
    for copy in sent.values():
        copy.wait_send()


def scratch():
    def v(*shape, dtype=BF):
        return pltpu.VMEM(shape, dtype)

    return [
        v(1024, CIN), v(PAIRS, 128, dtype=jnp.int32), v(TAPS, SHARE, CIN), v(D, 3 * HEAD), v(D, HEAD),
        v(2, 1024, 128, dtype=F32), v(32, D, dtype=F32), v(WIDE, D), v(2, 16, D), v(576, D), v(768, D),
        v(576, WIDE, dtype=F32), v(2, SHARE, PAIRS, dtype=F32), v(SHARE, PAIRS), v(SHARE, PAIRS),
        v(D, TOK), v(D, TOK), v(D, TOK),
        v(4, HEAD, TOK), v(4, 384, TOK), v(1024, HEAD), v(1024, HEAD), v(4, HEAD, TOK),
        v(4, 1024, TOK, dtype=F32), v(4, 1024, TOK, dtype=F32),
        v(4, 8, TOK, dtype=F32), v(4, 4, 8, TOK, dtype=F32),
        v(4, HEAD, TOK, dtype=F32), v(4, HEAD, TOK), v(4, HEAD, TOK), v(HEAD, TOK),
        v(4, 8, TOK, dtype=F32),
        v(4, HEAD, TOK, dtype=F32), v(4, HEAD, TOK), v(4, HEAD, TOK),
        v(1024, HEAD, dtype=F32), v(1024, HEAD, dtype=F32), v(4, TOK, HEAD), v(4, TOK, HEAD), v(TOK, D), v(TOK, D), v(8, TOK, dtype=F32),
        v(2, TOK, 384), v(2, TOK, 384), v(TOK, 384), v(TOK, 384),
        v(576, TOK),
        v(D, TOK), v(16, SHARE, TOK),
        v(2, 768, TOK), v(4, 2, HEAD, TOK), v(HEAD, TOK), v(HEAD, TOK), v(HEAD, TOK, dtype=F32), v(SHARE, TOK), v(SHARE, TOK),
        v(HEAD, D, dtype=F32), v(4, SHARE, D), v(4, SHARE, D), v(4, SHARE, D),
        v(4, 6, 48, 384), v(4, 2, 48, 384), v(4, 48, 384), v(4, 48, 384), v(4, 48, 384),
        v(576, WIDE), v(2, 256, CIN),
        v(4, 2, 64, 384), v(64, 384), v(64, 384), v(256, 384), v(256, 384), v(4, 64, 384), v(2, 64, 384),
        pltpu.SemaphoreType.DMA((SEMS,)), pltpu.SemaphoreType.DMA((SEMS,)), pltpu.SemaphoreType.DMA((8,)),
    ]


def widen(layer, conv, grads, o_layer, o_conv, o_bias, o_q, o_k, o_v, o_o, cin, gin, cout, gout, lsem, osem):
    loads = [pltpu.make_async_copy(grads.at[k], gin.at[k], lsem.at[k]) for k in range(4)]
    loads.append(pltpu.make_async_copy(conv, cin, lsem.at[4]))
    for load in loads:
        load.start()
    through = pltpu.make_async_copy(layer, o_layer, lsem.at[5])
    through.start()
    stores = [through]
    for k, o in enumerate((o_q, o_k, o_v, o_o)):
        loads[k].wait()
        gout[k] = gin[k].astype(F32)
        stores.append(pltpu.make_async_copy(gout.at[k], o, osem.at[k]))
        stores[-1].start()
    loads[4].wait()
    for t in range(TAPS):
        cout[t] = cin[SHARE * t : SHARE * t + SHARE, :].astype(F32)
        stores.append(pltpu.make_async_copy(cout.at[t], o_conv.at[t], osem.at[4 + t]))
        stores[-1].start()
    o_bias[...] = cin[TAPS * SHARE : TAPS * SHARE + 16, 0:SHARE].astype(F32)[0:1]
    for store in stores:
        store.wait()


def body(features, base_tokens, base_proj, conv_weight, conv_bias, w_query, w_key, w_value, w_out, cotangent):
    vmem = pl.BlockSpec(memory_space=pltpu.VMEM)
    hbm = pl.BlockSpec(memory_space=pl.ANY)
    layer = jax.ShapeDtypeStruct((SHARE, PAIRS), BF)
    narrow = pl.pallas_call(
        kernel,
        out_shape=(layer, jax.ShapeDtypeStruct((2, 256, CIN), BF), jax.ShapeDtypeStruct((4, SHARE, D), BF)),
        in_specs=[hbm, hbm, vmem, hbm, vmem, hbm, hbm, hbm, hbm, hbm],
        out_specs=(vmem,) * 3,
        scratch_shapes=scratch(),
        compiler_params=pltpu.CompilerParams(
            collective_id=0, has_side_effects=True, vmem_limit_bytes=60 * 1024 * 1024
        ),
        cost_estimate=pl.CostEstimate(flops=8_000_000_000, bytes_accessed=8_000_000, transcendentals=1_300_000),
        name="section",
    )(
        features, base_tokens.reshape(PAIRS, 128), base_proj, conv_weight, conv_bias.reshape(1, SHARE),
        w_query, w_key, w_value, w_out, cotangent.T,
    )
    square = jax.ShapeDtypeStruct((SHARE, D), F32)
    layer, conv, bias, gq, gk, gv, go = pl.pallas_call(
        widen,
        out_shape=(
            layer, jax.ShapeDtypeStruct((TAPS, SHARE, CIN), F32), jax.ShapeDtypeStruct((1, SHARE), F32),
            square, square, square, square,
        ),
        in_specs=[hbm] * 3,
        out_specs=(hbm, hbm, vmem, hbm, hbm, hbm, hbm),
        scratch_shapes=[
            pltpu.VMEM((512, CIN), BF), pltpu.VMEM((4, SHARE, D), BF),
            pltpu.VMEM((TAPS, SHARE, CIN), F32), pltpu.VMEM((4, SHARE, D), F32),
            pltpu.SemaphoreType.DMA((6,)), pltpu.SemaphoreType.DMA((9,)),
        ],
        compiler_params=pltpu.CompilerParams(vmem_limit_bytes=60 * 1024 * 1024),
        name="widen",
    )(narrow[0], narrow[1].reshape(512, CIN), narrow[2])
    return layer.T, conv, bias.reshape(SHARE), gq, gk, gv, go


def solution(mesh):
    placed = (
        P("seq", None), P("seq"), P(), P(None, "mp", None), P("mp"),
        P("mp", None), P("mp", None), P("mp", None), P("mp", None), P("seq", "mp"),
    )
    return jax.shard_map(
        body,
        mesh=mesh,
        in_specs=placed,
        out_specs=(
            P("seq", "mp"), P(None, "mp", None), P("mp"),
            P("mp", None), P("mp", None), P("mp", None), P("mp", None),
        ),
        check_vma=False,
    )
```
